128 devices in a mesh: dp: 8 (over z, core), expert: 16 (over x, y).
Axes of the slice: x: 4, y: 4, z: 4, core: 2. Of those that a mesh axis runs over, the one named last changes fastest.
Arguments:
- hidden_in: bfloat16 [16384, 1024], P(('dp', 'expert')), may hold values from -6 to 6
- routes: int32 [16384, 8], P(('dp', 'expert')), may hold values from 0 to 31, all different within a row
- first_gain: bfloat16 [1024], replicated, may hold values from 0.099609375 to 1.8984375
- query_weight: bfloat16 [1024, 1024], replicated, may hold values from -0.625 to 0.625
- key_weight: bfloat16 [1024, 512], replicated, may hold values from -0.625 to 0.625
- value_weight: bfloat16 [1024, 512], replicated, may hold values from -0.1875 to 0.1875
- output_weight: bfloat16 [1024, 1024], replicated, may hold values from -1 to 1
- second_gain: bfloat16 [1024], replicated, may hold values from 0.099609375 to 1.8984375
- router_weight: bfloat16 [1024, 32], replicated, may hold values from -0.09375 to 0.09375
- gateup_weight: bfloat16 [32, 1024, 1024], P('expert'), may hold values from -0.1875 to 0.1875
- down_weight: bfloat16 [32, 512, 1024], P('expert'), may hold values from -1 to 1
- cotangent: bfloat16 [16384, 1024], P(('dp', 'expert')), may hold values from -6 to 6
Outputs:
- layer_out: bfloat16 [16384, 1024], P(('dp', 'expert'))
- hidden_grad: bfloat16 [16384, 1024], P(('dp', 'expert'))
- gateup_grad: float32 [32, 1024, 1024], P('expert')
- down_grad: float32 [32, 512, 1024], P('expert')
- query_grad: float32 [1024, 1024], replicated
- key_grad: float32 [1024, 512], replicated
- value_grad: float32 [1024, 512], replicated
- output_grad: float32 [1024, 1024], replicated
- router_grad: float32 [1024, 32], replicated
- first_grad: float32 [1024], replicated
- second_grad: float32 [1024], replicated
The draws below stay inside these ranges and needn't reach their ends.
Inputs may be any that keep to these rules, and one draw needn't show every extreme that they name: `routes`: each row names 8 different experts, and every expert is named by some row.
All inputs are finite; a program needn't handle non-finite values.
Results may differ from the reference program's by a relative error of at most 0.025.
Values may be sent and summed in bfloat16 or wider, within the bound.
No kernel may reach another device: no remote copies, remote signals or barrier semaphores. Data moves between devices by JAX's collectives and lax.ppermute only.
A program may use at most 192 MiB of HBM per device.

```python
import jax
import jax.numpy as jnp
from jax import lax

D = 1024
H = 16
KV = 8
HD = 64
FF = 512
TOP = 8
TOK_DEV = 128
EXPERTS = 32
CAPACITY = 64
LENGTH = 2048
TOKENS = 16384
N_DP = 8
N_EXPERT = 16


def block_levels(stream_key, extent, split, smallest, high):
    gain = 1.0
    for dim, parts in split:
        draws = jax.random.uniform(jax.random.fold_in(jax.random.fold_in(stream_key, 6), dim), (parts,), jnp.float32, smallest / len(split), high / len(split))
        gain = gain * jnp.repeat(jnp.exp(draws), extent[dim] // parts).reshape((-1,) + (1,) * (len(extent) - 1 - dim))
    return gain


def picks_of(rng, rows, count, top, lift):
    sequence = jax.random.permutation(jax.random.fold_in(rng, 1), count)
    favour = sequence
    for power in range(3):
        favour = favour * favour // count
    favour = favour * lift // count
    tickets = jax.random.randint(jax.random.fold_in(rng, 2), (rows, count), 0, 4096) + favour
    sure = jax.random.permutation(jax.random.fold_in(rng, 3), rows)[jnp.arange(count) % rows]
    tickets = jnp.where(jnp.arange(rows)[:, None] == sure[None, :], 1 << 14, tickets)
    priority = tickets * count + jnp.arange(count)
    return lax.top_k(priority.astype(jnp.int32), top)[1].astype(jnp.int32)


def noise(rng, extent, deviation, reach, pieces=(), kind=jnp.bfloat16):
    drawn = deviation * jax.random.normal(rng, extent, jnp.float32)
    if pieces:
        drawn = drawn * block_levels(rng, extent, pieces, -0.22, 0.18)
    return jnp.clip(drawn, -reach, reach).astype(kind)


def setup_inputs(seed: int = 0) -> dict:
    keys = jax.random.split(jax.random.key(seed), 13)
    return {
        "hidden_in": noise(keys[0], (TOKENS, D), 1.0, 6.0, ((0, 128),)),
        "routes": picks_of(keys[1], TOKENS, EXPERTS, TOP, 4096),
        "first_gain": jnp.clip(1.0 + 0.18 * jax.random.normal(keys[2], (D,), jnp.float32), 0.099609375, 1.8984375).astype(jnp.bfloat16),
        "query_weight": noise(keys[3], (D, H * HD), (D // 12) ** -0.5, 0.625),
        "key_weight": noise(keys[4], (D, KV * HD), (D // 12) ** -0.5, 0.625),
        "value_weight": noise(keys[5], (D, KV * HD), D ** -0.5, 0.1875),
        "output_weight": noise(keys[6], (H * HD, D), (D // 32) ** -0.5, 1.0),
        "second_gain": jnp.clip(1.0 + 0.18 * jax.random.normal(keys[7], (D,), jnp.float32), 0.099609375, 1.8984375).astype(jnp.bfloat16),
        "router_weight": noise(keys[8], (D, EXPERTS), (4 * D) ** -0.5, 0.09375),
        "gateup_weight": noise(keys[9], (EXPERTS, D, 2 * FF), D ** -0.5, 0.1875, ((0, 16),)),
        "down_weight": noise(keys[10], (EXPERTS, FF, D), (FF // 16) ** -0.5, 1.0, ((0, 16),)),
        "cotangent": noise(keys[11], (TOKENS, D), 1.0, 6.0, ((0, 128),)),
    }


epsilon = 1e-06
score_scale = 0.015625
highest = lax.Precision.HIGHEST

@jax.custom_vjp
def low(v):
    return lax.optimization_barrier(v.astype(jnp.bfloat16)).astype(jnp.float32)

@jax.custom_vjp
def low_back(v):
    return v

def low_keep(v):
    return (low(v), None)

def low_pass(kept, grad):
    return (grad,)

def back_keep(v):
    return (v, None)

def back_low(kept, grad):
    return (low(grad),)
low.defvjp(low_keep, low_pass)
low_back.defvjp(back_keep, back_low)

def rope_tables(offset, amount):
    places = (offset + jnp.arange(amount)).astype(jnp.float32)
    inverse = 10000.0 ** (-jnp.arange(0, HD, 2).astype(jnp.float32) / HD)
    angles = places[:, None] * inverse[None, :]
    return (jnp.cos(angles), jnp.sin(angles))

def rotate(values, cosine_table, sine_table):
    middle = values.shape[-1] // 2
    former, latter = (values[..., :middle], values[..., middle:])
    cosine_cols, sine_cols = (cosine_table[:, None, :], sine_table[:, None, :])
    return jnp.concatenate([former * cosine_cols - latter * sine_cols, latter * cosine_cols + former * sine_cols], -1)

def rms_scale(values, gain_row):
    return values * lax.rsqrt(lax.optimization_barrier(jnp.mean(values * values, -1, keepdims=True)) + epsilon) * gain_row

def slot_tables(routes):
    device_total = N_DP * N_EXPERT
    pair_count = TOK_DEV * TOP
    pair_experts = routes.reshape(device_total, pair_count)
    counts = (pair_experts[:, :, None] == jnp.arange(EXPERTS).astype(jnp.int32)[None, None, :]).astype(jnp.int32)
    earlier = jnp.cumsum(counts, 1) - counts
    slot_rank = lax.optimization_barrier(jnp.sum(earlier * counts, -1)).astype(jnp.int32)
    retained = slot_rank < CAPACITY
    sources = jnp.arange(device_total).astype(jnp.int32)[:, None]
    target = jnp.where(retained, (pair_experts * device_total + sources) * CAPACITY + slot_rank, EXPERTS * device_total * CAPACITY).astype(jnp.int32)
    pair_ids = jnp.arange(device_total * pair_count).astype(jnp.int32)
    slot_table = jnp.full((EXPERTS * device_total * CAPACITY,), device_total * pair_count, jnp.int32)
    slot_table = slot_table.at[target.reshape(-1)].set(pair_ids, mode='drop')
    return (slot_table.reshape(EXPERTS, device_total * CAPACITY), retained.reshape(TOKENS, TOP))

def attend_block(query_block, first_query, key_seq, value_seq):
    raw_scores = jnp.einsum('qkgd,skd->kgqs', query_block, key_seq, precision=highest) * score_scale
    scores = low_back(raw_scores)
    query_places = first_query + jnp.arange(query_block.shape[0]).astype(jnp.int32)
    key_places = jnp.arange(key_seq.shape[0]).astype(jnp.int32)
    visible = key_places[None, :] <= query_places[:, None]
    weights = jnp.where(visible, jnp.exp(scores), 0.0)
    totals = lax.optimization_barrier(jnp.sum(weights, -1))
    mixture = low_back(jnp.einsum('kgqs,skd->kgqd', low(weights), value_seq, precision=highest))
    return mixture / totals[..., None]

def attend_sequence(running, members):
    query_seq, key_seq, value_seq = members
    query_rows = min(512, LENGTH)
    blocks = query_seq.reshape(LENGTH // query_rows, query_rows, KV, H // KV, HD)
    starts = (jnp.arange(LENGTH // query_rows) * query_rows).astype(jnp.int32)

    def one_block(member):
        return attend_block(member[0], member[1], key_seq, value_seq)
    mixed = lax.map(jax.checkpoint(one_block), (blocks, starts))
    mixed = jnp.transpose(mixed, (0, 3, 1, 2, 4)).reshape(LENGTH, H * HD)
    return (running, mixed)

def forward(hidden, first_gain, query_weight, key_weight, value_weight, output_weight, second_gain, router_weight, gateup_weight, down_weight, routes, slot_table, retained):
    normed_one = low(rms_scale(hidden, first_gain))
    query_pre = low_back(jnp.dot(normed_one, query_weight, precision=highest))
    key_pre = low_back(jnp.dot(normed_one, key_weight, precision=highest))
    value_rows = low(low_back(jnp.dot(normed_one, value_weight, precision=highest)))
    cosine_table, sine_table = rope_tables(0, LENGTH)
    query_rot = low(rotate(query_pre.reshape(N_DP, LENGTH, H, HD), cosine_table, sine_table)).reshape(N_DP, LENGTH, KV, H // KV, HD)
    key_rot = low(rotate(key_pre.reshape(N_DP, LENGTH, KV, HD), cosine_table, sine_table))
    value_seq = value_rows.reshape(N_DP, LENGTH, KV, HD)
    ignored, mixed = lax.scan(attend_sequence, jnp.zeros((), jnp.float32), (query_rot, key_rot, value_seq))
    attended = low(mixed.reshape(TOKENS, H * HD))
    middle = hidden + low_back(jnp.dot(attended, output_weight, precision=highest))
    normed_two = low(rms_scale(middle, second_gain))
    logits = low_back(jnp.dot(normed_two, router_weight, precision=highest))
    chosen = jnp.take_along_axis(logits, routes, 1)
    gate_prob = jax.nn.softmax(chosen, -1)
    slot_weight = jnp.concatenate([(gate_prob * retained.astype(jnp.float32)).reshape(-1), jnp.zeros((1,), jnp.float32)])
    padded = jnp.concatenate([normed_two, jnp.zeros((1, D), jnp.float32)])
    token_table = (slot_table // TOP).astype(jnp.int32)

    def one_expert(member):
        token_rows, weight_rows, gateup, down = member
        gathered = padded[token_rows]
        gate_up = low_back(jnp.dot(gathered, gateup, precision=highest))
        activated = low(jax.nn.silu(gate_up[:, :FF]) * gate_up[:, FF:])
        result = low(low_back(jnp.dot(activated, down, precision=highest)))
        return weight_rows[:, None] * result
    weighted_rows = lax.map(jax.checkpoint(one_expert), (token_table, slot_weight[slot_table], gateup_weight, down_weight))
    combined = jnp.zeros((TOKENS + 1, D), jnp.float32).at[token_table.reshape(-1)].add(weighted_rows.reshape(-1, D))
    return middle + combined[:TOKENS]

def reference(hidden_in, routes, first_gain, query_weight, key_weight, value_weight, output_weight, second_gain, router_weight, gateup_weight, down_weight, cotangent):
    slot_table, retained = slot_tables(routes)

    def layer(hidden, gain_one, weight_query, weight_key, weight_value, weight_output, gain_two, weight_router, weight_gateup, weight_down):
        return forward(hidden, gain_one, weight_query, weight_key, weight_value, weight_output, gain_two, weight_router, weight_gateup, weight_down, routes, slot_table, retained)
    result, pullback = jax.vjp(layer, hidden_in.astype(jnp.float32), first_gain.astype(jnp.float32), query_weight.astype(jnp.float32), key_weight.astype(jnp.float32), value_weight.astype(jnp.float32), output_weight.astype(jnp.float32), second_gain.astype(jnp.float32), router_weight.astype(jnp.float32), gateup_weight.astype(jnp.float32), down_weight.astype(jnp.float32))
    gradients = pullback(cotangent.astype(jnp.float32))
    return (result.astype(jnp.bfloat16), gradients[0].astype(jnp.bfloat16), gradients[8], gradients[9], gradients[2], gradients[3], gradients[4], gradients[5], gradients[7], gradients[1], gradients[6])
```

```python
import functools

import jax
import jax.numpy as jnp
from jax import lax
from jax.experimental import pallas as pl
from jax.experimental.pallas import tpu as pltpu
from jax.sharding import PartitionSpec as P

D = 1024
H = 16
KV = 8
HD = 64
FF = 512
TOP = 8
EXPERTS = 32
CAPACITY = 64
TOK = 128
SEQ = 2048

epsilon = 1e-06
score_scale = 0.015625

bf16 = jnp.bfloat16
f32 = jnp.float32
AXES = ("dp", "expert")

NT = (((1,), (1,)), ((), ()))
TN = (((0,), (0,)), ((), ()))


def dot(a, b):
    return jnp.dot(a, b, preferred_element_type=f32)


def dot_nt(a, b):
    return lax.dot_general(a, b, NT, preferred_element_type=f32)


def dot_tn(a, b):
    return lax.dot_general(a, b, TN, preferred_element_type=f32)


def moves(step):
    pairs = []
    for z in range(4):
        for c in range(2):
            for x in range(4):
                for y in range(4):
                    z2, c2, x2, y2 = step(z, c, x, y)
                    target = (((z2 % 4) * 2 + c2 % 2) * 4 + x2 % 4) * 4 + y2 % 4
                    pairs.append((((z * 2 + c) * 4 + x) * 4 + y, target))
    return pairs


def along_u(n):
    return moves(lambda z, c, x, y: (z, c, x, y + n) if c == 0 else (z, c, x + n, y))


def along_v(n):
    return moves(lambda z, c, x, y: (z, c, x + n, y) if c == 0 else (z, c, x, y + n))


def along_z(n):
    return moves(lambda z, c, x, y: (z + n, c, x, y))


def other_core():
    return moves(lambda z, c, x, y: (z, c + 1, x, y))


def pair_head():
    return moves(lambda z, c, x, y: (z, c, x, y ^ 1))


def send(array, pairs):
    return lax.ppermute(array, AXES, pairs)


def gather_axis(array, along):
    return [array] + [send(array, along(-n)) for n in (1, 2, 3)]


def sum_axis(parts, along):
    return [parts[0]] + [send(parts[n], along(n)) for n in (1, 2, 3)]


def added(parts):
    total = parts[0].astype(f32)
    for part in parts[1:]:
        total = total + part.astype(f32)
    return total


def call(body, outs, args, scratch=(), specs=None, flops=0, moved=0, limit=48, name=None):
    vmem = pl.BlockSpec(memory_space=pltpu.VMEM)
    return pl.pallas_call(
        body,
        out_shape=outs,
        in_specs=[vmem] * len(args) if specs is None else specs,
        out_specs=[vmem] * len(outs),
        scratch_shapes=list(scratch),
        compiler_params=pltpu.CompilerParams(vmem_limit_bytes=limit * 1024 * 1024),
        cost_estimate=pl.CostEstimate(flops=flops, bytes_accessed=moved, transcendentals=0),
        name=name,
    )(*args)


def shape(dims, kind=bf16):
    return jax.ShapeDtypeStruct(dims, kind)


def project_body(hid, gain, wq, wk, wv, cosine, sine, out, normed):
    hidden = hid[...].astype(f32)
    r1 = lax.rsqrt(jnp.mean(hidden * hidden, -1, keepdims=True) + epsilon)
    n1 = (hidden * r1 * gain[...]).astype(bf16)
    normed[...] = n1
    cos = cosine[...][None]
    sin = sine[...][None]

    def rotated(value, heads):
        value = value.T.reshape(heads, HD, TOK)
        a, b = value[:, : HD // 2], value[:, HD // 2 :]
        return jnp.concatenate([a * cos - b * sin, b * cos + a * sin], 1).astype(bf16)

    key = rotated(dot(n1, wk[...]), KV)
    value = dot(n1, wv[...]).T.reshape(KV, HD, TOK).astype(bf16)
    query = rotated(dot(n1, wq[...]), H)
    for h in range(H):
        out[h, 0:64] = query[h]
        out[h, 64:128] = key[h // 2]
        out[h, 128:192] = value[h // 2]


def attend_body(recv, att_send, att, totals, qkv):
    for s in range(16):
        qkv[:, 128 * s : 128 * s + 128] = recv[s]
    rows = lax.broadcasted_iota(jnp.int32, (256, 256), 0)
    cols = lax.broadcasted_iota(jnp.int32, (256, 256), 1)
    visible = rows <= cols
    for i in range(8):
        here = slice(256 * i, 256 * i + 256)
        query = qkv[0:64, here]
        weights = jnp.exp(dot_tn(qkv[64:128, here], query) * score_scale)
        weights = jnp.where(visible, weights, 0.0)
        total = jnp.sum(weights, 0, keepdims=True)
        mixture = dot(qkv[128:192, here], weights.astype(bf16))
        if i:
            before = slice(0, 256 * i)
            weights = jnp.exp(dot_tn(qkv[64:128, before], query) * score_scale)
            total = total + jnp.sum(weights, 0, keepdims=True)
            mixture = mixture + dot(qkv[128:192, before], weights.astype(bf16))
        mixed = mixture / total
        att[:, here] = mixed
        totals[:, here] = total
        att_send[2 * i] = mixed[:, :128].astype(bf16)
        att_send[2 * i + 1] = mixed[:, 128:].astype(bf16)


def middle_body(att_t, hid, wo, gain, middle, scale, normed):
    attended = att_t[...].reshape(D, TOK).T
    mid = hid[...].astype(f32) + dot(attended, wo[...])
    r2 = lax.rsqrt(jnp.mean(mid * mid, -1, keepdims=True) + epsilon)
    middle[...] = mid
    scale[...] = jnp.broadcast_to(r2, scale.shape)
    normed[...] = (mid * r2 * gain[...]).astype(bf16)


def expert_body(
    src, n2, cot, code, router, wgu, wd, part, x_out, g_out, act_out, gb_out, cot_v, wgu_v, wd_v, dx_v, sems
):
    copies = []
    for j in range(4):
        copies.append(pltpu.make_async_copy(cot.at[src[j], pl.ds(0, TOK)], cot_v.at[j], sems.at[j]))
    for e in range(2):
        copies.append(pltpu.make_async_copy(wgu.at[e], wgu_v.at[e], sems.at[4 + e]))
        copies.append(pltpu.make_async_copy(wd.at[e], wd_v.at[e], sems.at[6 + e]))
    for copy in copies:
        copy.start()
    slots = lax.broadcasted_iota(jnp.int32, (CAPACITY, TOK), 0).astype(f32)
    places = []
    gates = []
    for j in range(4):
        rows = n2[j]
        logits = dot_nt(router[...], rows)
        codes = code[src[j]]
        chosen = codes > -1.5
        top = jnp.max(jnp.where(chosen, logits, -1e30), 0, keepdims=True)
        powers = jnp.where(chosen, jnp.exp(logits - top), 0.0)
        prob = powers / jnp.sum(powers, 0, keepdims=True)
        where = [codes[e : e + 1] == slots for e in range(2)]
        places.append(jnp.concatenate([w.astype(f32) for w in where], 0).astype(bf16))
        gates.append([jnp.sum(jnp.where(where[e], prob[e : e + 1], 0.0), 1, keepdims=True) for e in range(2)])
        copies[j].wait()
        here = slice(64 * j, 64 * j + 64)
        picked = dot(places[j], rows).astype(bf16)
        x_out[0, here] = picked[:64]
        x_out[1, here] = picked[64:]
        picked = dot(places[j], cot_v[j]).astype(bf16)
        g_out[0, here] = picked[:64]
        g_out[1, here] = picked[64:]
    grad_gates = []
    for e in range(2):
        copies[4 + 2 * e].wait()
        copies[5 + 2 * e].wait()
        both = dot(x_out[e], wgu_v[e])
        active = dot_nt(g_out[e], wd_v[e])
        gate, up = both[:, :FF], both[:, FF:]
        s = 1.0 / (1.0 + jnp.exp(-gate))
        silu = gate * s
        act = silu * up
        weight = jnp.concatenate([gates[j][e] for j in range(4)], 0)
        act_out[e] = (act * weight).astype(bf16)
        grad_gates.append(jnp.sum(act * active, 1, keepdims=True))
        grad_active = active * weight
        gb_out[e, :, :FF] = (grad_active * up * s * (1.0 + gate * (1.0 - s))).astype(bf16)
        gb_out[e, :, FF:] = (grad_active * silu).astype(bf16)
        grad_x = dot_nt(gb_out[e], wgu_v[e]).astype(bf16)
        for j in range(4):
            dx_v[j, 64 * e : 64 * e + 64] = grad_x[64 * j : 64 * j + 64]
    first = src[4] * 2
    lane = lax.broadcasted_iota(jnp.int32, (16, D), 1) // TOK
    cell = lax.broadcasted_iota(jnp.int32, (16, D), 0) * 8 + lane
    for j in range(4):
        part[j, 0:TOK] = dot_tn(places[j], dx_v[j]).astype(bf16)
        tail = jnp.zeros((16, D), f32)
        for e in range(2):
            column = grad_gates[e][64 * j : 64 * j + 64]
            row = jnp.sum(places[j][64 * e : 64 * e + 64].astype(f32) * column, 0, keepdims=True)
            tail = jnp.where(cell == first + e, jnp.concatenate([row] * 8, 1), tail)
        part[j, TOK : TOK + 16] = tail.astype(bf16)


def expert_grad_body(*refs):
    x, g, act, gb = refs[0:4], refs[4:8], refs[8:12], refs[12:16]
    gu_out, down_out = refs[16:18]
    xs, gs, acts, gbs = refs[18:22]
    for i in range(4):
        here = slice(256 * i, 256 * i + 256)
        xs[here] = x[i][0]
        gs[here] = g[i][0]
        acts[here] = act[i][0]
        gbs[here] = gb[i][0]
    for b in range(4):
        here = slice(256 * b, 256 * b + 256)
        gu_out[0, here] = dot_tn(xs[:, here], gbs[...]).astype(bf16)
    for b in range(2):
        here = slice(256 * b, 256 * b + 256)
        down_out[0, here] = dot_tn(acts[:, here], gs[...]).astype(bf16)


def expert_result_body(src, act, code, wd, out, rows_v):
    slots = lax.broadcasted_iota(jnp.int32, (CAPACITY, TOK), 0).astype(f32)
    for e in range(2):
        result = dot(act[e], wd[e]).astype(bf16)
        for j in range(4):
            rows_v[j, 64 * e : 64 * e + 64] = result[64 * j : 64 * j + 64]
    for j in range(4):
        codes = code[src[j]]
        place = jnp.concatenate([(codes[e : e + 1] == slots).astype(f32) for e in range(2)], 0).astype(bf16)
        out[j] = dot_tn(place, rows_v[j]).astype(bf16)


def norm_back_body(
    p0, p1, p2, p3, n2, middle, scale, gain, cot, code, router, wo, grad_mid, low_mid, datt, router_grad, second
):
    total = added([p0[...], p1[...], p2[...], p3[...]])
    grad = total[:TOK]
    packed = total[TOK : TOK + 4]
    grad_gate = jnp.concatenate(
        [packed[k // 8 : k // 8 + 1, TOK * (k % 8) : TOK * (k % 8) + TOK] for k in range(EXPERTS)], 0
    )
    rows = n2[...]
    logits = dot_nt(router[...], rows)
    chosen = code[...] > -1.5
    top = jnp.max(jnp.where(chosen, logits, -1e30), 0, keepdims=True)
    powers = jnp.where(chosen, jnp.exp(logits - top), 0.0)
    prob = powers / jnp.sum(powers, 0, keepdims=True)
    grad_chosen = prob * (grad_gate - jnp.sum(prob * grad_gate, 0, keepdims=True))
    grad_logits = grad_chosen.astype(bf16)
    router_grad[...] = dot(grad_logits, rows)
    grad = grad + dot_tn(grad_logits, router[...])
    mid = middle[...]
    r2 = scale[:, 0:1]
    g2 = grad * gain[...]
    second[...] = jnp.sum(grad * mid * r2, 0, keepdims=True)
    grad_middle = cot[...].astype(f32) + r2 * g2 - mid * r2 * r2 * r2 * jnp.mean(g2 * mid, -1, keepdims=True)
    grad_mid[...] = grad_middle
    low = grad_middle.astype(bf16)
    low_mid[...] = low
    datt[...] = dot_nt(wo[...], low).astype(bf16).reshape(H, HD, TOK)


def output_grad_body(order, att, low, router_grad, second, out):
    grad = dot(att[...].reshape(D, TOK), low[...])
    for r in range(H):
        h = order[r]
        out[r, 64:80] = jnp.zeros((16, D), bf16)
    rows = grad.astype(bf16).reshape(H, HD, D)
    for h in range(H):
        r = order[H + h]
        out[r, 0:64] = rows[h]
        index = lax.broadcasted_iota(jnp.int32, (16, D), 0)
        tail = jnp.where(index == 0, router_grad[2 * h : 2 * h + 1], 0.0)
        tail = jnp.where(index == 1, router_grad[2 * h + 1 : 2 * h + 2], tail)
        if h == 0:
            tail = jnp.where(index == 2, second[...], tail)
        out[r, 64:80] = tail.astype(bf16)


def attend_back_body(odd, datt, qkv, att, totals, cosine, sine, n1, out, weight_grad, pair, dq, dk, dv, dmix, low):
    for s in range(16):
        dmix[:, 128 * s : 128 * s + 128] = datt[s]
    rows = lax.broadcasted_iota(jnp.int32, (256, 256), 0)
    cols = lax.broadcasted_iota(jnp.int32, (256, 256), 1)
    visible = rows <= cols
    dk[...] = jnp.zeros_like(dk)
    dv[...] = jnp.zeros_like(dv)
    for i in range(8):
        here = slice(256 * i, 256 * i + 256)
        query = qkv[0:64, here]
        inverse = 1.0 / totals[:, here]
        grad_att = dmix[:, here].astype(f32)
        delta = jnp.sum(grad_att * att[:, here], 0, keepdims=True) * inverse
        grad_mix = (grad_att * inverse).astype(bf16)
        for at, diagonal in ((slice(0, 256 * i), False), (here, True)):
            if at.stop == 0:
                continue
            key = qkv[64:128, at]
            weights = jnp.exp(dot_tn(key, query) * score_scale)
            if diagonal:
                weights = jnp.where(visible, weights, 0.0)
            grad_weights = dot_tn(qkv[128:192, at], grad_mix)
            grad_scores = (weights * (grad_weights - delta)).astype(bf16)
            more = dot(key, grad_scores)
            dq[:, here] = more if not diagonal or i == 0 else dq[:, here] + more
            dk[:, at] += dot_nt(query, grad_scores)
            dv[:, at] += dot_nt(grad_mix, weights.astype(bf16))

    def unrotated(value):
        value = value * score_scale
        a, b = value[: HD // 2], value[HD // 2 :]
        cos, sin = cosine[...], sine[...]
        return jnp.concatenate([a * cos + b * sin, b * cos - a * sin], 0).astype(bf16)

    low[0:64] = unrotated(dq[...])
    low[64:128] = unrotated(dk[...])
    low[128:192] = dv[...].astype(bf16)
    for s in range(16):
        out[s] = low[:, 128 * s : 128 * s + 128]
    grads = dot(low[...], n1[...].reshape(SEQ, D))
    weight_grad[...] = grads
    pair[...] = jnp.where(odd[0] == 1, grads[64:128], grads[128:192]).astype(bf16)


def hidden_grad_body(recv, hid, gain, grad_mid, wq, wk, wv, out):
    got = recv[...]
    grad_q = got[:, 0:64].reshape(D, TOK).T
    pairs = got[:, 64:192].astype(f32).reshape(KV, 2, 128, TOK)
    pairs = (pairs[:, 0] + pairs[:, 1]).astype(bf16)
    grad_k = pairs[:, 0:64].reshape(KV * HD, TOK).T
    grad_v = pairs[:, 64:128].reshape(KV * HD, TOK).T
    grad = dot_nt(grad_q, wq[...]) + dot_nt(grad_k, wk[...]) + dot_nt(grad_v, wv[...])
    hidden = hid[...].astype(f32)
    r1 = lax.rsqrt(jnp.mean(hidden * hidden, -1, keepdims=True) + epsilon)
    g1 = grad * gain[...]
    back = r1 * g1 - hidden * r1 * r1 * r1 * jnp.mean(g1 * hidden, -1, keepdims=True)
    out[...] = (grad_mid[...] + back).astype(bf16)


def slices_body(order, odd, weight_grad, pair, o0, o1, o2, o3, out):
    own = jnp.where(odd[0] == 1, weight_grad[128:192], weight_grad[64:128]) + pair[...].astype(f32)
    rest = added([o0[...], o1[...], o2[...], o3[...]])
    for b in range(8):
        here = slice(128 * b, 128 * b + 128)
        r = order[b]
        out[r, 0:64] = weight_grad[0:64, here].astype(bf16)
        out[r, 64:128] = own[:, here].astype(bf16)
        out[r, 128:208] = rest[:, here].astype(bf16)


def assemble_body(
    table, *refs
):
    mine, theirs = refs[0:4], refs[4:8]
    wq, wk, wv, gain = refs[8:12]
    q_out, k_out, v_out, o_out, r_out, f_out, s_out = refs[12:19]
    tiles, tails = refs[19:21]
    g = pl.program_id(0)

    def place(parts, base):
        for i in range(4):
            for j in range(4):
                h = table[8 + base + 4 * i + j]
                block = parts[i][j, 0]
                tiles[h] = block[0:128].astype(f32)
                o_out[pl.ds(pl.multiple_of(h * 64, 64), 64)] = block[128:192].astype(f32)
                tails[h] = block[192:208].astype(f32)

    @pl.when(g < 4)
    def _():
        place(mine, 0)

    @pl.when(g >= 4)
    def _():
        place(theirs, 16)

    for p in range(8):
        q_out[:, 128 * p : 128 * p + 128] = jnp.concatenate([tiles[2 * p][:, :64], tiles[2 * p + 1][:, :64]], 1)
    for m in range(4):
        here = slice(128 * m, 128 * m + 128)
        k_out[:, here] = jnp.concatenate([tiles[4 * m][:, 64:], tiles[4 * m + 2][:, 64:]], 1)
        v_out[:, here] = jnp.concatenate([tiles[4 * m + 1][:, 64:], tiles[4 * m + 3][:, 64:]], 1)
    for h in range(16):
        r_out[2 * h : 2 * h + 2] = tails[h][0:2]
    s_out[...] = jnp.broadcast_to(tails[0][2:3], s_out.shape)
    total = jnp.sum(q_out[...] * wq[...].astype(f32), 1, keepdims=True)
    total = total + jnp.sum(k_out[...] * wk[...].astype(f32), 1, keepdims=True)
    total = total + jnp.sum(v_out[...] * wv[...].astype(f32), 1, keepdims=True)
    f_out[...] = total / gain[...]


def assemble(table, mine, theirs, wq, wk, wv, gain):
    rows = 208
    grid_spec = pltpu.PrefetchScalarGridSpec(
        num_scalar_prefetch=1,
        grid=(8,),
        in_specs=[pl.BlockSpec((4, 1, rows, 128), lambda g, t: (0, g % 4, 0, 0))] * 8
        + [
            pl.BlockSpec((128, 1024), lambda g, t: (t[g], 0)),
            pl.BlockSpec((128, 512), lambda g, t: (t[g], 0)),
            pl.BlockSpec((128, 512), lambda g, t: (t[g], 0)),
            pl.BlockSpec((128, 1), lambda g, t: (t[g], 0)),
        ],
        out_specs=[
            pl.BlockSpec((128, 1024), lambda g, t: (t[g], 0)),
            pl.BlockSpec((128, 512), lambda g, t: (t[g], 0)),
            pl.BlockSpec((128, 512), lambda g, t: (t[g], 0)),
            pl.BlockSpec((1024, 128), lambda g, t: (0, t[g])),
            pl.BlockSpec((32, 128), lambda g, t: (0, t[g])),
            pl.BlockSpec((128, 1), lambda g, t: (t[g], 0)),
            pl.BlockSpec((8, 128), lambda g, t: (0, t[g])),
        ],
        scratch_shapes=[pltpu.VMEM((16, 128, 128), f32), pltpu.VMEM((16, 16, 128), f32)],
    )
    return pl.pallas_call(
        assemble_body,
        grid_spec=grid_spec,
        out_shape=[
            shape((1024, 1024), f32),
            shape((1024, 512), f32),
            shape((1024, 512), f32),
            shape((1024, 1024), f32),
            shape((32, 1024), f32),
            shape((1024, 1), f32),
            shape((8, 1024), f32),
        ],
        compiler_params=pltpu.CompilerParams(vmem_limit_bytes=48 * 1024 * 1024),
        name="assemble",
    )(table, *mine, *theirs, wq, wk, wv, gain)


def slot_codes(routes):
    chosen = (routes.T[:, None, :] == jnp.arange(EXPERTS)[None, :, None]).any(0)
    before = jnp.triu(jnp.ones((TOK, TOK), f32), 1)
    rank = jnp.dot(chosen.astype(bf16), before.astype(bf16), preferred_element_type=f32)
    kept = chosen & (rank < CAPACITY)
    return jnp.where(kept, rank, jnp.where(chosen, -1.0, -2.0))


def on_device(
    hidden_in,
    routes,
    first_gain,
    query_weight,
    key_weight,
    value_weight,
    output_weight,
    second_gain,
    router_weight,
    gateup_weight,
    down_weight,
    cotangent,
):
    dp, me = lax.axis_index("dp"), lax.axis_index("expert")
    z, core = dp // 2, dp % 2
    x, y = me // 4, me % 4
    steps = jnp.arange(4)

    def places(which):
        zero = ((x + steps[:, None]) % 4) * 4 + (y + steps[None, :]) % 4
        one = ((x + steps[None, :]) % 4) * 4 + (y + steps[:, None]) % 4
        return jnp.where(which == 0, zero, one).astype(jnp.int32)

    sources = places(core)
    vm = pl.BlockSpec(memory_space=pltpu.VMEM)
    sm = pl.BlockSpec(memory_space=pltpu.SMEM)
    anyspace = pl.BlockSpec(memory_space=pl.ANY)

    gain_one = first_gain.astype(f32)[None]
    gain_two = second_gain.astype(f32)[None]
    router_t = router_weight.T

    codes = slot_codes(routes)
    packed = jnp.pad(codes.astype(bf16).reshape(4, D), ((0, 12), (0, 0)))
    cot_all = lax.all_gather(jnp.concatenate([cotangent, packed], 0), "expert", axis=0, tiled=False)
    code_all = cot_all[:, TOK : TOK + 4].reshape(16, EXPERTS, TOK).astype(f32)
    code_mine = jnp.roll(code_all, -2 * me, axis=1)
    router_mine = jnp.roll(router_t, -2 * me, axis=0)

    inverse = 10000.0 ** (-jnp.arange(0, HD, 2).astype(f32) / HD)
    all_angles = inverse[:, None] * jnp.arange(SEQ).astype(f32)[None, :]
    cos_all, sin_all = jnp.cos(all_angles), jnp.sin(all_angles)
    angles = inverse[:, None] * (me * TOK + jnp.arange(TOK)).astype(f32)[None, :]

    to_heads, normed_one = call(
        project_body,
        [shape((16, 192, TOK)), shape((TOK, D))],
        [hidden_in, gain_one, query_weight, key_weight, value_weight, jnp.cos(angles), jnp.sin(angles)],
        flops=2 * TOK * D * 2048,
        moved=5 << 20,
        name="project",
    )
    at_heads = lax.all_to_all(to_heads, "expert", split_axis=0, concat_axis=0, tiled=True)
    normed_all = lax.all_gather(normed_one, "expert", axis=0, tiled=False)
    att_send, att, totals, qkv = call(
        attend_body,
        [shape((16, HD, TOK)), shape((HD, SEQ), f32), shape((1, SEQ), f32), shape((192, SEQ))],
        [at_heads],
        flops=4 * 10**9,
        moved=3 << 20,
        name="attend",
    )
    att_t = lax.all_to_all(att_send, "expert", split_axis=0, concat_axis=0, tiled=True)
    middle, scale_two, normed_two = call(
        middle_body,
        [shape((TOK, D), f32), shape((TOK, 128), f32), shape((TOK, D))],
        [att_t, hidden_in, output_weight, gain_two],
        flops=2 * TOK * D * D,
        moved=4 << 20,
        name="middle",
    )

    row = jnp.stack(gather_axis(normed_two, along_u))
    chunks = gather_axis(row, along_v)
    worked = {}
    for i in (0, 1, 3, 2):
        ids = jnp.concatenate([sources[i], me[None].astype(jnp.int32)])
        worked[i] = call(
            expert_body,
            [
                shape((4, TOK + 16, D)),
                shape((2, 256, D)),
                shape((2, 256, D)),
                shape((2, 256, FF)),
                shape((2, 256, 2 * FF)),
            ],
            [ids, chunks[i], cot_all, code_mine, router_mine, gateup_weight, down_weight],
            scratch=[
                pltpu.VMEM((4, TOK, D), bf16),
                pltpu.VMEM((2, D, 2 * FF), bf16),
                pltpu.VMEM((2, FF, D), bf16),
                pltpu.VMEM((4, TOK, D), bf16),
                pltpu.SemaphoreType.DMA((8,)),
            ],
            specs=[sm, vm, anyspace, vm, vm, anyspace, anyspace],
            flops=4 * 10**9,
            moved=14 << 20,
            name="experts",
        )
    parts = sum_axis([worked[i][0] for i in range(4)], along_v)
    grad_rows = sum_axis([added([p[j] for p in parts]).astype(bf16) for j in range(4)], along_u)

    saved = [[worked[i][k] for i in range(4)] for k in range(1, 5)]

    def half(width):
        return pl.BlockSpec((1, 256, width), lambda e: (e, 0, 0))

    gateup_grad, down_grad = pl.pallas_call(
        expert_grad_body,
        grid=(2,),
        in_specs=[half(D)] * 8 + [half(FF)] * 4 + [half(2 * FF)] * 4,
        out_specs=[pl.BlockSpec((1, D, 2 * FF), lambda e: (e, 0, 0)), pl.BlockSpec((1, FF, D), lambda e: (e, 0, 0))],
        out_shape=[shape((2, D, 2 * FF)), shape((2, FF, D))],
        scratch_shapes=[
            pltpu.VMEM((1024, D), bf16),
            pltpu.VMEM((1024, D), bf16),
            pltpu.VMEM((1024, FF), bf16),
            pltpu.VMEM((1024, 2 * FF), bf16),
        ],
        compiler_params=pltpu.CompilerParams(vmem_limit_bytes=56 * 1024 * 1024),
        cost_estimate=pl.CostEstimate(flops=7 * 10**9, bytes_accessed=24 << 20, transcendentals=0),
        name="expert_grads",
    )(*saved[0], *saved[1], *saved[2], *saved[3])
    gateup_grad, down_grad = lax.psum((gateup_grad, down_grad), "dp")

    results = []
    for i in range(4):
        (result,) = call(
            expert_result_body,
            [shape((4, TOK, D))],
            [sources[i], saved[2][i], code_mine, down_weight],
            scratch=[pltpu.VMEM((4, TOK, D), bf16)],
            specs=[sm, vm, vm, vm],
            flops=10**9,
            moved=4 << 20,
            name="expert_results",
        )
        results.append(result)
    result_parts = sum_axis(results, along_v)
    result_rows = sum_axis([added([p[j] for p in result_parts]).astype(bf16) for j in range(4)], along_u)
    layer_out = (middle + added(result_rows)).astype(bf16)

    grad_middle, grad_middle_low, to_back, router_grad, second_part = call(
        norm_back_body,
        [
            shape((TOK, D), f32),
            shape((TOK, D)),
            shape((H, HD, TOK)),
            shape((EXPERTS, D), f32),
            shape((1, D), f32),
        ],
        [
            *grad_rows,
            normed_two,
            middle,
            scale_two,
            gain_two,
            cotangent,
            codes,
            router_t,
            output_weight,
        ],
        flops=3 * 10**8,
        moved=5 << 20,
        name="norm_back",
    )
    at_back = lax.all_to_all(to_back, "expert", split_axis=0, concat_axis=0, tiled=True)

    order = sources.reshape(-1)
    rank_of = jnp.sum(jnp.where(order[None, :] == jnp.arange(16)[:, None], jnp.arange(16)[None, :], 0), 1)
    (o_part,) = call(
        output_grad_body,
        [shape((16, 80, D))],
        [jnp.concatenate([order, rank_of]).astype(jnp.int32), att_t, grad_middle_low, router_grad, second_part],
        specs=[sm, vm, vm, vm, vm],
        flops=2 * TOK * D * D,
        moved=5 << 20,
        name="output_grad",
    )
    o_rows = sum_axis([o_part[4 * i : 4 * i + 4] for i in range(4)], along_v)
    o_rows = sum_axis([added([p[j] for p in o_rows]).astype(bf16) for j in range(4)], along_u)

    odd = (me % 2)[None].astype(jnp.int32)
    to_tokens, weight_grad, pair = call(
        attend_back_body,
        [shape((16, 192, TOK)), shape((192, D), f32), shape((HD, D))],
        [odd, at_back, qkv, att, totals, cos_all, sin_all, normed_all],
        scratch=[
            pltpu.VMEM((HD, SEQ), f32),
            pltpu.VMEM((HD, SEQ), f32),
            pltpu.VMEM((HD, SEQ), f32),
            pltpu.VMEM((HD, SEQ), bf16),
            pltpu.VMEM((192, SEQ), bf16),
        ],
        specs=[sm] + [vm] * 7,
        flops=10**10,
        moved=10 << 20,
        name="attend_back",
    )
    at_tokens = lax.all_to_all(to_tokens, "expert", split_axis=0, concat_axis=0, tiled=True)
    (hidden_grad,) = call(
        hidden_grad_body,
        [shape((TOK, D))],
        [at_tokens, hidden_in, gain_one, grad_middle, query_weight, key_weight, value_weight],
        flops=2 * TOK * D * 2048,
        moved=6 << 20,
        name="hidden_grad",
    )

    pair = send(pair, pair_head())
    blocks = jnp.arange(8)
    offsets = ((blocks // 4 + core) % 2) * 4 + ((blocks % 4) - z) % 4
    (slices,) = call(
        slices_body,
        [shape((8, 208, 128))],
        [offsets.astype(jnp.int32), odd, weight_grad, pair, *o_rows],
        specs=[sm, sm] + [vm] * 6,
        flops=10**6,
        moved=3 << 20,
        name="slices",
    )
    halves = added([slices[:4], send(slices[4:], other_core())]).astype(bf16)
    block = added(sum_axis([halves[k] for k in range(4)], along_z))
    block = jnp.concatenate([block[:128].T, block[128:]], 0).astype(bf16)
    block = jnp.stack(gather_axis(block, along_z))
    block = jnp.stack(gather_axis(block, along_u))
    mine = gather_axis(block, along_v)
    theirs = [send(part, other_core()) for part in mine]
    own_blocks = jnp.concatenate([core * 4 + (z + steps) % 4, (1 - core) * 4 + (z + steps) % 4])
    table = jnp.concatenate([own_blocks, places(core).reshape(-1), places(1 - core).reshape(-1)]).astype(jnp.int32)
    query_grad, key_grad, value_grad, output_grad, router_out, first_grad, second_grad = assemble(
        table, mine, theirs, query_weight, key_weight, value_weight, first_gain.astype(f32)[:, None]
    )
    return (
        layer_out,
        hidden_grad,
        gateup_grad.astype(f32),
        down_grad.astype(f32),
        query_grad,
        key_grad,
        value_grad,
        output_grad,
        router_out.T,
        first_grad[:, 0],
        second_grad[0],
    )


def solution(mesh):
    rows = P(("dp", "expert"), None)
    experts = P("expert", None, None)
    return jax.shard_map(
        on_device,
        mesh=mesh,
        in_specs=(rows, rows, P(), P(), P(), P(), P(), P(), P(), experts, experts, rows),
        out_specs=(rows, rows, experts, experts, P(), P(), P(), P(), P(), P(), P()),
        check_vma=False,
    )
```

```python
import jax
import jax.numpy as jnp
import numpy as np
from jax import lax
from jax.experimental import pallas as pl
from jax.experimental.pallas import tpu as pltpu
from jax.sharding import PartitionSpec as P

D = 1024
H = 16
KV = 8
HD = 64
FF = 512
TOP = 8
EXPERTS = 32
CAPACITY = 64
TOK = 128
SEQ = 2048

epsilon = 1e-06
score_scale = 0.015625

bf16 = jnp.bfloat16
f32 = jnp.float32
AXES = ("dp", "expert")

NT = (((1,), (1,)), ((), ()))
TN = (((0,), (0,)), ((), ()))

VM = pl.BlockSpec(memory_space=pltpu.VMEM)
HBM = pl.BlockSpec(memory_space=pltpu.HBM)
ANY = pl.BlockSpec(memory_space=pl.ANY)


def dot(a, b):
    return jnp.dot(a, b, preferred_element_type=f32)


def dot_nt(a, b):
    return lax.dot_general(a, b, NT, preferred_element_type=f32)


def dot_tn(a, b):
    return lax.dot_general(a, b, TN, preferred_element_type=f32)


def moves(step):
    pairs = []
    for z in range(4):
        for c in range(2):
            for x in range(4):
                for y in range(4):
                    z2, c2, x2, y2 = step(z, c, x, y)
                    target = (((z2 % 4) * 2 + c2 % 2) * 4 + x2 % 4) * 4 + y2 % 4
                    pairs.append((((z * 2 + c) * 4 + x) * 4 + y, target))
    return pairs


def along_u(n):
    return moves(lambda z, c, x, y: (z, c, x, y + n) if c == 0 else (z, c, x + n, y))


def along_v(n):
    return moves(lambda z, c, x, y: (z, c, x + n, y) if c == 0 else (z, c, x, y + n))


def along_z(n):
    return moves(lambda z, c, x, y: (z + n, c, x, y))


def other_core():
    return moves(lambda z, c, x, y: (z, c + 1, x, y))


def pair_head():
    return moves(lambda z, c, x, y: (z, c, x, y ^ 1))


def other_pair():
    return moves(lambda z, c, x, y: (z, c + 1, x, y ^ 1))


def send(array, pairs):
    return lax.ppermute(array, AXES, pairs)


def gather_axis(array, along):
    return [array] + [send(array, along(-n)) for n in (1, 2, 3)]


def sum_axis(parts, along):
    return [parts[0]] + [send(parts[n], along(n)) for n in (1, 2, 3)]


def added(parts):
    total = parts[0].astype(f32)
    for part in parts[1:]:
        total = total + part.astype(f32)
    return total


class Place:
    def __init__(self):
        dp, self.me = lax.axis_index("dp"), lax.axis_index("expert")
        self.z, self.core = lax.div(dp, 2), lax.rem(dp, 2)
        self.x, self.y = lax.div(self.me, 4), lax.rem(self.me, 4)

    def source(self, i, j, core=None):
        core = self.core if core is None else core
        zero = lax.rem(self.x + i, 4) * 4 + lax.rem(self.y + j, 4)
        one = lax.rem(self.x + j, 4) * 4 + lax.rem(self.y + i, 4)
        return jnp.where(core == 0, zero, one)


class Order:
    def __init__(self):
        self.last = ()

    def call(self, body, outs, args, scratch=(), specs=None, out_specs=None, limit=16, us=1, name=None, after=()):
        before = self.last + tuple(after)
        count, skip = len(args), len(before)

        def run(*refs):
            body(*refs[:count], *refs[count + skip :])

        results = pl.pallas_call(
            run,
            out_shape=outs,
            in_specs=(list(specs) if specs is not None else [VM] * count) + [ANY] * skip,
            out_specs=out_specs if out_specs is not None else [VM] * len(outs),
            scratch_shapes=list(scratch),
            compiler_params=pltpu.CompilerParams(vmem_limit_bytes=limit * 1024 * 1024),
            cost_estimate=pl.CostEstimate(flops=us * 10**9, bytes_accessed=1024, transcendentals=0),
            name=name,
        )(*args, *before)
        self.last = (results[0],)
        return results

    def stack(self, parts, after=()):
        kind = shape((4, *parts[0].shape), parts[0].dtype)
        return self.call(stack_body, [kind], parts, after=after, name="stack")[0]

    def sum4(self, parts, name):
        return self.call(sum4_body, [shape(parts[0].shape[1:])] * 4, parts, name=name)


def shape(dims, kind=bf16):
    return jax.ShapeDtypeStruct(dims, kind)


def outside(dims, kind=bf16):
    return pltpu.HBM(dims, kind)


def held_outside(array):
    return pltpu.with_memory_space_constraint(array, pltpu.HBM)


def stack_body(*refs):
    for n in range(4):
        refs[4][n] = refs[n][...]


def pack_body(cot, routes, out, codes):
    index = lax.broadcasted_iota(jnp.int32, (EXPERTS, TOK), 0)
    chosen = index < 0
    for j in range(TOP):
        chosen = chosen | (routes[j : j + 1] == index)
    rows = lax.broadcasted_iota(jnp.int32, (TOK, TOK), 0)
    cols = lax.broadcasted_iota(jnp.int32, (TOK, TOK), 1)
    rank = dot(chosen.astype(f32).astype(bf16), (rows < cols).astype(f32).astype(bf16))
    code = jnp.where(chosen & (rank < CAPACITY), rank, jnp.where(chosen, -1.0, -2.0))
    codes[...] = code
    out[0:TOK] = cot[...]
    packed = jnp.concatenate([code[4 * c : 4 * c + 4] for c in range(8)], 1)
    out[TOK : TOK + 16] = jnp.concatenate([packed, jnp.zeros((12, D), f32)], 0).astype(bf16)


def unpacked(rows):
    return jnp.concatenate([rows[:, TOK * c : TOK * c + TOK] for c in range(8)], 0)


def project_body(hid, gain, wq, wk, wv, cosine, sine, out, normed, wq_v, wk_v, wv_v, cos_v, sin_v, sems):
    me = lax.axis_index("expert")
    copies = []
    for weight, held in ((wk, wk_v), (wv, wv_v), (wq, wq_v)):
        for n in range(4):
            here = pl.ds(256 * n, 256)
            copies.append(pltpu.make_async_copy(weight.at[here], held.at[here], sems.at[len(copies)]))
    copies.append(pltpu.make_async_copy(cosine.at[me], cos_v, sems.at[12]))
    copies.append(pltpu.make_async_copy(sine.at[me], sin_v, sems.at[13]))
    for copy in copies:
        copy.start()
    hidden = hid[...].astype(f32)
    r1 = lax.rsqrt(jnp.mean(hidden * hidden, -1, keepdims=True) + epsilon)
    n1 = (hidden * r1 * gain[...]).astype(bf16)
    normed[...] = n1
    for copy in copies[12:] + copies[:4]:
        copy.wait()
    cos = cos_v[...][None]
    sin = sin_v[...][None]

    def rotated(value, heads):
        value = value.T.reshape(heads, HD, TOK)
        a, b = value[:, : HD // 2], value[:, HD // 2 :]
        return jnp.concatenate([a * cos - b * sin, b * cos + a * sin], 1).astype(bf16)

    key = rotated(dot(n1, wk_v[...]), KV)
    for copy in copies[4:8]:
        copy.wait()
    value = dot(n1, wv_v[...]).T.reshape(KV, HD, TOK).astype(bf16)
    for copy in copies[8:12]:
        copy.wait()
    query = rotated(dot(n1, wq_v[...]), H)
    for h in range(H):
        out[h, 0:64] = query[h]
        out[h, 64:128] = key[h // 2]
        out[h, 128:192] = value[h // 2]


def attend_body(recv, att_send, att_out, totals, qkv_out, att, qkv, sems):
    for s in range(16):
        qkv[:, 128 * s : 128 * s + 128] = recv[s]
    copies = [pltpu.make_async_copy(qkv, qkv_out, sems.at[8])]
    copies[0].start()
    rows = lax.broadcasted_iota(jnp.int32, (256, 256), 0)
    cols = lax.broadcasted_iota(jnp.int32, (256, 256), 1)
    visible = rows <= cols
    for i in range(8):
        here = slice(256 * i, 256 * i + 256)
        query = qkv[0:64, here]
        weights = jnp.exp(dot_tn(qkv[64:128, here], query) * score_scale)
        weights = jnp.where(visible, weights, 0.0)
        total = jnp.sum(weights, 0, keepdims=True)
        mixture = dot(qkv[128:192, here], weights.astype(bf16))
        if i:
            before = slice(0, 256 * i)
            weights = jnp.exp(dot_tn(qkv[64:128, before], query) * score_scale)
            total = total + jnp.sum(weights, 0, keepdims=True)
            mixture = mixture + dot(qkv[128:192, before], weights.astype(bf16))
        mixed = mixture / total
        att[:, here] = mixed
        totals[:, here] = total
        att_send[2 * i] = mixed[:, :128].astype(bf16)
        att_send[2 * i + 1] = mixed[:, 128:].astype(bf16)
        copies.append(pltpu.make_async_copy(att.at[:, pl.ds(256 * i, 256)], att_out.at[:, pl.ds(256 * i, 256)], sems.at[i]))
        copies[-1].start()
    for copy in copies:
        copy.wait()


def middle_body(att_t, hid, wo, gain, middle, scale, normed):
    attended = att_t[...].reshape(D, TOK).T
    mid = hid[...].astype(f32) + dot(attended, wo[...])
    r2 = lax.rsqrt(jnp.mean(mid * mid, -1, keepdims=True) + epsilon)
    middle[...] = mid
    scale[...] = jnp.broadcast_to(r2, scale.shape)
    normed[...] = (mid * r2 * gain[...]).astype(bf16)


def softmax_chosen(logits, codes):
    chosen = codes > -1.5
    top = jnp.max(jnp.where(chosen, logits, -1e30), 0, keepdims=True)
    powers = jnp.where(chosen, jnp.exp(logits - top), 0.0)
    return powers / jnp.sum(powers, 0, keepdims=True)


def row_of(table, index):
    rows = lax.broadcasted_iota(jnp.int32, table.shape, 0)
    return jnp.sum(jnp.where(rows == index, table, 0.0), 0, keepdims=True)


def expert_body(i, n2, cot, router, wgu, wd, part, x_out, g_out, act_out, gb_out, cot_v, x, g, act_v, gb, dx, sems):
    at = Place()
    me = at.me
    fetched = [pltpu.make_async_copy(cot.at[at.source(i, j)], cot_v.at[j], sems.at[6 + j]) for j in range(4)]
    for copy in fetched:
        copy.start()
    slots = lax.broadcasted_iota(jnp.int32, (CAPACITY, TOK), 0).astype(f32)
    places = []
    gates = []
    for j in range(4):
        rows = n2[j]
        logits = dot_nt(router[...], rows)
        fetched[j].wait()
        codes = unpacked(cot_v[j, TOK : TOK + 16][0:4].astype(f32))
        prob = softmax_chosen(logits, codes)
        where = [row_of(codes, 2 * me + e) == slots for e in range(2)]
        places.append(jnp.concatenate([w.astype(f32) for w in where], 0).astype(bf16))
        gates.append([jnp.sum(jnp.where(where[e], row_of(prob, 2 * me + e), 0.0), 1, keepdims=True) for e in range(2)])
        here = slice(64 * j, 64 * j + 64)
        picked = dot(places[j], rows).astype(bf16)
        x[0, here] = picked[:64]
        x[1, here] = picked[64:]
        picked = dot(places[j], cot_v[j, 0:TOK]).astype(bf16)
        g[0, here] = picked[:64]
        g[1, here] = picked[64:]
    copies = [pltpu.make_async_copy(x, x_out, sems.at[0]), pltpu.make_async_copy(g, g_out, sems.at[1])]
    for copy in copies:
        copy.start()
    grad_gates = []
    for e in range(2):
        both = dot(x[e], wgu[e])
        active = dot_nt(g[e], wd[e])
        gate, up = both[:, :FF], both[:, FF:]
        s = 1.0 / (1.0 + jnp.exp(-gate))
        silu = gate * s
        act = silu * up
        weight = jnp.concatenate([gates[j][e] for j in range(4)], 0)
        act_v[e] = (act * weight).astype(bf16)
        grad_gates.append(jnp.sum(act * active, 1, keepdims=True))
        grad_active = active * weight
        gb[e, :, :FF] = (grad_active * up * s * (1.0 + gate * (1.0 - s))).astype(bf16)
        gb[e, :, FF:] = (grad_active * silu).astype(bf16)
        for n, (held, out) in enumerate(((act_v, act_out), (gb, gb_out))):
            copies.append(pltpu.make_async_copy(held.at[e], out.at[e], sems.at[2 + 2 * e + n]))
            copies[-1].start()
        grad_x = dot_nt(gb[e], wgu[e]).astype(bf16)
        for j in range(4):
            dx[j, 64 * e : 64 * e + 64] = grad_x[64 * j : 64 * j + 64]
    lane = lax.broadcasted_iota(jnp.int32, (16, D), 1) // TOK
    row = lax.broadcasted_iota(jnp.int32, (16, D), 0)
    cell = jnp.where(row < 4, lane * 4 + row, -1)
    for j in range(4):
        part[j, 0:TOK] = dot_tn(places[j], dx[j]).astype(bf16)
        tail = jnp.zeros((16, D), f32)
        for e in range(2):
            column = grad_gates[e][64 * j : 64 * j + 64]
            value = jnp.sum(places[j][64 * e : 64 * e + 64].astype(f32) * column, 0, keepdims=True)
            tail = jnp.where(cell == 2 * me + e, jnp.concatenate([value] * 8, 1), tail)
        part[j, TOK : TOK + 16] = tail.astype(bf16)
    for copy in copies:
        copy.wait()


def expert_grad_body(*refs):
    x, g, act, gb = refs[0:4], refs[4:8], refs[8:12], refs[12:16]
    gu_out, down_out, xs, gs, acts, gbs, up_v, down_v, sems = refs[16:]
    written = []
    copies = []
    for e in range(2):
        for i in range(4):
            here = pl.ds(256 * i, 256)
            for n, (ref, held) in enumerate(((x[i], xs), (gb[i], gbs), (act[i], acts), (g[i], gs))):
                copies.append(pltpu.make_async_copy(ref.at[e], held.at[e, here], sems.at[16 * e + 4 * i + n]))
    for copy in copies:
        copy.start()
    for e in range(2):
        for copy in copies[16 * e : 16 * e + 16]:
            copy.wait()
        for b in range(4):
            here = slice(256 * b, 256 * b + 256)
            up_v[e, here] = dot_tn(xs[e, :, here], gbs[e]).astype(bf16)
            written.append(pltpu.make_async_copy(up_v.at[e, here], gu_out.at[e, here], sems.at[32 + 6 * e + b]))
            written[-1].start()
        for b in range(2):
            here = slice(256 * b, 256 * b + 256)
            down_v[e, here] = dot_tn(acts[e, :, here], gs[e]).astype(bf16)
            written.append(pltpu.make_async_copy(down_v.at[e, here], down_out.at[e, here], sems.at[36 + 6 * e + b]))
            written[-1].start()
    for copy in written:
        copy.wait()


def expert_result_body(a0, a1, a2, a3, wd, cot, o0, o1, o2, o3, rows_v, code_v, sems):
    at = Place()
    copies = [
        pltpu.make_async_copy(cot.at[at.source(r // 4, r % 4), pl.ds(TOK, 16)], code_v.at[r], sems.at[r])
        for r in range(16)
    ]
    for copy in copies:
        copy.start()
    slots = lax.broadcasted_iota(jnp.int32, (CAPACITY, TOK), 0).astype(f32)
    for i, act in enumerate((a0, a1, a2, a3)):
        for e in range(2):
            result = dot(act[e], wd[e]).astype(bf16)
            for j in range(4):
                rows_v[4 * i + j, 64 * e : 64 * e + 64] = result[64 * j : 64 * j + 64]
    for copy in copies:
        copy.wait()
    for r in range(16):
        codes = unpacked(code_v[r][0:4].astype(f32))
        place = [(row_of(codes, 2 * at.me + e) == slots).astype(f32) for e in range(2)]
        rows = dot_tn(jnp.concatenate(place, 0).astype(bf16), rows_v[r]).astype(bf16)
        (o0, o1, o2, o3)[r // 4][r % 4] = rows


def norm_back_body(
    p0, p1, p2, p3, n2, middle, scale, gain, cot, code, router, wo, grad_mid, low_mid, datt, router_grad, second, wo_v, sem
):
    fetch = pltpu.make_async_copy(wo, wo_v, sem)
    fetch.start()
    total = added([p0[...], p1[...], p2[...], p3[...]])
    grad = total[:TOK]
    grad_gate = unpacked(total[TOK : TOK + 4])
    rows = n2[...]
    prob = softmax_chosen(dot_nt(router[...], rows), code[...])
    grad_chosen = prob * (grad_gate - jnp.sum(prob * grad_gate, 0, keepdims=True))
    grad_logits = grad_chosen.astype(bf16)
    router_grad[...] = dot(grad_logits, rows)
    grad = grad + dot_tn(grad_logits, router[...])
    mid = middle[...]
    r2 = scale[:, 0:1]
    g2 = grad * gain[...]
    second[...] = jnp.sum(grad * mid * r2, 0, keepdims=True)
    grad_middle = cot[...].astype(f32) + r2 * g2 - mid * r2 * r2 * r2 * jnp.mean(g2 * mid, -1, keepdims=True)
    grad_mid[...] = grad_middle
    low = grad_middle.astype(bf16)
    low_mid[...] = low
    fetch.wait()
    datt[...] = dot_nt(wo_v[...], low).astype(bf16).reshape(H, HD, TOK)


def output_grad_body(att, low, router_grad, second, near, far, rows_v):
    at = Place()
    rows_v[:, 0:64] = dot(att[...].reshape(D, TOK), low[...]).astype(bf16).reshape(H, HD, D)
    index = lax.broadcasted_iota(jnp.int32, (16, D), 0)
    for h in range(H):
        tail = jnp.where(index == 0, router_grad[2 * h : 2 * h + 1], 0.0)
        tail = jnp.where(index == 1, router_grad[2 * h + 1 : 2 * h + 2], tail)
        if h == 0:
            tail = jnp.where(index == 2, second[...], tail)
        rows_v[h, 64:80] = tail.astype(bf16)
    for core, out in ((at.core, near), (1 - at.core, far)):
        for r in range(H):
            h = at.source(r // 4, r % 4, core)
            for b in range(4):
                column = pl.multiple_of(core * 512 + 128 * b, 128)
                out[lax.rem(b - at.z + 4, 4), r] = rows_v[h, :, pl.ds(column, 128)]


def split_sum_body(p0, p1, p2, p3, *outs):
    for n, out in enumerate(outs):
        here = slice(4 * n, 4 * n + 4)
        out[...] = added([p0[here], p1[here], p2[here], p3[here]]).astype(bf16)


def finish_body(middle, p0, p1, p2, p3, out):
    out[...] = (middle[...] + added([p0[...], p1[...], p2[...], p3[...]])).astype(bf16)


def sum4_body(*refs):
    for n in range(4):
        refs[n - 4][...] = added([ref[n] for ref in refs[:-4]]).astype(bf16)


def attend_back_body(datt, qkv_in, att_in, totals, cosine, sine, out, dq, dk, dv, dmix, qkv, att, sems):
    copies = [pltpu.make_async_copy(qkv_in, qkv, sems.at[0]), pltpu.make_async_copy(att_in, att, sems.at[1])]
    for copy in copies:
        copy.start()
    for s in range(16):
        dmix[:, 128 * s : 128 * s + 128] = datt[s]
    rows = lax.broadcasted_iota(jnp.int32, (256, 256), 0)
    cols = lax.broadcasted_iota(jnp.int32, (256, 256), 1)
    visible = rows <= cols
    dk[...] = jnp.zeros_like(dk)
    dv[...] = jnp.zeros_like(dv)
    for copy in copies:
        copy.wait()
    for i in range(8):
        here = slice(256 * i, 256 * i + 256)
        query = qkv[0:64, here]
        inverse = 1.0 / totals[:, here]
        grad_att = dmix[:, here].astype(f32)
        delta = jnp.sum(grad_att * att[:, here], 0, keepdims=True) * inverse
        grad_mix = (grad_att * inverse).astype(bf16)
        for at, diagonal in ((slice(0, 256 * i), False), (here, True)):
            if at.stop == 0:
                continue
            key = qkv[64:128, at]
            weights = jnp.exp(dot_tn(key, query) * score_scale)
            if diagonal:
                weights = jnp.where(visible, weights, 0.0)
            grad_weights = dot_tn(qkv[128:192, at], grad_mix)
            grad_scores = (weights * (grad_weights - delta)).astype(bf16)
            more = dot(key, grad_scores)
            dq[:, here] = more if not diagonal or i == 0 else dq[:, here] + more
            dk[:, at] += dot_nt(query, grad_scores)
            dv[:, at] += dot_nt(grad_mix, weights.astype(bf16))

    def unrotated(value):
        value = value * score_scale
        a, b = value[: HD // 2], value[HD // 2 :]
        cos, sin = cosine[...], sine[...]
        return jnp.concatenate([a * cos + b * sin, b * cos - a * sin], 0).astype(bf16)

    low_q, low_k, low_v = unrotated(dq[...]), unrotated(dk[...]), dv[...].astype(bf16)
    for s in range(16):
        out[s, 0:64] = low_q[:, 128 * s : 128 * s + 128]
        out[s, 64:128] = low_k[:, 128 * s : 128 * s + 128]
        out[s, 128:192] = low_v[:, 128 * s : 128 * s + 128]


def weight_grad_body(grads, n0, n1, n2, n3, near, far, low, rows_v, sems):
    at = Place()
    copies = [pltpu.make_async_copy(n, rows_v.at[i], sems.at[i]) for i, n in enumerate((n0, n1, n2, n3))]
    for copy in copies:
        copy.start()
    for r in range(16):
        low[:, 128 * r : 128 * r + 128] = grads[at.source(r // 4, r % 4)]
    total = jnp.zeros((192, D), f32)
    for i in range(4):
        copies[i].wait()
        total = total + dot(low[:, 512 * i : 512 * i + 512], rows_v[i].reshape(512, D))
    odd = lax.rem(at.y, 2) == 1
    place_columns(at, total[0:64], near, far, 0)
    place_columns(at, jnp.where(odd, total[128:192], total[64:128]), near, far, 64)
    place_columns(at, jnp.where(odd, total[64:128], total[128:192]), near, far, 128)


def hidden_grad_body(recv, hid, gain, grad_mid, wq_in, wk_in, wv_in, out, wq, wk, wv, sems):
    copies = []
    for n, (source, held) in enumerate(((wk_in, wk), (wv_in, wv), (wq_in, wq))):
        for k in range(2):
            here = pl.ds(512 * k, 512)
            copies.append(pltpu.make_async_copy(source.at[here], held.at[here], sems.at[2 * n + k]))
    for copy in copies:
        copy.start()
    got = recv[...]
    grad_q = got[:, 0:64].reshape(D, TOK).T
    pairs = got[:, 64:192].astype(f32).reshape(KV, 2, 128, TOK)
    pairs = (pairs[:, 0] + pairs[:, 1]).astype(bf16)
    grad_k = pairs[:, 0:64].reshape(KV * HD, TOK).T
    grad_v = pairs[:, 64:128].reshape(KV * HD, TOK).T
    for copy in copies:
        copy.wait()
    grad = dot_nt(grad_k, wk[...]) + dot_nt(grad_v, wv[...]) + dot_nt(grad_q, wq[...])
    hidden = hid[...].astype(f32)
    r1 = lax.rsqrt(jnp.mean(hidden * hidden, -1, keepdims=True) + epsilon)
    g1 = grad * gain[...]
    back = r1 * g1 - hidden * r1 * r1 * r1 * jnp.mean(g1 * hidden, -1, keepdims=True)
    out[...] = (grad_mid[...] + back).astype(bf16)


def place_columns(at, rows, near, far, start):
    for b in range(8):
        r = lax.rem(b % 4 - at.z + 4, 4)

        def fill(out, b=b, r=r):
            out[r, start : start + rows.shape[0]] = rows[:, 128 * b : 128 * b + 128].astype(bf16)

        pl.when(at.core == b // 4)(lambda fill=fill: fill(near))
        pl.when(at.core != b // 4)(lambda fill=fill: fill(far))


def core_sum_body(near, other, o0, o1, o2, o3):
    for n, out in enumerate((o0, o1, o2, o3)):
        out[...] = added([near[n], other[n]]).astype(bf16)


def z_sum_body(p0, p1, p2, p3, out, pair):
    total = added([p0[...], p1[...], p2[...], p3[...]]).astype(bf16)
    out[...] = total[0:128]
    pair[...] = total[128:192]


def pair_sum_body(mine, pair, o0, o1, o2, o3, out):
    weights = mine[0:128].astype(f32)
    weights = jnp.concatenate([weights[0:64], weights[64:128] + pair[...].astype(f32)], 0)
    out[0:128] = weights.T.astype(bf16)
    out[128:208] = added([o0[...], o1[...], o2[...], o3[...]]).astype(bf16)


def assemble_body(half, table, *refs):
    parts = refs[0:4]
    wq, wk, wv, gain = refs[4:8]
    q_out, k_out, v_out, o_out, r_out, e_out, tiles, tails = refs[9 + 6 * half :]
    k = pl.program_id(0)
    for i in range(4):
        for j in range(4):
            h = table[8 + 16 * half + 4 * i + j]
            block = parts[i][j, k]
            tiles[h] = block[0:128].astype(f32)
            o_out[pl.ds(pl.multiple_of(h * 64, 64), 64)] = block[128:192].astype(f32)
            tails[h] = block[192:208].astype(f32)
    for p in range(8):
        q_out[:, 128 * p : 128 * p + 128] = jnp.concatenate([tiles[2 * p][:, :64], tiles[2 * p + 1][:, :64]], 1)
    for m in range(4):
        here = slice(128 * m, 128 * m + 128)
        k_out[:, here] = jnp.concatenate([tiles[4 * m][:, 64:], tiles[4 * m + 2][:, 64:]], 1)
        v_out[:, here] = jnp.concatenate([tiles[4 * m + 1][:, 64:], tiles[4 * m + 3][:, 64:]], 1)
    for h in range(16):
        r_out[2 * h : 2 * h + 2] = tails[h][0:2]
    total = jnp.sum(q_out[...] * wq[...].astype(f32), 1, keepdims=True)
    total = total + jnp.sum(k_out[...] * wk[...].astype(f32), 1, keepdims=True)
    total = total + jnp.sum(v_out[...] * wv[...].astype(f32), 1, keepdims=True)
    first = jnp.broadcast_to(total / gain[...], (128, 128)).T
    index = lax.broadcasted_iota(jnp.int32, (8, 128), 0)
    e_out[...] = jnp.where(index == 0, first[0:8], jnp.broadcast_to(tails[0][2:3], (8, 128)))


def assemble(half, table, parts, wq, wk, wv, gain, after, begun=()):
    def at(g, t):
        return t[4 * half + g]

    rows = pl.BlockSpec((128, 1024), lambda g, t: (at(g, t), 0))
    half_rows = pl.BlockSpec((128, 512), lambda g, t: (at(g, t), 0))
    column = pl.BlockSpec((128, 1), lambda g, t: (at(g, t), 0))
    grid_spec = pltpu.PrefetchScalarGridSpec(
        num_scalar_prefetch=1,
        grid=(4,),
        in_specs=[VM] * 4 + [rows, half_rows, half_rows, column, ANY] + [ANY] * len(begun),
        out_specs=[
            rows,
            half_rows,
            half_rows,
            pl.BlockSpec((1024, 128), lambda g, t: (0, at(g, t))),
            pl.BlockSpec((32, 128), lambda g, t: (0, at(g, t))),
            pl.BlockSpec((8, 128), lambda g, t: (0, at(g, t))),
        ],
        scratch_shapes=[pltpu.VMEM((16, 128, 128), f32), pltpu.VMEM((16, 16, 128), f32)],
    )
    return pl.pallas_call(
        lambda *refs: assemble_body(half, *refs),
        grid_spec=grid_spec,
        out_shape=[
            shape((1024, 1024), f32),
            shape((1024, 512), f32),
            shape((1024, 512), f32),
            shape((1024, 1024), f32),
            shape((32, 1024), f32),
            shape((8, 1024), f32),
        ],
        input_output_aliases={10 + n: n for n in range(len(begun))},
        compiler_params=pltpu.CompilerParams(vmem_limit_bytes=24 * 1024 * 1024),
        cost_estimate=pl.CostEstimate(flops=30 * 10**9, bytes_accessed=1024, transcendentals=0),
        name="assemble",
    )(table, *parts, wq, wk, wv, gain, after, *begun)


def widen_body(up, down, token, up_out, down_out):
    up_out[...] = up[...].astype(f32)
    down_out[...] = down[...].astype(f32)


def widen(up, down, after):
    def spec(rows):
        return pl.BlockSpec((1, rows, D), lambda e, n: (e, n, 0))

    return pl.pallas_call(
        widen_body,
        grid=(2, 4),
        in_specs=[spec(256), spec(128), ANY],
        out_specs=[spec(256), spec(128)],
        out_shape=[shape((2, D, 2 * FF), f32), shape((2, FF, D), f32)],
        compiler_params=pltpu.CompilerParams(vmem_limit_bytes=16 * 1024 * 1024),
        name="widen",
    )(up, down, after)


def on_device(
    hidden_in,
    routes,
    first_gain,
    query_weight,
    key_weight,
    value_weight,
    output_weight,
    second_gain,
    router_weight,
    gateup_weight,
    down_weight,
    cotangent,
):
    at = Place()
    z, core = at.z, at.core
    order = Order()
    steps = jnp.arange(4)
    gain_one = first_gain.astype(f32)[None]
    gain_two = second_gain.astype(f32)[None]
    router_t = router_weight.T
    inverse = 10000.0 ** (-np.arange(0, HD, 2).astype(np.float32) / HD)
    angles = inverse[:, None] * np.arange(SEQ).astype(np.float32)[None, :]
    cos_all, sin_all = np.cos(angles).astype(np.float32), np.sin(angles).astype(np.float32)

    def by_source(table):
        return held_outside(jnp.asarray(table.reshape(HD // 2, 16, TOK).transpose(1, 0, 2)))

    cot_packed, codes = order.call(
        pack_body, [shape((TOK + 16, D)), shape((EXPERTS, TOK), f32)], [cotangent, routes.T], name="pack"
    )
    cot_all = held_outside(lax.all_gather(cot_packed, "expert", axis=0, tiled=False))
    to_heads, normed_one = order.call(
        project_body,
        [shape((16, 192, TOK)), shape((TOK, D))],
        [
            hidden_in,
            gain_one,
            held_outside(query_weight),
            held_outside(key_weight),
            held_outside(value_weight),
            by_source(cos_all),
            by_source(sin_all),
        ],
        specs=[VM, VM, HBM, HBM, HBM, HBM, HBM],
        scratch=[
            pltpu.VMEM((D, D), bf16),
            pltpu.VMEM((D, 512), bf16),
            pltpu.VMEM((D, 512), bf16),
            pltpu.VMEM((HD // 2, TOK), f32),
            pltpu.VMEM((HD // 2, TOK), f32),
            pltpu.SemaphoreType.DMA((14,)),
        ],
        name="project",
    )
    at_heads = lax.all_to_all(to_heads, "expert", split_axis=0, concat_axis=0, tiled=True)
    att_send, att, totals, qkv = order.call(
        attend_body,
        [shape((16, HD, TOK)), outside((HD, SEQ), f32), shape((1, SEQ), f32), outside((192, SEQ))],
        [at_heads],
        out_specs=[VM, HBM, VM, HBM],
        scratch=[pltpu.VMEM((HD, SEQ), f32), pltpu.VMEM((192, SEQ), bf16), pltpu.SemaphoreType.DMA((9,))],
        name="attend",
    )
    att_t = lax.all_to_all(att_send, "expert", split_axis=0, concat_axis=0, tiled=True)
    middle, scale_two, normed_two = order.call(
        middle_body,
        [shape((TOK, D), f32), shape((TOK, 128), f32), shape((TOK, D))],
        [att_t, hidden_in, output_weight, gain_two],
        name="middle",
    )
    row = order.stack(gather_axis(normed_two, along_u))
    chunks = gather_axis(row, along_v)
    worked = {}
    for i in (0, 1, 3, 2):
        worked[i] = order.call(
            lambda *refs, i=i: expert_body(i, *refs),
            [
                shape((4, TOK + 16, D)),
                outside((2, 256, D)),
                outside((2, 256, D)),
                outside((2, 256, FF)),
                outside((2, 256, 2 * FF)),
            ],
            [chunks[i], cot_all, router_t, gateup_weight, down_weight],
            specs=[VM, HBM, VM, VM, VM],
            out_specs=[VM, HBM, HBM, HBM, HBM],
            scratch=[
                pltpu.VMEM((4, TOK + 16, D), bf16),
                pltpu.VMEM((2, 256, D), bf16),
                pltpu.VMEM((2, 256, D), bf16),
                pltpu.VMEM((2, 256, FF), bf16),
                pltpu.VMEM((2, 256, 2 * FF), bf16),
                pltpu.VMEM((4, TOK, D), bf16),
                pltpu.SemaphoreType.DMA((10,)),
            ],
            us=6,
            limit=24,
            name="experts",
        )
    parts = sum_axis([worked[i][0] for i in range(4)], along_v)
    normed_parts = gather_axis(normed_one, along_u)
    saved = [[held_outside(worked[i][k]) for i in range(4)] for k in range(1, 5)]
    gateup_grad, down_grad = order.call(
        expert_grad_body,
        [outside((2, D, 2 * FF)), outside((2, FF, D))],
        [*saved[0], *saved[1], *saved[2], *saved[3]],
        specs=[HBM] * 16,
        scratch=[
            pltpu.VMEM((2, 1024, D), bf16),
            pltpu.VMEM((2, 1024, D), bf16),
            pltpu.VMEM((2, 1024, FF), bf16),
            pltpu.VMEM((2, 1024, 2 * FF), bf16),
            pltpu.VMEM((2, D, 2 * FF), bf16),
            pltpu.VMEM((2, FF, D), bf16),
            pltpu.SemaphoreType.DMA((44,)),
        ],
        out_specs=[HBM] * 2,
        limit=40,
        us=11,
        name="expert_grads",
    )
    gateup_grad, down_grad = lax.psum((gateup_grad, down_grad), "dp")
    results = order.call(
        expert_result_body,
        [shape((4, TOK, D))] * 4,
        [*[worked[i][3] for i in range(4)], down_weight, cot_all],
        specs=[VM] * 5 + [HBM],
        scratch=[
            pltpu.VMEM((16, TOK, D), bf16),
            pltpu.VMEM((16, 16, D), bf16),
            pltpu.SemaphoreType.DMA((16,)),
        ],
        limit=24,
        us=5,
        name="expert_results",
    )
    grad_rows = sum_axis(order.sum4(parts, "sum_grads"), along_u)
    normed_all = gather_axis(order.stack(normed_parts), along_v)
    normed_all = [held_outside(part) for part in normed_all]
    grad_middle, grad_middle_low, to_back, router_grad, second_part = order.call(
        norm_back_body,
        [
            outside((TOK, D), f32),
            shape((TOK, D)),
            shape((H, HD, TOK)),
            shape((EXPERTS, D), f32),
            shape((1, D), f32),
        ],
        [
            *grad_rows,
            normed_two,
            middle,
            scale_two,
            gain_two,
            cotangent,
            codes,
            router_t,
            held_outside(output_weight),
        ],
        specs=[VM] * 11 + [HBM],
        out_specs=[pl.BlockSpec(), VM, VM, VM, VM],
        scratch=[pltpu.VMEM((D, D), bf16), pltpu.SemaphoreType.DMA],
        name="norm_back",
    )
    at_back = lax.all_to_all(to_back, "expert", split_axis=0, concat_axis=0, tiled=True)
    o_near, o_far = order.call(
        output_grad_body,
        [shape((4, 16, 80, 128))] * 2,
        [att_t, grad_middle_low, router_grad, second_part],
        scratch=[pltpu.VMEM((H, 80, D), bf16)],
        limit=24,
        us=2,
        after=(at_back,),
        name="output_grad",
    )
    o_far = send(o_far, other_core())
    (to_tokens,) = order.call(
        attend_back_body,
        [shape((16, 192, TOK))],
        [at_back, held_outside(qkv), held_outside(att), totals, jnp.asarray(cos_all), jnp.asarray(sin_all)],
        specs=[VM, HBM, HBM, VM, VM, VM],
        limit=24,
        scratch=[
            pltpu.VMEM((HD, SEQ), f32),
            pltpu.VMEM((HD, SEQ), f32),
            pltpu.VMEM((HD, SEQ), f32),
            pltpu.VMEM((HD, SEQ), bf16),
            pltpu.VMEM((192, SEQ), bf16),
            pltpu.VMEM((HD, SEQ), f32),
            pltpu.SemaphoreType.DMA((2,)),
        ],
        us=8,
        name="attend_back",
    )
    at_tokens = lax.all_to_all(to_tokens, "expert", split_axis=0, concat_axis=0, tiled=True)
    o_parts = sum_axis(order.sum4([o_near, o_far], "sum_output"), along_z)
    near, far = order.call(
        weight_grad_body,
        [shape((4, 192, 128))] * 2,
        [to_tokens, *normed_all],
        specs=[VM] + [HBM] * 4,
        scratch=[pltpu.VMEM((192, SEQ), bf16), pltpu.VMEM((4, 4, TOK, D), bf16), pltpu.SemaphoreType.DMA((4,))],
        limit=24,
        us=4,
        name="weight_grad",
    )
    o_parts = sum_axis(
        order.call(split_sum_body, [shape((4, 80, 128))] * 4, o_parts, name="sum_output"), along_v
    )
    pieces = order.call(core_sum_body, [shape((192, 128))] * 4, [near, send(far, other_core())], name="core_sum")
    pieces = sum_axis(pieces, along_z)
    o_parts = sum_axis(order.sum4(o_parts, "sum_output"), along_u)
    result_rows = sum_axis(order.sum4(sum_axis(results, along_v), "sum_results"), along_u)
    mine, pair = order.call(z_sum_body, [shape((128, 128)), shape((64, 128))], pieces, name="z_sum")
    (block,) = order.call(pair_sum_body, [shape((208, 128))], [mine, send(pair, pair_head()), *o_parts], name="pair_sum")
    block = order.stack(gather_axis(block, along_z))
    block = gather_axis(block, along_u)
    (layer_out,) = order.call(finish_body, [shape((TOK, D))], [middle, *result_rows], name="finish")
    (hidden_grad,) = order.call(
        hidden_grad_body,
        [shape((TOK, D))],
        [
            at_tokens,
            hidden_in,
            gain_one,
            grad_middle,
            held_outside(query_weight),
            held_outside(key_weight),
            held_outside(value_weight),
        ],
        specs=[VM] * 4 + [HBM] * 3,
        scratch=[
            pltpu.VMEM((D, D), bf16),
            pltpu.VMEM((D, 512), bf16),
            pltpu.VMEM((D, 512), bf16),
            pltpu.SemaphoreType.DMA((6,)),
        ],
        us=3,
        name="hidden_grad",
    )
    block = gather_axis(order.stack(block), along_v)
    gateup_grad, down_grad = widen(held_outside(gateup_grad), held_outside(down_grad), order.last[0])
    order.last = (down_grad,)
    others = [send(part, other_core()) for part in block]
    i, j = steps[:, None], steps[None, :]
    own_blocks = jnp.concatenate([core * 4 + (z + steps) % 4, (1 - core) * 4 + (z + steps) % 4])
    table = jnp.concatenate([own_blocks, at.source(i, j).reshape(-1), at.source(i, j, 1 - core).reshape(-1)])
    table = table.astype(jnp.int32)
    weights = (query_weight, key_weight, value_weight, first_gain.astype(f32)[:, None])
    begun = assemble(0, table, block, *weights, down_grad)
    query_grad, key_grad, value_grad, output_grad, router_out, ends = assemble(
        1, table, others, *weights, hidden_grad, begun
    )
    return (
        layer_out,
        hidden_grad,
        gateup_grad,
        down_grad,
        query_grad,
        key_grad,
        value_grad,
        output_grad,
        router_out.T,
        ends[0],
        ends[1],
    )


def solution(mesh):
    rows = P(("dp", "expert"), None)
    experts = P("expert", None, None)
    return jax.shard_map(
        on_device,
        mesh=mesh,
        in_specs=(rows, rows, P(), P(), P(), P(), P(), P(), P(), experts, experts, rows),
        out_specs=(rows, rows, experts, experts, P(), P(), P(), P(), P(), P(), P()),
        check_vma=False,
    )
```

```python
import jax
import jax.numpy as jnp
import numpy as np
from jax import lax
from jax.experimental import pallas as pl
from jax.experimental.pallas import tpu as pltpu
from jax.sharding import PartitionSpec as P

D = 1024
H = 16
KV = 8
HD = 64
FF = 512
TOP = 8
EXPERTS = 32
CAPACITY = 64
TOK = 128
SEQ = 2048

epsilon = 1e-06
score_scale = 0.015625

bf16 = jnp.bfloat16
f32 = jnp.float32
AXES = ("dp", "expert")

NT = (((1,), (1,)), ((), ()))
TN = (((0,), (0,)), ((), ()))

VM = pl.BlockSpec(memory_space=pltpu.VMEM)
HBM = pl.BlockSpec(memory_space=pltpu.HBM)
ANY = pl.BlockSpec(memory_space=pl.ANY)


def dot(a, b):
    return jnp.dot(a, b, preferred_element_type=f32)


def dot_nt(a, b):
    return lax.dot_general(a, b, NT, preferred_element_type=f32)


def dot_tn(a, b):
    return lax.dot_general(a, b, TN, preferred_element_type=f32)


def moves(step):
    pairs = []
    for z in range(4):
        for c in range(2):
            for x in range(4):
                for y in range(4):
                    z2, c2, x2, y2 = step(z, c, x, y)
                    target = (((z2 % 4) * 2 + c2 % 2) * 4 + x2 % 4) * 4 + y2 % 4
                    pairs.append((((z * 2 + c) * 4 + x) * 4 + y, target))
    return pairs


def along_u(n):
    return moves(lambda z, c, x, y: (z, c, x, y + n) if c == 0 else (z, c, x + n, y))


def along_v(n):
    return moves(lambda z, c, x, y: (z, c, x + n, y) if c == 0 else (z, c, x, y + n))


def along_z(n):
    return moves(lambda z, c, x, y: (z + n, c, x, y))


def other_core():
    return moves(lambda z, c, x, y: (z, c + 1, x, y))


def pair_head():
    return moves(lambda z, c, x, y: (z, c, x, y ^ 1))


def other_pair():
    return moves(lambda z, c, x, y: (z, c + 1, x, y ^ 1))


def send(array, pairs):
    return lax.ppermute(array, AXES, pairs)


def gather_axis(array, along):
    return [array] + [send(array, along(-n)) for n in (1, 2, 3)]


def sum_axis(parts, along):
    return [parts[0]] + [send(parts[n], along(n)) for n in (1, 2, 3)]


def added(parts):
    total = parts[0].astype(f32)
    for part in parts[1:]:
        total = total + part.astype(f32)
    return total


class Place:
    def __init__(self):
        dp, self.me = lax.axis_index("dp"), lax.axis_index("expert")
        self.z, self.core = lax.div(dp, 2), lax.rem(dp, 2)
        self.x, self.y = lax.div(self.me, 4), lax.rem(self.me, 4)

    def source(self, i, j, core=None):
        core = self.core if core is None else core
        zero = lax.rem(self.x + i, 4) * 4 + lax.rem(self.y + j, 4)
        one = lax.rem(self.x + j, 4) * 4 + lax.rem(self.y + i, 4)
        return jnp.where(core == 0, zero, one)


class Order:
    def __init__(self):
        self.last = ()

    def call(self, body, outs, args, scratch=(), specs=None, out_specs=None, limit=16, us=1, name=None, after=()):
        before = self.last + tuple(after)
        count, skip = len(args), len(before)

        def run(*refs):
            body(*refs[:count], *refs[count + skip :])

        results = pl.pallas_call(
            run,
            out_shape=outs,
            in_specs=(list(specs) if specs is not None else [VM] * count) + [ANY] * skip,
            out_specs=out_specs if out_specs is not None else [VM] * len(outs),
            scratch_shapes=list(scratch),
            compiler_params=pltpu.CompilerParams(vmem_limit_bytes=limit * 1024 * 1024),
            cost_estimate=pl.CostEstimate(flops=us * 10**9, bytes_accessed=1024, transcendentals=0),
            name=name,
        )(*args, *before)
        self.last = (results[0],)
        return results

    def stack(self, parts, after=()):
        kind = shape((4, *parts[0].shape), parts[0].dtype)
        return self.call(stack_body, [kind], parts, after=after, name="stack")[0]

    def sum4(self, parts, name):
        return self.call(sum4_body, [shape(parts[0].shape[1:])] * 4, parts, name=name)


def shape(dims, kind=bf16):
    return jax.ShapeDtypeStruct(dims, kind)


def outside(dims, kind=bf16):
    return pltpu.HBM(dims, kind)


def held_outside(array):
    return pltpu.with_memory_space_constraint(array, pltpu.HBM)


def stack_body(*refs):
    for n in range(4):
        refs[4][n] = refs[n][...]


def split_body(right, left, first, last):
    first[...] = right[0:2]
    last[...] = left[2:4]


def rows_at(refs, j):
    return refs[j * len(refs) // 4].at[j % (4 // len(refs))]


def unpacked(rows):
    return jnp.concatenate([rows[:, TOK * c : TOK * c + TOK] for c in range(8)], 0)


def project_body(hid, gain, routes, wq, wk, wv, cosine, sine, out, normed, codes, wq_v, wk_v, wv_v, cos_v, sin_v, sems):
    me = lax.axis_index("expert")
    copies = []
    for weight, held in ((wk, wk_v), (wv, wv_v), (wq, wq_v)):
        for n in range(4):
            here = pl.ds(256 * n, 256)
            copies.append(pltpu.make_async_copy(weight.at[here], held.at[here], sems.at[len(copies)]))
    copies.append(pltpu.make_async_copy(cosine.at[me], cos_v, sems.at[12]))
    copies.append(pltpu.make_async_copy(sine.at[me], sin_v, sems.at[13]))
    for copy in copies:
        copy.start()
    hidden = hid[...].astype(f32)
    r1 = lax.rsqrt(jnp.mean(hidden * hidden, -1, keepdims=True) + epsilon)
    n1 = (hidden * r1 * gain[...]).astype(bf16)
    normed[...] = n1
    index = lax.broadcasted_iota(jnp.int32, (EXPERTS, TOK), 0)
    chosen = index < 0
    for j in range(TOP):
        chosen = chosen | (routes[j : j + 1] == index)
    rows = lax.broadcasted_iota(jnp.int32, (TOK, TOK), 0)
    cols = lax.broadcasted_iota(jnp.int32, (TOK, TOK), 1)
    rank = dot(chosen.astype(f32).astype(bf16), (rows < cols).astype(f32).astype(bf16))
    code = jnp.where(chosen & (rank < CAPACITY), rank, jnp.where(chosen, -1.0, -2.0))
    codes[...] = code
    for copy in copies[12:] + copies[:4]:
        copy.wait()
    cos = cos_v[...][None]
    sin = sin_v[...][None]

    def rotated(value, heads):
        value = value.T.reshape(heads, HD, TOK)
        a, b = value[:, : HD // 2], value[:, HD // 2 :]
        return jnp.concatenate([a * cos - b * sin, b * cos + a * sin], 1).astype(bf16)

    key = rotated(dot(n1, wk_v[...]), KV)
    for copy in copies[4:8]:
        copy.wait()
    value = dot(n1, wv_v[...]).T.reshape(KV, HD, TOK).astype(bf16)
    for copy in copies[8:12]:
        copy.wait()
    query = rotated(dot(n1, wq_v[...]), H)
    for h in range(H):
        out[h, 0:64] = query[h]
        out[h, 64:128] = key[h // 2]
        out[h, 128:192] = value[h // 2]
        out[h, 192:224] = code.astype(bf16)


def attend_body(recv, att_send, att_out, totals, qkv_out, codes, att, qkv, sems):
    for s in range(16):
        qkv[:, 128 * s : 128 * s + 128] = recv[s, 0:192]
        codes[s] = recv[s, 192:224].astype(f32)
    copies = [pltpu.make_async_copy(qkv, qkv_out, sems.at[8])]
    copies[0].start()
    rows = lax.broadcasted_iota(jnp.int32, (256, 256), 0)
    cols = lax.broadcasted_iota(jnp.int32, (256, 256), 1)
    visible = rows <= cols
    for i in range(8):
        here = slice(256 * i, 256 * i + 256)
        query = qkv[0:64, here]
        weights = jnp.exp(dot_tn(qkv[64:128, here], query) * score_scale)
        weights = jnp.where(visible, weights, 0.0)
        total = jnp.sum(weights, 0, keepdims=True)
        mixture = dot(qkv[128:192, here], weights.astype(bf16))
        if i:
            before = slice(0, 256 * i)
            weights = jnp.exp(dot_tn(qkv[64:128, before], query) * score_scale)
            total = total + jnp.sum(weights, 0, keepdims=True)
            mixture = mixture + dot(qkv[128:192, before], weights.astype(bf16))
        mixed = mixture / total
        att[:, here] = mixed
        totals[:, here] = total
        att_send[2 * i] = mixed[:, :128].astype(bf16)
        att_send[2 * i + 1] = mixed[:, 128:].astype(bf16)
        copies.append(pltpu.make_async_copy(att.at[:, pl.ds(256 * i, 256)], att_out.at[:, pl.ds(256 * i, 256)], sems.at[i]))
        copies[-1].start()
    for copy in copies:
        copy.wait()


def middle_body(att_t, hid, wo, gain, middle, scale, normed):
    attended = att_t[...].reshape(D, TOK).T
    mid = hid[...].astype(f32) + dot(attended, wo[...])
    r2 = lax.rsqrt(jnp.mean(mid * mid, -1, keepdims=True) + epsilon)
    middle[...] = mid
    scale[...] = jnp.broadcast_to(r2, scale.shape)
    normed[...] = (mid * r2 * gain[...]).astype(bf16)


def softmax_chosen(logits, codes):
    chosen = codes > -1.5
    top = jnp.max(jnp.where(chosen, logits, -1e30), 0, keepdims=True)
    powers = jnp.where(chosen, jnp.exp(logits - top), 0.0)
    return powers / jnp.sum(powers, 0, keepdims=True)


def row_of(table, index):
    rows = lax.broadcasted_iota(jnp.int32, table.shape, 0)
    return jnp.sum(jnp.where(rows == index, table, 0.0), 0, keepdims=True)


def expert_body(i, *refs):
    n2, (cot, code, router, *refs) = refs[: 1 + (i == 2)], refs[1 + (i == 2) :]
    if i == 0:
        wgu_in, wd_in, part, x_out, g_out, act_out, gb_out, wgu, wd = refs[:9]
    else:
        wgu, wd, part, x_out, g_out, act_out, gb_out = refs[:7]
    cot_v, x, g, act_v, gb, dx, sems = refs[-7:]
    at = Place()
    me = at.me
    fetched = [pltpu.make_async_copy(cot.at[at.source(i, j)], cot_v.at[j], sems.at[6 + j]) for j in range(4)]
    for copy in fetched:
        copy.start()
    weights = []
    if i == 0:
        for e in range(2):
            weights.append(pltpu.make_async_copy(wgu_in.at[e], wgu.at[e], sems.at[10 + 2 * e]))
            weights.append(pltpu.make_async_copy(wd_in.at[e], wd.at[e], sems.at[11 + 2 * e]))
        for copy in weights:
            copy.start()
    slots = lax.broadcasted_iota(jnp.int32, (CAPACITY, TOK), 0).astype(f32)
    places = []
    gates = []
    for j in range(4):
        rows = rows_at(n2, j)[...]
        logits = dot_nt(router[...], rows)
        fetched[j].wait()
        codes = code[at.source(i, j)]
        prob = softmax_chosen(logits, codes)
        where = [row_of(codes, 2 * me + e) == slots for e in range(2)]
        places.append(jnp.concatenate([w.astype(f32) for w in where], 0).astype(bf16))
        gates.append([jnp.sum(jnp.where(where[e], row_of(prob, 2 * me + e), 0.0), 1, keepdims=True) for e in range(2)])
        here = slice(64 * j, 64 * j + 64)
        picked = dot(places[j], rows).astype(bf16)
        x[0, here] = picked[:64]
        x[1, here] = picked[64:]
        picked = dot(places[j], cot_v[j]).astype(bf16)
        g[0, here] = picked[:64]
        g[1, here] = picked[64:]
    copies = [pltpu.make_async_copy(x, x_out, sems.at[0]), pltpu.make_async_copy(g, g_out, sems.at[1])]
    for copy in copies:
        copy.start()
    grad_gates = []
    for e in range(2):
        for copy in weights[2 * e : 2 * e + 2]:
            copy.wait()
        both = dot(x[e], wgu[e])
        active = dot_nt(g[e], wd[e])
        gate, up = both[:, :FF], both[:, FF:]
        s = 1.0 / (1.0 + jnp.exp(-gate))
        silu = gate * s
        act = silu * up
        weight = jnp.concatenate([gates[j][e] for j in range(4)], 0)
        act_v[e] = (act * weight).astype(bf16)
        grad_gates.append(jnp.sum(act * active, 1, keepdims=True))
        grad_active = active * weight
        gb[e, :, :FF] = (grad_active * up * s * (1.0 + gate * (1.0 - s))).astype(bf16)
        gb[e, :, FF:] = (grad_active * silu).astype(bf16)
        for n, (held, out) in enumerate(((act_v, act_out), (gb, gb_out))):
            copies.append(pltpu.make_async_copy(held.at[e], out.at[e], sems.at[2 + 2 * e + n]))
            copies[-1].start()
        grad_x = dot_nt(gb[e], wgu[e]).astype(bf16)
        for j in range(4):
            dx[j, 64 * e : 64 * e + 64] = grad_x[64 * j : 64 * j + 64]
    lane = lax.broadcasted_iota(jnp.int32, (16, D), 1) // TOK
    row = lax.broadcasted_iota(jnp.int32, (16, D), 0)
    cell = jnp.where(row < 4, lane * 4 + row, -1)
    for j in range(4):
        part[j, 0:TOK] = dot_tn(places[j], dx[j]).astype(bf16)
        tail = jnp.zeros((16, D), f32)
        for e in range(2):
            column = grad_gates[e][64 * j : 64 * j + 64]
            value = jnp.sum(places[j][64 * e : 64 * e + 64].astype(f32) * column, 0, keepdims=True)
            tail = jnp.where(cell == 2 * me + e, jnp.concatenate([value] * 8, 1), tail)
        part[j, TOK : TOK + 16] = tail.astype(bf16)
    for copy in copies:
        copy.wait()


def expert_grad_body(*refs):
    x, g, act, gb = refs[0:4], refs[4:8], refs[8:12], refs[12:16]
    done, gu_out, down_out, xs, gs, acts, gbs, up_v, down_v, sems = refs[16:]
    done[...] = jnp.zeros_like(done)
    written = []
    copies = []
    for e in range(2):
        for i in range(4):
            here = pl.ds(256 * i, 256)
            for n, (ref, held) in enumerate(((x[i], xs), (gb[i], gbs), (act[i], acts), (g[i], gs))):
                copies.append(pltpu.make_async_copy(ref.at[e], held.at[e, here], sems.at[16 * e + 4 * i + n]))
    for copy in copies:
        copy.start()
    for e in range(2):
        for copy in copies[16 * e : 16 * e + 16]:
            copy.wait()
        for b in range(4):
            here = slice(256 * b, 256 * b + 256)
            up_v[e, here] = dot_tn(xs[e, :, here], gbs[e]).astype(bf16)
            written.append(pltpu.make_async_copy(up_v.at[e, here], gu_out.at[e, here], sems.at[32 + 6 * e + b]))
            written[-1].start()
        for b in range(2):
            here = slice(256 * b, 256 * b + 256)
            down_v[e, here] = dot_tn(acts[e, :, here], gs[e]).astype(bf16)
            written.append(pltpu.make_async_copy(down_v.at[e, here], down_out.at[e, here], sems.at[36 + 6 * e + b]))
            written[-1].start()
    for copy in written:
        copy.wait()


def expert_result_body(a0, a1, a2, a3, wd, code, done, out, rows_v, out_v, sems):
    at = Place()
    done[...] = jnp.zeros_like(done)
    slots = lax.broadcasted_iota(jnp.int32, (CAPACITY, TOK), 0).astype(f32)
    for i, act in enumerate((a0, a1, a2, a3)):
        for e in range(2):
            result = dot(act[e], wd[e]).astype(bf16)
            for j in range(4):
                rows_v[4 * i + j, 64 * e : 64 * e + 64] = result[64 * j : 64 * j + 64]
    written = []
    for r in range(16):
        codes = code[at.source(r // 4, r % 4)]
        place = [(row_of(codes, 2 * at.me + e) == slots).astype(f32) for e in range(2)]
        out_v[r] = dot_tn(jnp.concatenate(place, 0).astype(bf16), rows_v[r]).astype(bf16)
        written.append(pltpu.make_async_copy(out_v.at[r], out.at[at.source(r // 4, r % 4)], sems.at[r]))
        written[-1].start()
    for copy in written:
        copy.wait()


def norm_back_body(
    p0, p1, p2, p3, n2, middle, scale, gain, cot, code, router, wo, grad_mid, low_mid, datt, router_grad, second, wo_v, sem
):
    fetch = pltpu.make_async_copy(wo, wo_v, sem)
    fetch.start()
    total = added([p0[...], p1[...], p2[...], p3[...]])
    grad = total[:TOK]
    grad_gate = unpacked(total[TOK : TOK + 4])
    rows = n2[...]
    prob = softmax_chosen(dot_nt(router[...], rows), code[...])
    grad_chosen = prob * (grad_gate - jnp.sum(prob * grad_gate, 0, keepdims=True))
    grad_logits = grad_chosen.astype(bf16)
    router_grad[...] = dot(grad_logits, rows)
    grad = grad + dot_tn(grad_logits, router[...])
    mid = middle[...]
    r2 = scale[:, 0:1]
    g2 = grad * gain[...]
    second[...] = jnp.sum(grad * mid * r2, 0, keepdims=True)
    grad_middle = cot[...].astype(f32) + r2 * g2 - mid * r2 * r2 * r2 * jnp.mean(g2 * mid, -1, keepdims=True)
    grad_mid[...] = grad_middle
    low = grad_middle.astype(bf16)
    low_mid[...] = low
    fetch.wait()
    datt[...] = dot_nt(wo_v[...], low).astype(bf16).reshape(H, HD, TOK)


def touch_body(array, out):
    out[...] = jnp.zeros_like(out)


def finish_body(middle, result, out):
    out[...] = (middle[...] + result[...].astype(f32)).astype(bf16)


def sum4_body(*refs):
    for n in range(4):
        refs[n - 4][...] = added([ref[n] for ref in refs[:-4]]).astype(bf16)


def attend_back_body(datt, qkv_in, att_in, totals, cosine, sine, out, dq, dk, dv, dmix, qkv, att, sems):
    copies = [pltpu.make_async_copy(qkv_in, qkv, sems.at[0]), pltpu.make_async_copy(att_in, att, sems.at[1])]
    for copy in copies:
        copy.start()
    for s in range(16):
        dmix[:, 128 * s : 128 * s + 128] = datt[s]
    rows = lax.broadcasted_iota(jnp.int32, (256, 256), 0)
    cols = lax.broadcasted_iota(jnp.int32, (256, 256), 1)
    visible = rows <= cols
    dk[...] = jnp.zeros_like(dk)
    dv[...] = jnp.zeros_like(dv)
    for copy in copies:
        copy.wait()
    for i in range(8):
        here = slice(256 * i, 256 * i + 256)
        query = qkv[0:64, here]
        inverse = 1.0 / totals[:, here]
        grad_att = dmix[:, here].astype(f32)
        delta = jnp.sum(grad_att * att[:, here], 0, keepdims=True) * inverse
        grad_mix = (grad_att * inverse).astype(bf16)
        for at, diagonal in ((slice(0, 256 * i), False), (here, True)):
            if at.stop == 0:
                continue
            key = qkv[64:128, at]
            weights = jnp.exp(dot_tn(key, query) * score_scale)
            if diagonal:
                weights = jnp.where(visible, weights, 0.0)
            grad_weights = dot_tn(qkv[128:192, at], grad_mix)
            grad_scores = (weights * (grad_weights - delta)).astype(bf16)
            more = dot(key, grad_scores)
            dq[:, here] = more if not diagonal or i == 0 else dq[:, here] + more
            dk[:, at] += dot_nt(query, grad_scores)
            dv[:, at] += dot_nt(grad_mix, weights.astype(bf16))

    def unrotated(value):
        value = value * score_scale
        a, b = value[: HD // 2], value[HD // 2 :]
        cos, sin = cosine[...], sine[...]
        return jnp.concatenate([a * cos + b * sin, b * cos - a * sin], 0).astype(bf16)

    low_q, low_k, low_v = unrotated(dq[...]), unrotated(dk[...]), dv[...].astype(bf16)
    for s in range(16):
        out[s, 0:64] = low_q[:, 128 * s : 128 * s + 128]
        out[s, 64:128] = low_k[:, 128 * s : 128 * s + 128]
        out[s, 128:192] = low_v[:, 128 * s : 128 * s + 128]


def weight_grad_body(own, recv, n1, att, low, router_grad, second, *refs):
    more = refs[: 4 * own]
    outs, rows_v, one_v, low_v = refs[4 * own : -3], refs[-3], refs[-2], refs[-1]
    at = Place()
    core = at.core if own else 1 - at.core
    columns = pl.ds(pl.multiple_of(core * 512, 512), 512)
    got = recv[...]
    query = got[:, 0:64]
    pairs = got[:, 64:192].astype(f32).reshape(KV, 2, 128, TOK)
    pairs = (pairs[:, 0] + pairs[:, 1]).astype(bf16)
    rows = jnp.concatenate([query.reshape(KV, 2, 64, TOK), pairs.reshape(KV, 2, 64, TOK)], 2)
    rows_v[...] = rows.reshape(H, 128, TOK)
    one_v[...] = n1[:, columns]
    low_v[...] = low[:, columns]
    index = lax.broadcasted_iota(jnp.int32, (16, 512), 0)
    for i in range(4):
        for j in range(4):
            h = at.source(i, j, core)
            tail = jnp.where(index == 0, row_of(router_grad[:, columns], 2 * h), 0.0)
            tail = jnp.where(index == 1, row_of(router_grad[:, columns], 2 * h + 1), tail)
            tail = jnp.where((index == 2) & (h == 0), second[:, columns], tail)
            part = jnp.concatenate([dot(rows_v[h], one_v[...]), dot(att[h], low_v[...]), tail], 0)
            if own:
                part = part + more[i][j].astype(f32)
            outs[i][j] = part.astype(bf16)


def place_pieces_body(w0, w1, w2, w3, o0, o1, o2, o3):
    at = Place()
    total = added([w0[...], w1[...], w2[...], w3[...]]).astype(bf16)
    for b in range(4):
        for k, out in enumerate((o0, o1, o2, o3)):

            @pl.when(lax.rem(at.z + k, 4) == b)
            def _(b=b, out=out):
                out[...] = total[:, 128 * b : 128 * b + 128]


def hidden_grad_body(recv, hid, gain, grad_mid, wq_in, wk_in, wv_in, out, wq, wk, wv, sems):
    copies = []
    for n, (source, held) in enumerate(((wk_in, wk), (wv_in, wv), (wq_in, wq))):
        for k in range(2):
            here = pl.ds(512 * k, 512)
            copies.append(pltpu.make_async_copy(source.at[here], held.at[here], sems.at[2 * n + k]))
    for copy in copies:
        copy.start()
    got = recv[...]
    grad_q = got[:, 0:64].reshape(D, TOK).T
    pairs = got[:, 64:192].astype(f32).reshape(KV, 2, 128, TOK)
    pairs = (pairs[:, 0] + pairs[:, 1]).astype(bf16)
    grad_k = pairs[:, 0:64].reshape(KV * HD, TOK).T
    grad_v = pairs[:, 64:128].reshape(KV * HD, TOK).T
    for copy in copies:
        copy.wait()
    grad = dot_nt(grad_k, wk[...]) + dot_nt(grad_v, wv[...]) + dot_nt(grad_q, wq[...])
    hidden = hid[...].astype(f32)
    r1 = lax.rsqrt(jnp.mean(hidden * hidden, -1, keepdims=True) + epsilon)
    g1 = grad * gain[...]
    back = r1 * g1 - hidden * r1 * r1 * r1 * jnp.mean(g1 * hidden, -1, keepdims=True)
    out[...] = (grad_mid[...] + back).astype(bf16)


def z_sum_body(p0, p1, p2, p3, out):
    total = added([p0[...], p1[...], p2[...], p3[...]])
    out[0:128] = total[0:128].T.astype(bf16)
    out[128:208] = total[128:208].astype(bf16)


def assemble_body(half, table, *refs):
    parts = refs[0:4]
    wq, wk, wv, gain = refs[4:8]
    q_out, k_out, v_out, o_out, r_out, e_out, tiles, tails = refs[9 + 6 * half :]
    k = pl.program_id(0)
    for i in range(4):
        for j in range(4):
            h = table[8 + 16 * half + 4 * i + j]
            block = parts[i][j, k]
            tiles[h] = block[0:128].astype(f32)
            o_out[pl.ds(pl.multiple_of(h * 64, 64), 64)] = block[128:192].astype(f32)
            tails[h] = block[192:208].astype(f32)
    for p in range(8):
        q_out[:, 128 * p : 128 * p + 128] = jnp.concatenate([tiles[2 * p][:, :64], tiles[2 * p + 1][:, :64]], 1)
    for m in range(4):
        here = slice(128 * m, 128 * m + 128)
        k_out[:, here] = jnp.concatenate([tiles[4 * m][:, 64:], tiles[4 * m + 2][:, 64:]], 1)
        v_out[:, here] = jnp.concatenate([tiles[4 * m + 1][:, 64:], tiles[4 * m + 3][:, 64:]], 1)
    for h in range(16):
        r_out[2 * h : 2 * h + 2] = tails[h][0:2]
    total = jnp.sum(q_out[...] * wq[...].astype(f32), 1, keepdims=True)
    total = total + jnp.sum(k_out[...] * wk[...].astype(f32), 1, keepdims=True)
    total = total + jnp.sum(v_out[...] * wv[...].astype(f32), 1, keepdims=True)
    first = jnp.broadcast_to(total / gain[...], (128, 128)).T
    index = lax.broadcasted_iota(jnp.int32, (8, 128), 0)
    e_out[...] = jnp.where(index == 0, first[0:8], jnp.broadcast_to(tails[0][2:3], (8, 128)))


def assemble(half, table, parts, wq, wk, wv, gain, after, begun=()):
    def at(g, t):
        return t[4 * half + g]

    rows = pl.BlockSpec((128, 1024), lambda g, t: (at(g, t), 0))
    half_rows = pl.BlockSpec((128, 512), lambda g, t: (at(g, t), 0))
    column = pl.BlockSpec((128, 1), lambda g, t: (at(g, t), 0))
    grid_spec = pltpu.PrefetchScalarGridSpec(
        num_scalar_prefetch=1,
        grid=(4,),
        in_specs=[VM] * 4 + [rows, half_rows, half_rows, column, ANY] + [ANY] * len(begun),
        out_specs=[
            rows,
            half_rows,
            half_rows,
            pl.BlockSpec((1024, 128), lambda g, t: (0, at(g, t))),
            pl.BlockSpec((32, 128), lambda g, t: (0, at(g, t))),
            pl.BlockSpec((8, 128), lambda g, t: (0, at(g, t))),
        ],
        scratch_shapes=[pltpu.VMEM((16, 128, 128), f32), pltpu.VMEM((16, 16, 128), f32)],
    )
    return pl.pallas_call(
        lambda *refs: assemble_body(half, *refs),
        grid_spec=grid_spec,
        out_shape=[
            shape((1024, 1024), f32),
            shape((1024, 512), f32),
            shape((1024, 512), f32),
            shape((1024, 1024), f32),
            shape((32, 1024), f32),
            shape((8, 1024), f32),
        ],
        input_output_aliases={10 + n: n for n in range(len(begun))},
        compiler_params=pltpu.CompilerParams(vmem_limit_bytes=24 * 1024 * 1024),
        cost_estimate=pl.CostEstimate(flops=30 * 10**9, bytes_accessed=1024, transcendentals=0),
        name="assemble",
    )(table, *parts, wq, wk, wv, gain, after, *begun)


def widen_body(up, down, token, up_out, down_out, done):
    done[...] = jnp.zeros_like(done)
    up_out[...] = up[...].astype(f32)
    down_out[...] = down[...].astype(f32)


def widen(up, down, after):
    def spec(rows):
        return pl.BlockSpec((1, rows, D), lambda e, n: (e, n, 0))

    return pl.pallas_call(
        widen_body,
        grid=(2, 4),
        in_specs=[spec(256), spec(128), ANY],
        out_specs=[spec(256), spec(128), pl.BlockSpec((8, 128), lambda e, n: (0, 0))],
        out_shape=[outside((2, D, 2 * FF), f32), outside((2, FF, D), f32), shape((8, 128), f32)],
        compiler_params=pltpu.CompilerParams(vmem_limit_bytes=16 * 1024 * 1024),
        name="widen",
    )(up, down, after)


def on_device(
    hidden_in,
    routes,
    first_gain,
    query_weight,
    key_weight,
    value_weight,
    output_weight,
    second_gain,
    router_weight,
    gateup_weight,
    down_weight,
    cotangent,
):
    at = Place()
    z, core = at.z, at.core
    order = Order()
    steps = jnp.arange(4)
    gain_one = first_gain.astype(f32)[None]
    gain_two = second_gain.astype(f32)[None]
    router_t = router_weight.T
    inverse = 10000.0 ** (-np.arange(0, HD, 2).astype(np.float32) / HD)
    angles = inverse[:, None] * np.arange(SEQ).astype(np.float32)[None, :]
    cos_all, sin_all = np.cos(angles).astype(np.float32), np.sin(angles).astype(np.float32)

    def by_source(table):
        return held_outside(jnp.asarray(table.reshape(HD // 2, 16, TOK).transpose(1, 0, 2)))

    cot_all = held_outside(lax.all_gather(cotangent, "expert", axis=0, tiled=False))
    to_heads, normed_one, codes = order.call(
        project_body,
        [shape((16, 224, TOK)), shape((TOK, D)), shape((EXPERTS, TOK), f32)],
        [
            hidden_in,
            gain_one,
            routes.T,
            held_outside(query_weight),
            held_outside(key_weight),
            held_outside(value_weight),
            by_source(cos_all),
            by_source(sin_all),
        ],
        specs=[VM, VM, VM, HBM, HBM, HBM, HBM, HBM],
        scratch=[
            pltpu.VMEM((D, D), bf16),
            pltpu.VMEM((D, 512), bf16),
            pltpu.VMEM((D, 512), bf16),
            pltpu.VMEM((HD // 2, TOK), f32),
            pltpu.VMEM((HD // 2, TOK), f32),
            pltpu.SemaphoreType.DMA((14,)),
        ],
        name="project",
    )
    at_heads = lax.all_to_all(to_heads, "expert", split_axis=0, concat_axis=0, tiled=True)
    att_low, att, totals, qkv, code_all = order.call(
        attend_body,
        [
            shape((16, HD, TOK)),
            outside((HD, SEQ), f32),
            shape((1, SEQ), f32),
            outside((192, SEQ)),
            shape((16, EXPERTS, TOK), f32),
        ],
        [at_heads],
        out_specs=[VM, HBM, VM, HBM, VM],
        scratch=[pltpu.VMEM((HD, SEQ), f32), pltpu.VMEM((192, SEQ), bf16), pltpu.SemaphoreType.DMA((9,))],
        name="attend",
    )
    att_t = lax.all_to_all(att_low, "expert", split_axis=0, concat_axis=0, tiled=True)
    middle, scale_two, normed_two = order.call(
        middle_body,
        [shape((TOK, D), f32), shape((TOK, 128), f32), shape((TOK, D))],
        [att_t, hidden_in, output_weight, gain_two],
        name="middle",
    )
    row = order.stack(gather_axis(normed_two, along_u), after=(cot_all,))
    right, left = send(row, along_v(-1)), send(row, along_v(1))
    chunks = {0: [row], 1: [right], 3: [left]}
    worked = {}
    held = [held_outside(gateup_weight), held_outside(down_weight)]
    for i in (0, 1, 3, 2):
        if i == 3:
            halves = order.call(split_body, [shape((2, TOK, D))] * 2, [right, left], name="split")
            chunks[2] = [send(halves[0], along_v(-1)), send(halves[1], along_v(1))]
        worked[i] = order.call(
            lambda *refs, i=i: expert_body(i, *refs),
            [
                shape((4, TOK + 16, D)),
                outside((2, 256, D)),
                outside((2, 256, D)),
                outside((2, 256, FF)),
                outside((2, 256, 2 * FF)),
            ]
            + ([shape((2, D, 2 * FF)), shape((2, FF, D))] if i == 0 else []),
            [*chunks[i], cot_all, code_all, router_t, *held],
            specs=[VM] * len(chunks[i]) + [HBM, VM, VM] + [HBM if i == 0 else VM] * 2,
            out_specs=[VM, HBM, HBM, HBM, HBM] + [VM] * (2 if i == 0 else 0),
            scratch=[
                pltpu.VMEM((4, TOK, D), bf16),
                pltpu.VMEM((2, 256, D), bf16),
                pltpu.VMEM((2, 256, D), bf16),
                pltpu.VMEM((2, 256, FF), bf16),
                pltpu.VMEM((2, 256, 2 * FF), bf16),
                pltpu.VMEM((4, TOK, D), bf16),
                pltpu.SemaphoreType.DMA((14,)),
            ],
            us=6,
            limit=24,
            name="experts",
        )
        if i == 0:
            held = worked[i][5:]
    parts = sum_axis([worked[i][0] for i in range(4)], along_v)
    saved = [[held_outside(worked[i][k]) for i in range(4)] for k in range(1, 5)]
    done, gateup_grad, down_grad = order.call(
        expert_grad_body,
        [shape((8, 128), f32), outside((2, D, 2 * FF)), outside((2, FF, D))],
        [*saved[0], *saved[1], *saved[2], *saved[3]],
        specs=[HBM] * 16,
        scratch=[
            pltpu.VMEM((2, 1024, D), bf16),
            pltpu.VMEM((2, 1024, D), bf16),
            pltpu.VMEM((2, 1024, FF), bf16),
            pltpu.VMEM((2, 1024, 2 * FF), bf16),
            pltpu.VMEM((2, D, 2 * FF), bf16),
            pltpu.VMEM((2, FF, D), bf16),
            pltpu.SemaphoreType.DMA((44,)),
        ],
        out_specs=[VM, HBM, HBM],
        limit=40,
        us=11,
        name="expert_grads",
    )
    gateup_grad, down_grad = lax.psum((gateup_grad, down_grad), "dp")
    grad_rows = sum_axis(order.sum4(parts, "sum_grads"), along_u)
    grad_middle, grad_middle_low, to_back, router_grad, second_part = order.call(
        norm_back_body,
        [
            outside((TOK, D), f32),
            shape((TOK, D)),
            shape((H, HD, TOK)),
            shape((EXPERTS, D), f32),
            shape((1, D), f32),
        ],
        [
            *grad_rows,
            normed_two,
            middle,
            scale_two,
            gain_two,
            cotangent,
            codes,
            router_t,
            held_outside(output_weight),
        ],
        specs=[VM] * 11 + [HBM],
        out_specs=[pl.BlockSpec(), VM, VM, VM, VM],
        scratch=[pltpu.VMEM((D, D), bf16), pltpu.SemaphoreType.DMA],
        name="norm_back",
    )
    at_back = lax.all_to_all(to_back, "expert", split_axis=0, concat_axis=0, tiled=True)
    (to_tokens,) = order.call(
        attend_back_body,
        [shape((16, 192, TOK))],
        [at_back, held_outside(qkv), held_outside(att), totals, jnp.asarray(cos_all), jnp.asarray(sin_all)],
        specs=[VM, HBM, HBM, VM, VM, VM],
        limit=24,
        scratch=[
            pltpu.VMEM((HD, SEQ), f32),
            pltpu.VMEM((HD, SEQ), f32),
            pltpu.VMEM((HD, SEQ), f32),
            pltpu.VMEM((HD, SEQ), bf16),
            pltpu.VMEM((192, SEQ), bf16),
            pltpu.VMEM((HD, SEQ), f32),
            pltpu.SemaphoreType.DMA((2,)),
        ],
        name="attend_back",
    )
    at_tokens = lax.all_to_all(to_tokens, "expert", split_axis=0, concat_axis=0, tiled=True)
    sources = [at_tokens, normed_one, att_t, grad_middle_low, router_grad, second_part]
    held_rows = [pltpu.VMEM((H, 128, TOK), bf16), pltpu.VMEM((TOK, 512), bf16), pltpu.VMEM((TOK, 512), bf16)]
    far = order.call(
        lambda *refs: weight_grad_body(0, *refs),
        [shape((4, 208, 512))] * 4,
        sources,
        scratch=held_rows,
        limit=24,
        name="weight_grad",
    )
    far = [send(part, other_core()) for part in far]
    (hidden_grad,) = order.call(
        hidden_grad_body,
        [shape((TOK, D))],
        [
            at_tokens,
            hidden_in,
            gain_one,
            grad_middle,
            held_outside(query_weight),
            held_outside(key_weight),
            held_outside(value_weight),
        ],
        specs=[VM] * 4 + [HBM] * 3,
        scratch=[
            pltpu.VMEM((D, D), bf16),
            pltpu.VMEM((D, 512), bf16),
            pltpu.VMEM((D, 512), bf16),
            pltpu.SemaphoreType.DMA((6,)),
        ],
        name="hidden_grad",
    )
    weight_parts = order.call(
        lambda *refs: weight_grad_body(1, *refs),
        [shape((4, 208, 512))] * 4,
        [*sources, *far],
        scratch=held_rows,
        limit=24,
        name="weight_grad",
    )
    weight_parts = sum_axis(weight_parts, along_v)
    done, results = order.call(
        expert_result_body,
        [shape((8, 128), f32), outside((16, TOK, D))],
        [*[worked[i][3] for i in range(4)], down_weight, code_all],
        out_specs=[VM, HBM],
        scratch=[
            pltpu.VMEM((16, TOK, D), bf16),
            pltpu.VMEM((16, TOK, D), bf16),
            pltpu.SemaphoreType.DMA((16,)),
        ],
        limit=24,
        us=5,
        name="expert_results",
    )
    result = lax.psum_scatter(results, "expert", scatter_dimension=0, tiled=False)
    weight_rows = sum_axis(order.sum4(weight_parts, "sum_weights"), along_u)
    order.call(touch_body, [shape((8, 128), f32)], [held_outside(gateup_grad)], specs=[HBM], name="touch")
    pieces = order.call(place_pieces_body, [shape((208, 128))] * 4, weight_rows, name="pieces")
    (block,) = order.call(z_sum_body, [shape((208, 128))], sum_axis(pieces, along_z), name="z_sum")
    block = order.stack(gather_axis(block, along_z))
    block = gather_axis(block, along_u)
    block = gather_axis(order.stack(block), along_v)
    gateup_grad, down_grad, done = widen(held_outside(gateup_grad), held_outside(down_grad), order.last[0])
    order.last = (done,)
    others = [send(part, other_core()) for part in block]
    i, j = steps[:, None], steps[None, :]
    own_blocks = jnp.concatenate([core * 4 + (z + steps) % 4, (1 - core) * 4 + (z + steps) % 4])
    table = jnp.concatenate([own_blocks, at.source(i, j).reshape(-1), at.source(i, j, 1 - core).reshape(-1)])
    table = table.astype(jnp.int32)
    weights = (query_weight, key_weight, value_weight, first_gain.astype(f32)[:, None])
    begun = assemble(0, table, block, *weights, done)
    query_grad, key_grad, value_grad, output_grad, router_out, ends = assemble(
        1, table, others, *weights, done, begun
    )
    order.last = (ends,)
    (layer_out,) = order.call(finish_body, [shape((TOK, D))], [middle, result], name="finish")
    return (
        layer_out,
        hidden_grad,
        gateup_grad,
        down_grad,
        query_grad,
        key_grad,
        value_grad,
        output_grad,
        router_out.T,
        ends[0],
        ends[1],
    )


def solution(mesh):
    rows = P(("dp", "expert"), None)
    experts = P("expert", None, None)
    return jax.shard_map(
        on_device,
        mesh=mesh,
        in_specs=(rows, rows, P(), P(), P(), P(), P(), P(), P(), experts, experts, rows),
        out_specs=(rows, rows, experts, experts, P(), P(), P(), P(), P(), P(), P()),
        check_vma=False,
    )
```

```python
import jax
import jax.numpy as jnp
import numpy as np
from jax import lax
from jax.experimental import pallas as pl
from jax.experimental.pallas import tpu as pltpu
from jax.sharding import PartitionSpec as P

D = 1024
H = 16
KV = 8
HD = 64
FF = 512
TOP = 8
EXPERTS = 32
CAPACITY = 64
TOK = 128
SEQ = 2048

epsilon = 1e-06
score_scale = 0.015625

bf16 = jnp.bfloat16
f32 = jnp.float32
AXES = ("dp", "expert")

NT = (((1,), (1,)), ((), ()))
TN = (((0,), (0,)), ((), ()))

VM = pl.BlockSpec(memory_space=pltpu.VMEM)
HBM = pl.BlockSpec(memory_space=pltpu.HBM)
ANY = pl.BlockSpec(memory_space=pl.ANY)


def dot(a, b):
    return jnp.dot(a, b, preferred_element_type=f32)


def dot_nt(a, b):
    return lax.dot_general(a, b, NT, preferred_element_type=f32)


def dot_tn(a, b):
    return lax.dot_general(a, b, TN, preferred_element_type=f32)


def moves(step):
    pairs = []
    for z in range(4):
        for c in range(2):
            for x in range(4):
                for y in range(4):
                    z2, c2, x2, y2 = step(z, c, x, y)
                    target = (((z2 % 4) * 2 + c2 % 2) * 4 + x2 % 4) * 4 + y2 % 4
                    pairs.append((((z * 2 + c) * 4 + x) * 4 + y, target))
    return pairs


def along_u(n):
    return moves(lambda z, c, x, y: (z, c, x, y + n) if c == 0 else (z, c, x + n, y))


def along_v(n):
    return moves(lambda z, c, x, y: (z, c, x + n, y) if c == 0 else (z, c, x, y + n))


def along_z(n):
    return moves(lambda z, c, x, y: (z + n, c, x, y))


def other_core():
    return moves(lambda z, c, x, y: (z, c + 1, x, y))


def pair_head():
    return moves(lambda z, c, x, y: (z, c, x, y ^ 1))


def other_pair():
    return moves(lambda z, c, x, y: (z, c + 1, x, y ^ 1))


def send(array, pairs):
    return lax.ppermute(array, AXES, pairs)


def gather_axis(array, along):
    return [array] + [send(array, along(-n)) for n in (1, 2, 3)]


def sum_axis(parts, along):
    return [parts[0]] + [send(parts[n], along(n)) for n in (1, 2, 3)]


def added(parts):
    total = parts[0].astype(f32)
    for part in parts[1:]:
        total = total + part.astype(f32)
    return total


class Place:
    def __init__(self):
        dp, self.me = lax.axis_index("dp"), lax.axis_index("expert")
        self.z, self.core = lax.div(dp, 2), lax.rem(dp, 2)
        self.x, self.y = lax.div(self.me, 4), lax.rem(self.me, 4)

    def source(self, i, j, core=None):
        core = self.core if core is None else core
        zero = lax.rem(self.x + i, 4) * 4 + lax.rem(self.y + j, 4)
        one = lax.rem(self.x + j, 4) * 4 + lax.rem(self.y + i, 4)
        return jnp.where(core == 0, zero, one)


class Order:
    def __init__(self):
        self.last = ()

    def call(self, body, outs, args, scratch=(), specs=None, out_specs=None, limit=16, us=1, name=None, after=()):
        before = self.last + tuple(after)
        count, skip = len(args), len(before)

        def run(*refs):
            body(*refs[:count], *refs[count + skip :])

        results = pl.pallas_call(
            run,
            out_shape=outs,
            in_specs=(list(specs) if specs is not None else [VM] * count) + [ANY] * skip,
            out_specs=out_specs if out_specs is not None else [VM] * len(outs),
            scratch_shapes=list(scratch),
            compiler_params=pltpu.CompilerParams(vmem_limit_bytes=limit * 1024 * 1024),
            cost_estimate=pl.CostEstimate(flops=us * 10**9, bytes_accessed=1024, transcendentals=0),
            name=name,
        )(*args, *before)
        self.last = (results[0],)
        return results

    def stack(self, parts, after=()):
        kind = shape((4, *parts[0].shape), parts[0].dtype)
        return self.call(stack_body, [kind], parts, after=after, name="stack")[0]

    def sum4(self, parts, name):
        return self.call(sum4_body, [shape(parts[0].shape[1:])] * 4, parts, name=name)


def shape(dims, kind=bf16):
    return jax.ShapeDtypeStruct(dims, kind)


def outside(dims, kind=bf16):
    return pltpu.HBM(dims, kind)


def held_outside(array):
    return pltpu.with_memory_space_constraint(array, pltpu.HBM)


def stack_body(*refs):
    for n in range(4):
        refs[4][n] = refs[n][...]


def split_body(right, left, first, last):
    first[...] = right[0:2]
    last[...] = left[2:4]


def rows_at(refs, j):
    return refs[j * len(refs) // 4].at[j % (4 // len(refs))]


def unpacked(rows):
    return jnp.concatenate([rows[:, TOK * c : TOK * c + TOK] for c in range(8)], 0)


def project_body(hid, gain, routes, wq, wk, wv, cosine, sine, out, normed, codes, wq_v, wk_v, wv_v, cos_v, sin_v, sems):
    me = lax.axis_index("expert")
    copies = []
    for weight, held in ((wk, wk_v), (wv, wv_v), (wq, wq_v)):
        for n in range(4):
            here = pl.ds(256 * n, 256)
            copies.append(pltpu.make_async_copy(weight.at[here], held.at[here], sems.at[len(copies)]))
    copies.append(pltpu.make_async_copy(cosine.at[me], cos_v, sems.at[12]))
    copies.append(pltpu.make_async_copy(sine.at[me], sin_v, sems.at[13]))
    for copy in copies:
        copy.start()
    hidden = hid[...].astype(f32)
    r1 = lax.rsqrt(jnp.mean(hidden * hidden, -1, keepdims=True) + epsilon)
    n1 = (hidden * r1 * gain[...]).astype(bf16)
    normed[...] = n1
    index = lax.broadcasted_iota(jnp.int32, (EXPERTS, TOK), 0)
    chosen = index < 0
    for j in range(TOP):
        chosen = chosen | (routes[j : j + 1] == index)
    rows = lax.broadcasted_iota(jnp.int32, (TOK, TOK), 0)
    cols = lax.broadcasted_iota(jnp.int32, (TOK, TOK), 1)
    rank = dot(chosen.astype(f32).astype(bf16), (rows < cols).astype(f32).astype(bf16))
    code = jnp.where(chosen & (rank < CAPACITY), rank, jnp.where(chosen, -1.0, -2.0))
    codes[...] = code
    for copy in copies[12:] + copies[:4]:
        copy.wait()
    cos = cos_v[...][None]
    sin = sin_v[...][None]

    def rotated(value, heads):
        value = value.T.reshape(heads, HD, TOK)
        a, b = value[:, : HD // 2], value[:, HD // 2 :]
        return jnp.concatenate([a * cos - b * sin, b * cos + a * sin], 1).astype(bf16)

    key = rotated(dot(n1, wk_v[...]), KV)
    for copy in copies[4:8]:
        copy.wait()
    value = dot(n1, wv_v[...]).T.reshape(KV, HD, TOK).astype(bf16)
    for copy in copies[8:12]:
        copy.wait()
    query = rotated(dot(n1, wq_v[...]), H)
    for h in range(H):
        out[h, 0:64] = query[h]
        out[h, 64:128] = key[h // 2]
        out[h, 128:192] = value[h // 2]
        out[h, 192:224] = code.astype(bf16)


def attend_body(recv, att_send, att_out, totals, qkv_out, codes, att, qkv, sems):
    for s in range(16):
        qkv[:, 128 * s : 128 * s + 128] = recv[s, 0:192]
        codes[s] = recv[s, 192:224].astype(f32)
    copies = [pltpu.make_async_copy(qkv, qkv_out, sems.at[8])]
    copies[0].start()
    rows = lax.broadcasted_iota(jnp.int32, (256, 256), 0)
    cols = lax.broadcasted_iota(jnp.int32, (256, 256), 1)
    visible = rows <= cols
    for i in range(8):
        here = slice(256 * i, 256 * i + 256)
        query = qkv[0:64, here]
        weights = jnp.exp(dot_tn(qkv[64:128, here], query) * score_scale)
        weights = jnp.where(visible, weights, 0.0)
        total = jnp.sum(weights, 0, keepdims=True)
        mixture = dot(qkv[128:192, here], weights.astype(bf16))
        if i:
            before = slice(0, 256 * i)
            weights = jnp.exp(dot_tn(qkv[64:128, before], query) * score_scale)
            total = total + jnp.sum(weights, 0, keepdims=True)
            mixture = mixture + dot(qkv[128:192, before], weights.astype(bf16))
        mixed = mixture / total
        att[:, here] = mixed
        totals[:, here] = total
        att_send[2 * i] = mixed[:, :128].astype(bf16)
        att_send[2 * i + 1] = mixed[:, 128:].astype(bf16)
        copies.append(pltpu.make_async_copy(att.at[:, pl.ds(256 * i, 256)], att_out.at[:, pl.ds(256 * i, 256)], sems.at[i]))
        copies[-1].start()
    for copy in copies:
        copy.wait()


def middle_body(att_t, hid, wo, gain, middle, scale, normed):
    attended = att_t[...].reshape(D, TOK).T
    mid = hid[...].astype(f32) + dot(attended, wo[...])
    r2 = lax.rsqrt(jnp.mean(mid * mid, -1, keepdims=True) + epsilon)
    middle[...] = mid
    scale[...] = jnp.broadcast_to(r2, scale.shape)
    normed[...] = (mid * r2 * gain[...]).astype(bf16)


def softmax_chosen(logits, codes):
    chosen = codes > -1.5
    top = jnp.max(jnp.where(chosen, logits, -1e30), 0, keepdims=True)
    powers = jnp.where(chosen, jnp.exp(logits - top), 0.0)
    return powers / jnp.sum(powers, 0, keepdims=True)


def row_of(table, index):
    rows = lax.broadcasted_iota(jnp.int32, table.shape, 0)
    return jnp.sum(jnp.where(rows == index, table, 0.0), 0, keepdims=True)


def expert_body(i, *refs):
    n2, (cot, code, router, *refs) = refs[: 1 + (i == 2)], refs[1 + (i == 2) :]
    if i == 0:
        wgu_in, wd_in, part, x_out, g_out, act_out, gb_out, wgu, wd = refs[:9]
    else:
        wgu, wd, part, x_out, g_out, act_out, gb_out = refs[:7]
    cot_v, x, g, act_v, gb, dx, sems = refs[-7:]
    at = Place()
    me = at.me
    fetched = [pltpu.make_async_copy(cot.at[at.source(i, j)], cot_v.at[j], sems.at[6 + j]) for j in range(4)]
    for copy in fetched:
        copy.start()
    weights = []
    if i == 0:
        for e in range(2):
            weights.append(pltpu.make_async_copy(wgu_in.at[e], wgu.at[e], sems.at[10 + 2 * e]))
            weights.append(pltpu.make_async_copy(wd_in.at[e], wd.at[e], sems.at[11 + 2 * e]))
        for copy in weights:
            copy.start()
    slots = lax.broadcasted_iota(jnp.int32, (CAPACITY, TOK), 0).astype(f32)
    places = []
    gates = []
    for j in range(4):
        rows = rows_at(n2, j)[...]
        logits = dot_nt(router[...], rows)
        fetched[j].wait()
        codes = code[at.source(i, j)]
        prob = softmax_chosen(logits, codes)
        where = [row_of(codes, 2 * me + e) == slots for e in range(2)]
        places.append(jnp.concatenate([w.astype(f32) for w in where], 0).astype(bf16))
        gates.append([jnp.sum(jnp.where(where[e], row_of(prob, 2 * me + e), 0.0), 1, keepdims=True) for e in range(2)])
        here = slice(64 * j, 64 * j + 64)
        picked = dot(places[j], rows).astype(bf16)
        x[0, here] = picked[:64]
        x[1, here] = picked[64:]
        picked = dot(places[j], cot_v[j]).astype(bf16)
        g[0, here] = picked[:64]
        g[1, here] = picked[64:]
    copies = [pltpu.make_async_copy(x, x_out, sems.at[0]), pltpu.make_async_copy(g, g_out, sems.at[1])]
    for copy in copies:
        copy.start()
    grad_gates = []
    for e in range(2):
        for copy in weights[2 * e : 2 * e + 2]:
            copy.wait()
        both = dot(x[e], wgu[e])
        active = dot_nt(g[e], wd[e])
        gate, up = both[:, :FF], both[:, FF:]
        s = 1.0 / (1.0 + jnp.exp(-gate))
        silu = gate * s
        act = silu * up
        weight = jnp.concatenate([gates[j][e] for j in range(4)], 0)
        act_v[e] = (act * weight).astype(bf16)
        grad_gates.append(jnp.sum(act * active, 1, keepdims=True))
        grad_active = active * weight
        gb[e, :, :FF] = (grad_active * up * s * (1.0 + gate * (1.0 - s))).astype(bf16)
        gb[e, :, FF:] = (grad_active * silu).astype(bf16)
        for n, (held, out) in enumerate(((act_v, act_out), (gb, gb_out))):
            copies.append(pltpu.make_async_copy(held.at[e], out.at[e], sems.at[2 + 2 * e + n]))
            copies[-1].start()
        grad_x = dot_nt(gb[e], wgu[e]).astype(bf16)
        for j in range(4):
            dx[j, 64 * e : 64 * e + 64] = grad_x[64 * j : 64 * j + 64]
    lane = lax.broadcasted_iota(jnp.int32, (16, D), 1) // TOK
    row = lax.broadcasted_iota(jnp.int32, (16, D), 0)
    cell = jnp.where(row < 4, lane * 4 + row, -1)
    for j in range(4):
        part[j, 0:TOK] = dot_tn(places[j], dx[j]).astype(bf16)
        tail = jnp.zeros((16, D), f32)
        for e in range(2):
            column = grad_gates[e][64 * j : 64 * j + 64]
            value = jnp.sum(places[j][64 * e : 64 * e + 64].astype(f32) * column, 0, keepdims=True)
            tail = jnp.where(cell == 2 * me + e, jnp.concatenate([value] * 8, 1), tail)
        part[j, TOK : TOK + 16] = tail.astype(bf16)
    for copy in copies:
        copy.wait()


def expert_grad_body(*refs):
    x, g, act, gb = refs[0:4], refs[4:8], refs[8:12], refs[12:16]
    done, gu_out, down_out, xs, gs, acts, gbs, up_v, down_v, sems = refs[16:]
    done[...] = jnp.zeros_like(done)
    written = []
    copies = []
    for e in range(2):
        for i in range(4):
            here = pl.ds(256 * i, 256)
            for n, (ref, held) in enumerate(((x[i], xs), (gb[i], gbs), (act[i], acts), (g[i], gs))):
                copies.append(pltpu.make_async_copy(ref.at[e], held.at[e, here], sems.at[16 * e + 4 * i + n]))
    for copy in copies:
        copy.start()
    for e in range(2):
        for copy in copies[16 * e : 16 * e + 16]:
            copy.wait()
        for b in range(4):
            here = slice(256 * b, 256 * b + 256)
            up_v[e, here] = dot_tn(xs[e, :, here], gbs[e]).astype(bf16)
            written.append(pltpu.make_async_copy(up_v.at[e, here], gu_out.at[e, here], sems.at[32 + 6 * e + b]))
            written[-1].start()
        for b in range(2):
            here = slice(256 * b, 256 * b + 256)
            down_v[e, here] = dot_tn(acts[e, :, here], gs[e]).astype(bf16)
            written.append(pltpu.make_async_copy(down_v.at[e, here], down_out.at[e, here], sems.at[36 + 6 * e + b]))
            written[-1].start()
    for copy in written:
        copy.wait()


def expert_result_body(a0, a1, a2, a3, wd, code, done, out, rows_v, out_v, sems):
    at = Place()
    done[...] = jnp.zeros_like(done)
    slots = lax.broadcasted_iota(jnp.int32, (CAPACITY, TOK), 0).astype(f32)
    for i, act in enumerate((a0, a1, a2, a3)):
        for e in range(2):
            result = dot(act[e], wd[e]).astype(bf16)
            for j in range(4):
                rows_v[4 * i + j, 64 * e : 64 * e + 64] = result[64 * j : 64 * j + 64]
    written = []
    for r in range(16):
        codes = code[at.source(r // 4, r % 4)]
        place = [(row_of(codes, 2 * at.me + e) == slots).astype(f32) for e in range(2)]
        out_v[r] = dot_tn(jnp.concatenate(place, 0).astype(bf16), rows_v[r]).astype(bf16)
        written.append(pltpu.make_async_copy(out_v.at[r], out.at[at.source(r // 4, r % 4)], sems.at[r]))
        written[-1].start()
    for copy in written:
        copy.wait()


def norm_back_body(
    p0, p1, p2, p3, n2, middle, scale, gain, cot, code, router, wo, grad_mid, low_mid, datt, router_grad, second, wo_v, sem
):
    fetch = pltpu.make_async_copy(wo, wo_v, sem)
    fetch.start()
    total = added([p0[...], p1[...], p2[...], p3[...]])
    grad = total[:TOK]
    grad_gate = unpacked(total[TOK : TOK + 4])
    rows = n2[...]
    prob = softmax_chosen(dot_nt(router[...], rows), code[...])
    grad_chosen = prob * (grad_gate - jnp.sum(prob * grad_gate, 0, keepdims=True))
    grad_logits = grad_chosen.astype(bf16)
    router_grad[...] = dot(grad_logits, rows)
    grad = grad + dot_tn(grad_logits, router[...])
    mid = middle[...]
    r2 = scale[:, 0:1]
    g2 = grad * gain[...]
    second[...] = jnp.sum(grad * mid * r2, 0, keepdims=True)
    grad_middle = cot[...].astype(f32) + r2 * g2 - mid * r2 * r2 * r2 * jnp.mean(g2 * mid, -1, keepdims=True)
    grad_mid[...] = grad_middle
    low = grad_middle.astype(bf16)
    low_mid[...] = low
    fetch.wait()
    datt[...] = dot_nt(wo_v[...], low).astype(bf16).reshape(H, HD, TOK)


def touch_body(array, out):
    out[...] = jnp.zeros_like(out)


def finish_body(middle, result, out):
    out[...] = (middle[...] + result[...].astype(f32)).astype(bf16)


def sum4_body(*refs):
    for n in range(4):
        refs[n - 4][...] = added([ref[n] for ref in refs[:-4]]).astype(bf16)


def attend_back_body(datt, qkv_in, att_in, totals, cosine, sine, out, dq, dk, dv, dmix, qkv, att, sems):
    copies = [pltpu.make_async_copy(qkv_in, qkv, sems.at[0]), pltpu.make_async_copy(att_in, att, sems.at[1])]
    for copy in copies:
        copy.start()
    for s in range(16):
        dmix[:, 128 * s : 128 * s + 128] = datt[s]
    rows = lax.broadcasted_iota(jnp.int32, (256, 256), 0)
    cols = lax.broadcasted_iota(jnp.int32, (256, 256), 1)
    visible = rows <= cols
    dk[...] = jnp.zeros_like(dk)
    dv[...] = jnp.zeros_like(dv)
    for copy in copies:
        copy.wait()
    for i in range(8):
        here = slice(256 * i, 256 * i + 256)
        query = qkv[0:64, here]
        inverse = 1.0 / totals[:, here]
        grad_att = dmix[:, here].astype(f32)
        delta = jnp.sum(grad_att * att[:, here], 0, keepdims=True) * inverse
        grad_mix = (grad_att * inverse).astype(bf16)
        for at, diagonal in ((slice(0, 256 * i), False), (here, True)):
            if at.stop == 0:
                continue
            key = qkv[64:128, at]
            weights = jnp.exp(dot_tn(key, query) * score_scale)
            if diagonal:
                weights = jnp.where(visible, weights, 0.0)
            grad_weights = dot_tn(qkv[128:192, at], grad_mix)
            grad_scores = (weights * (grad_weights - delta)).astype(bf16)
            more = dot(key, grad_scores)
            dq[:, here] = more if not diagonal or i == 0 else dq[:, here] + more
            dk[:, at] += dot_nt(query, grad_scores)
            dv[:, at] += dot_nt(grad_mix, weights.astype(bf16))

    def unrotated(value):
        value = value * score_scale
        a, b = value[: HD // 2], value[HD // 2 :]
        cos, sin = cosine[...], sine[...]
        return jnp.concatenate([a * cos + b * sin, b * cos - a * sin], 0).astype(bf16)

    low_q, low_k, low_v = unrotated(dq[...]), unrotated(dk[...]), dv[...].astype(bf16)
    for s in range(16):
        out[s, 0:64] = low_q[:, 128 * s : 128 * s + 128]
        out[s, 64:128] = low_k[:, 128 * s : 128 * s + 128]
        out[s, 128:192] = low_v[:, 128 * s : 128 * s + 128]


def weight_grad_body(own, recv, n1, att, low, router_grad, second, *refs):
    more = refs[: 4 * own]
    outs, rows_v, one_v, low_v = refs[4 * own : -3], refs[-3], refs[-2], refs[-1]
    at = Place()
    core = at.core if own else 1 - at.core
    columns = pl.ds(pl.multiple_of(core * 512, 512), 512)
    got = recv[...]
    query = got[:, 0:64]
    pairs = got[:, 64:192].astype(f32).reshape(KV, 2, 128, TOK)
    pairs = (pairs[:, 0] + pairs[:, 1]).astype(bf16)
    rows = jnp.concatenate([query.reshape(KV, 2, 64, TOK), pairs.reshape(KV, 2, 64, TOK)], 2)
    rows_v[...] = rows.reshape(H, 128, TOK)
    one_v[...] = n1[:, columns]
    low_v[...] = low[:, columns]
    index = lax.broadcasted_iota(jnp.int32, (16, 512), 0)
    for i in range(4):
        for j in range(4):
            h = at.source(i, j, core)
            tail = jnp.where(index == 0, row_of(router_grad[:, columns], 2 * h), 0.0)
            tail = jnp.where(index == 1, row_of(router_grad[:, columns], 2 * h + 1), tail)
            tail = jnp.where((index == 2) & (h == 0), second[:, columns], tail)
            part = jnp.concatenate([dot(rows_v[h], one_v[...]), dot(att[h], low_v[...]), tail], 0)
            if own:
                part = part + more[i][j].astype(f32)
            outs[i][j] = part.astype(bf16)


def half_sum_body(w0, w1, w2, w3, out):
    out[...] = added([w0[...], w1[...], w2[...], w3[...]]).astype(bf16)


def hidden_grad_body(recv, hid, gain, grad_mid, wq_in, wk_in, wv_in, out, wq, wk, wv, sems):
    copies = []
    for n, (source, held) in enumerate(((wk_in, wk), (wv_in, wv), (wq_in, wq))):
        for k in range(2):
            here = pl.ds(512 * k, 512)
            copies.append(pltpu.make_async_copy(source.at[here], held.at[here], sems.at[2 * n + k]))
    for copy in copies:
        copy.start()
    got = recv[...]
    grad_q = got[:, 0:64].reshape(D, TOK).T
    pairs = got[:, 64:192].astype(f32).reshape(KV, 2, 128, TOK)
    pairs = (pairs[:, 0] + pairs[:, 1]).astype(bf16)
    grad_k = pairs[:, 0:64].reshape(KV * HD, TOK).T
    grad_v = pairs[:, 64:128].reshape(KV * HD, TOK).T
    for copy in copies:
        copy.wait()
    grad = dot_nt(grad_k, wk[...]) + dot_nt(grad_v, wv[...]) + dot_nt(grad_q, wq[...])
    hidden = hid[...].astype(f32)
    r1 = lax.rsqrt(jnp.mean(hidden * hidden, -1, keepdims=True) + epsilon)
    g1 = grad * gain[...]
    back = r1 * g1 - hidden * r1 * r1 * r1 * jnp.mean(g1 * hidden, -1, keepdims=True)
    out[...] = (grad_mid[...] + back).astype(bf16)


def z_sum_body(p0, p1, p2, p3, out):
    at = Place()
    total = added([p0[...], p1[...], p2[...], p3[...]])
    for b in range(4):
        part = total[:, 128 * b : 128 * b + 128]
        k = lax.rem(b - at.z + 4, 4)
        out[k, 0:128] = part[0:128].T.astype(bf16)
        out[k, 128:208] = part[128:208].astype(bf16)


def assemble_body(half, table, *refs):
    parts = refs[0:4]
    wq, wk, wv, gain = refs[4:8]
    q_out, k_out, v_out, o_out, r_out, e_out, tiles, tails = refs[9 + 6 * half :]
    k = pl.program_id(0)
    for i in range(4):
        for j in range(4):
            h = table[8 + 16 * half + 4 * i + j]
            block = parts[i][j, k]
            tiles[h] = block[0:128].astype(f32)
            o_out[pl.ds(pl.multiple_of(h * 64, 64), 64)] = block[128:192].astype(f32)
            tails[h] = block[192:208].astype(f32)
    for p in range(8):
        q_out[:, 128 * p : 128 * p + 128] = jnp.concatenate([tiles[2 * p][:, :64], tiles[2 * p + 1][:, :64]], 1)
    for m in range(4):
        here = slice(128 * m, 128 * m + 128)
        k_out[:, here] = jnp.concatenate([tiles[4 * m][:, 64:], tiles[4 * m + 2][:, 64:]], 1)
        v_out[:, here] = jnp.concatenate([tiles[4 * m + 1][:, 64:], tiles[4 * m + 3][:, 64:]], 1)
    for h in range(16):
        r_out[2 * h : 2 * h + 2] = tails[h][0:2]
    total = jnp.sum(q_out[...] * wq[...].astype(f32), 1, keepdims=True)
    total = total + jnp.sum(k_out[...] * wk[...].astype(f32), 1, keepdims=True)
    total = total + jnp.sum(v_out[...] * wv[...].astype(f32), 1, keepdims=True)
    first = jnp.broadcast_to(total / gain[...], (128, 128)).T
    index = lax.broadcasted_iota(jnp.int32, (8, 128), 0)
    e_out[...] = jnp.where(index == 0, first[0:8], jnp.broadcast_to(tails[0][2:3], (8, 128)))


def assemble(half, table, parts, wq, wk, wv, gain, after, begun=()):
    def at(g, t):
        return t[4 * half + g]

    rows = pl.BlockSpec((128, 1024), lambda g, t: (at(g, t), 0))
    half_rows = pl.BlockSpec((128, 512), lambda g, t: (at(g, t), 0))
    column = pl.BlockSpec((128, 1), lambda g, t: (at(g, t), 0))
    grid_spec = pltpu.PrefetchScalarGridSpec(
        num_scalar_prefetch=1,
        grid=(4,),
        in_specs=[VM] * 4 + [rows, half_rows, half_rows, column, ANY] + [ANY] * len(begun),
        out_specs=[
            rows,
            half_rows,
            half_rows,
            pl.BlockSpec((1024, 128), lambda g, t: (0, at(g, t))),
            pl.BlockSpec((32, 128), lambda g, t: (0, at(g, t))),
            pl.BlockSpec((8, 128), lambda g, t: (0, at(g, t))),
        ],
        scratch_shapes=[pltpu.VMEM((16, 128, 128), f32), pltpu.VMEM((16, 16, 128), f32)],
    )
    return pl.pallas_call(
        lambda *refs: assemble_body(half, *refs),
        grid_spec=grid_spec,
        out_shape=[
            shape((1024, 1024), f32),
            shape((1024, 512), f32),
            shape((1024, 512), f32),
            shape((1024, 1024), f32),
            shape((32, 1024), f32),
            shape((8, 1024), f32),
        ],
        input_output_aliases={10 + n: n for n in range(len(begun))},
        compiler_params=pltpu.CompilerParams(vmem_limit_bytes=24 * 1024 * 1024),
        cost_estimate=pl.CostEstimate(flops=30 * 10**9, bytes_accessed=1024, transcendentals=0),
        name="assemble",
    )(table, *parts, wq, wk, wv, gain, after, *begun)


def widen_body(up, down, token, up_out, down_out, done):
    done[...] = jnp.zeros_like(done)
    up_out[...] = up[...].astype(f32)
    down_out[...] = down[...].astype(f32)


def widen(up, down, after):
    def spec(rows):
        return pl.BlockSpec((1, rows, D), lambda e, n: (e, n, 0))

    return pl.pallas_call(
        widen_body,
        grid=(2, 4),
        in_specs=[spec(256), spec(128), ANY],
        out_specs=[spec(256), spec(128), pl.BlockSpec((8, 128), lambda e, n: (0, 0))],
        out_shape=[outside((2, D, 2 * FF), f32), outside((2, FF, D), f32), shape((8, 128), f32)],
        compiler_params=pltpu.CompilerParams(vmem_limit_bytes=16 * 1024 * 1024),
        name="widen",
    )(up, down, after)


def on_device(
    hidden_in,
    routes,
    first_gain,
    query_weight,
    key_weight,
    value_weight,
    output_weight,
    second_gain,
    router_weight,
    gateup_weight,
    down_weight,
    cotangent,
):
    at = Place()
    z, core = at.z, at.core
    order = Order()
    steps = jnp.arange(4)
    gain_one = first_gain.astype(f32)[None]
    gain_two = second_gain.astype(f32)[None]
    router_t = router_weight.T
    inverse = 10000.0 ** (-np.arange(0, HD, 2).astype(np.float32) / HD)
    angles = inverse[:, None] * np.arange(SEQ).astype(np.float32)[None, :]
    cos_all, sin_all = np.cos(angles).astype(np.float32), np.sin(angles).astype(np.float32)

    def by_source(table):
        return held_outside(jnp.asarray(table.reshape(HD // 2, 16, TOK).transpose(1, 0, 2)))

    cot_all = held_outside(lax.all_gather(cotangent, "expert", axis=0, tiled=False))
    to_heads, normed_one, codes = order.call(
        project_body,
        [shape((16, 224, TOK)), shape((TOK, D)), shape((EXPERTS, TOK), f32)],
        [
            hidden_in,
            gain_one,
            routes.T,
            held_outside(query_weight),
            held_outside(key_weight),
            held_outside(value_weight),
            by_source(cos_all),
            by_source(sin_all),
        ],
        specs=[VM, VM, VM, HBM, HBM, HBM, HBM, HBM],
        scratch=[
            pltpu.VMEM((D, D), bf16),
            pltpu.VMEM((D, 512), bf16),
            pltpu.VMEM((D, 512), bf16),
            pltpu.VMEM((HD // 2, TOK), f32),
            pltpu.VMEM((HD // 2, TOK), f32),
            pltpu.SemaphoreType.DMA((14,)),
        ],
        name="project",
    )
    at_heads = lax.all_to_all(to_heads, "expert", split_axis=0, concat_axis=0, tiled=True)
    att_low, att, totals, qkv, code_all = order.call(
        attend_body,
        [
            shape((16, HD, TOK)),
            outside((HD, SEQ), f32),
            shape((1, SEQ), f32),
            outside((192, SEQ)),
            shape((16, EXPERTS, TOK), f32),
        ],
        [at_heads],
        out_specs=[VM, HBM, VM, HBM, VM],
        scratch=[pltpu.VMEM((HD, SEQ), f32), pltpu.VMEM((192, SEQ), bf16), pltpu.SemaphoreType.DMA((9,))],
        name="attend",
    )
    att_t = lax.all_to_all(att_low, "expert", split_axis=0, concat_axis=0, tiled=True)
    middle, scale_two, normed_two = order.call(
        middle_body,
        [shape((TOK, D), f32), shape((TOK, 128), f32), shape((TOK, D))],
        [att_t, hidden_in, output_weight, gain_two],
        name="middle",
    )
    row = order.stack(gather_axis(normed_two, along_u), after=(cot_all,))
    right, left = send(row, along_v(-1)), send(row, along_v(1))
    chunks = {0: [row], 1: [right], 3: [left]}
    worked = {}
    held = [held_outside(gateup_weight), held_outside(down_weight)]
    for i in (0, 1, 3, 2):
        if i == 1:
            halves = order.call(split_body, [shape((2, TOK, D))] * 2, [right, left], name="split")
            chunks[2] = [send(halves[0], along_v(-1)), send(halves[1], along_v(1))]
        worked[i] = order.call(
            lambda *refs, i=i: expert_body(i, *refs),
            [
                shape((4, TOK + 16, D)),
                outside((2, 256, D)),
                outside((2, 256, D)),
                outside((2, 256, FF)),
                outside((2, 256, 2 * FF)),
            ]
            + ([shape((2, D, 2 * FF)), shape((2, FF, D))] if i == 0 else []),
            [*chunks[i], cot_all, code_all, router_t, *held],
            specs=[VM] * len(chunks[i]) + [HBM, VM, VM] + [HBM if i == 0 else VM] * 2,
            out_specs=[VM, HBM, HBM, HBM, HBM] + [VM] * (2 if i == 0 else 0),
            scratch=[
                pltpu.VMEM((4, TOK, D), bf16),
                pltpu.VMEM((2, 256, D), bf16),
                pltpu.VMEM((2, 256, D), bf16),
                pltpu.VMEM((2, 256, FF), bf16),
                pltpu.VMEM((2, 256, 2 * FF), bf16),
                pltpu.VMEM((4, TOK, D), bf16),
                pltpu.SemaphoreType.DMA((14,)),
            ],
            us=6,
            limit=24,
            name="experts",
        )
        if i == 0:
            held = worked[i][5:]
    parts = sum_axis([worked[i][0] for i in range(4)], along_v)
    saved = [[held_outside(worked[i][k]) for i in range(4)] for k in range(1, 5)]
    done, gateup_grad, down_grad = order.call(
        expert_grad_body,
        [shape((8, 128), f32), outside((2, D, 2 * FF)), outside((2, FF, D))],
        [*saved[0], *saved[1], *saved[2], *saved[3]],
        specs=[HBM] * 16,
        scratch=[
            pltpu.VMEM((2, 1024, D), bf16),
            pltpu.VMEM((2, 1024, D), bf16),
            pltpu.VMEM((2, 1024, FF), bf16),
            pltpu.VMEM((2, 1024, 2 * FF), bf16),
            pltpu.VMEM((2, D, 2 * FF), bf16),
            pltpu.VMEM((2, FF, D), bf16),
            pltpu.SemaphoreType.DMA((44,)),
        ],
        out_specs=[VM, HBM, HBM],
        limit=40,
        us=11,
        name="expert_grads",
    )
    gateup_grad, down_grad = lax.psum((gateup_grad, down_grad), "dp")
    grad_rows = sum_axis(order.sum4(parts, "sum_grads"), along_u)
    grad_middle, grad_middle_low, to_back, router_grad, second_part = order.call(
        norm_back_body,
        [
            outside((TOK, D), f32),
            shape((TOK, D)),
            shape((H, HD, TOK)),
            shape((EXPERTS, D), f32),
            shape((1, D), f32),
        ],
        [
            *grad_rows,
            normed_two,
            middle,
            scale_two,
            gain_two,
            cotangent,
            codes,
            router_t,
            held_outside(output_weight),
        ],
        specs=[VM] * 11 + [HBM],
        out_specs=[pl.BlockSpec(), VM, VM, VM, VM],
        scratch=[pltpu.VMEM((D, D), bf16), pltpu.SemaphoreType.DMA],
        name="norm_back",
    )
    at_back = lax.all_to_all(to_back, "expert", split_axis=0, concat_axis=0, tiled=True)
    (to_tokens,) = order.call(
        attend_back_body,
        [shape((16, 192, TOK))],
        [at_back, held_outside(qkv), held_outside(att), totals, jnp.asarray(cos_all), jnp.asarray(sin_all)],
        specs=[VM, HBM, HBM, VM, VM, VM],
        limit=24,
        scratch=[
            pltpu.VMEM((HD, SEQ), f32),
            pltpu.VMEM((HD, SEQ), f32),
            pltpu.VMEM((HD, SEQ), f32),
            pltpu.VMEM((HD, SEQ), bf16),
            pltpu.VMEM((192, SEQ), bf16),
            pltpu.VMEM((HD, SEQ), f32),
            pltpu.SemaphoreType.DMA((2,)),
        ],
        name="attend_back",
    )
    at_tokens = lax.all_to_all(to_tokens, "expert", split_axis=0, concat_axis=0, tiled=True)
    sources = [at_tokens, normed_one, att_t, grad_middle_low, router_grad, second_part]
    held_rows = [pltpu.VMEM((H, 128, TOK), bf16), pltpu.VMEM((TOK, 512), bf16), pltpu.VMEM((TOK, 512), bf16)]
    far = order.call(
        lambda *refs: weight_grad_body(0, *refs),
        [shape((4, 208, 512))] * 4,
        sources,
        scratch=held_rows,
        limit=24,
        name="weight_grad",
    )
    far = [send(part, other_core()) for part in far]
    (hidden_grad,) = order.call(
        hidden_grad_body,
        [shape((TOK, D))],
        [
            at_tokens,
            hidden_in,
            gain_one,
            grad_middle,
            held_outside(query_weight),
            held_outside(key_weight),
            held_outside(value_weight),
        ],
        specs=[VM] * 4 + [HBM] * 3,
        scratch=[
            pltpu.VMEM((D, D), bf16),
            pltpu.VMEM((D, 512), bf16),
            pltpu.VMEM((D, 512), bf16),
            pltpu.SemaphoreType.DMA((6,)),
        ],
        name="hidden_grad",
    )
    weight_parts = order.call(
        lambda *refs: weight_grad_body(1, *refs),
        [shape((4, 208, 512))] * 4,
        [*sources, *far],
        scratch=held_rows,
        limit=24,
        name="weight_grad",
    )
    weight_parts = sum_axis(weight_parts, along_v)
    done, results = order.call(
        expert_result_body,
        [shape((8, 128), f32), outside((16, TOK, D))],
        [*[worked[i][3] for i in range(4)], down_weight, code_all],
        out_specs=[VM, HBM],
        scratch=[
            pltpu.VMEM((16, TOK, D), bf16),
            pltpu.VMEM((16, TOK, D), bf16),
            pltpu.SemaphoreType.DMA((16,)),
        ],
        limit=24,
        us=5,
        name="expert_results",
    )
    result = lax.psum_scatter(results, "expert", scatter_dimension=0, tiled=False)
    weight_rows = sum_axis(order.sum4(weight_parts, "sum_weights"), along_u)
    order.call(touch_body, [shape((8, 128), f32)], [held_outside(gateup_grad)], specs=[HBM], name="touch")
    (half,) = order.call(half_sum_body, [shape((208, 512))], weight_rows, name="half")
    (block,) = order.call(z_sum_body, [shape((4, 208, 128))], gather_axis(half, along_z), name="z_sum")
    block = gather_axis(block, along_u)
    block = gather_axis(order.stack(block), along_v)
    gateup_grad, down_grad, done = widen(held_outside(gateup_grad), held_outside(down_grad), order.last[0])
    order.last = (done,)
    others = [send(part, other_core()) for part in block]
    i, j = steps[:, None], steps[None, :]
    own_blocks = jnp.concatenate([core * 4 + (z + steps) % 4, (1 - core) * 4 + (z + steps) % 4])
    table = jnp.concatenate([own_blocks, at.source(i, j).reshape(-1), at.source(i, j, 1 - core).reshape(-1)])
    table = table.astype(jnp.int32)
    weights = (query_weight, key_weight, value_weight, first_gain.astype(f32)[:, None])
    begun = assemble(0, table, block, *weights, done)
    query_grad, key_grad, value_grad, output_grad, router_out, ends = assemble(
        1, table, others, *weights, done, begun
    )
    order.last = (ends,)
    (layer_out,) = order.call(finish_body, [shape((TOK, D))], [middle, result], name="finish")
    return (
        layer_out,
        hidden_grad,
        gateup_grad,
        down_grad,
        query_grad,
        key_grad,
        value_grad,
        output_grad,
        router_out.T,
        ends[0],
        ends[1],
    )


def solution(mesh):
    rows = P(("dp", "expert"), None)
    experts = P("expert", None, None)
    return jax.shard_map(
        on_device,
        mesh=mesh,
        in_specs=(rows, rows, P(), P(), P(), P(), P(), P(), P(), experts, experts, rows),
        out_specs=(rows, rows, experts, experts, P(), P(), P(), P(), P(), P(), P()),
        check_vma=False,
    )
```

```python
import jax
import jax.numpy as jnp
import numpy as np
from jax import lax
from jax.experimental import pallas as pl
from jax.experimental.pallas import tpu as pltpu
from jax.sharding import PartitionSpec as P

D = 1024
H = 16
KV = 8
HD = 64
FF = 512
TOP = 8
EXPERTS = 32
CAPACITY = 64
TOK = 128
SEQ = 2048

epsilon = 1e-06
score_scale = 0.015625

bf16 = jnp.bfloat16
f32 = jnp.float32
AXES = ("dp", "expert")

NT = (((1,), (1,)), ((), ()))
TN = (((0,), (0,)), ((), ()))

VM = pl.BlockSpec(memory_space=pltpu.VMEM)
HBM = pl.BlockSpec(memory_space=pltpu.HBM)
ANY = pl.BlockSpec(memory_space=pl.ANY)


def dot(a, b):
    return jnp.dot(a, b, preferred_element_type=f32)


def dot_nt(a, b):
    return lax.dot_general(a, b, NT, preferred_element_type=f32)


def dot_tn(a, b):
    return lax.dot_general(a, b, TN, preferred_element_type=f32)


def moves(step):
    pairs = []
    for z in range(4):
        for c in range(2):
            for x in range(4):
                for y in range(4):
                    z2, c2, x2, y2 = step(z, c, x, y)
                    target = (((z2 % 4) * 2 + c2 % 2) * 4 + x2 % 4) * 4 + y2 % 4
                    pairs.append((((z * 2 + c) * 4 + x) * 4 + y, target))
    return pairs


def along_u(n):
    return moves(lambda z, c, x, y: (z, c, x, y + n) if c == 0 else (z, c, x + n, y))


def along_v(n):
    return moves(lambda z, c, x, y: (z, c, x + n, y) if c == 0 else (z, c, x, y + n))


def along_z(n):
    return moves(lambda z, c, x, y: (z + n, c, x, y))


def other_core():
    return moves(lambda z, c, x, y: (z, c + 1, x, y))


def pair_head():
    return moves(lambda z, c, x, y: (z, c, x, y ^ 1))


def other_pair():
    return moves(lambda z, c, x, y: (z, c + 1, x, y ^ 1))


def send(array, pairs):
    return lax.ppermute(array, AXES, pairs)


def gather_axis(array, along):
    return [array] + [send(array, along(-n)) for n in (1, 2, 3)]


def sum_axis(parts, along):
    return [parts[0]] + [send(parts[n], along(n)) for n in (1, 2, 3)]


def added(parts):
    total = parts[0].astype(f32)
    for part in parts[1:]:
        total = total + part.astype(f32)
    return total


class Place:
    def __init__(self):
        dp, self.me = lax.axis_index("dp"), lax.axis_index("expert")
        self.z, self.core = lax.div(dp, 2), lax.rem(dp, 2)
        self.x, self.y = lax.div(self.me, 4), lax.rem(self.me, 4)

    def source(self, i, j, core=None):
        core = self.core if core is None else core
        zero = lax.rem(self.x + i, 4) * 4 + lax.rem(self.y + j, 4)
        one = lax.rem(self.x + j, 4) * 4 + lax.rem(self.y + i, 4)
        return jnp.where(core == 0, zero, one)


class Order:
    def __init__(self):
        self.last = ()

    def call(self, body, outs, args, scratch=(), specs=None, out_specs=None, limit=16, us=1, name=None, after=()):
        before = self.last + tuple(after)
        count, skip = len(args), len(before)

        def run(*refs):
            body(*refs[:count], *refs[count + skip :])

        results = pl.pallas_call(
            run,
            out_shape=outs,
            in_specs=(list(specs) if specs is not None else [VM] * count) + [ANY] * skip,
            out_specs=out_specs if out_specs is not None else [VM] * len(outs),
            scratch_shapes=list(scratch),
            compiler_params=pltpu.CompilerParams(vmem_limit_bytes=limit * 1024 * 1024),
            cost_estimate=pl.CostEstimate(flops=us * 10**9, bytes_accessed=1024, transcendentals=0),
            name=name,
        )(*args, *before)
        self.last = (results[0],)
        return results

    def stack(self, parts, after=()):
        kind = shape((4, *parts[0].shape), parts[0].dtype)
        return self.call(stack_body, [kind], parts, after=after, name="stack")[0]

    def sum4(self, parts, name):
        return self.call(sum4_body, [shape(parts[0].shape[1:])] * 4, parts, name=name)


def shape(dims, kind=bf16):
    return jax.ShapeDtypeStruct(dims, kind)


def outside(dims, kind=bf16):
    return pltpu.HBM(dims, kind)


def held_outside(array):
    return pltpu.with_memory_space_constraint(array, pltpu.HBM)


def stack_body(*refs):
    for n in range(4):
        refs[4][n] = refs[n][...]


def split_body(right, left, first, last):
    first[...] = right[0:2]
    last[...] = left[2:4]


def rows_at(refs, j):
    return refs[j * len(refs) // 4].at[j % (4 // len(refs))]


def unpacked(rows):
    return jnp.concatenate([rows[:, TOK * c : TOK * c + TOK] for c in range(8)], 0)


def project_body(hid, gain, routes, wq, wk, wv, cosine, sine, out, normed, codes, wq_v, wk_v, wv_v, cos_v, sin_v, sems):
    me = lax.axis_index("expert")
    copies = []
    for weight, held in ((wk, wk_v), (wv, wv_v), (wq, wq_v)):
        for n in range(4):
            here = pl.ds(256 * n, 256)
            copies.append(pltpu.make_async_copy(weight.at[here], held.at[here], sems.at[len(copies)]))
    copies.append(pltpu.make_async_copy(cosine.at[me], cos_v, sems.at[12]))
    copies.append(pltpu.make_async_copy(sine.at[me], sin_v, sems.at[13]))
    for copy in copies:
        copy.start()
    hidden = hid[...].astype(f32)
    r1 = lax.rsqrt(jnp.mean(hidden * hidden, -1, keepdims=True) + epsilon)
    n1 = (hidden * r1 * gain[...]).astype(bf16)
    normed[...] = n1
    index = lax.broadcasted_iota(jnp.int32, (EXPERTS, TOK), 0)
    chosen = index < 0
    for j in range(TOP):
        chosen = chosen | (routes[j : j + 1] == index)
    rows = lax.broadcasted_iota(jnp.int32, (TOK, TOK), 0)
    cols = lax.broadcasted_iota(jnp.int32, (TOK, TOK), 1)
    rank = dot(chosen.astype(f32).astype(bf16), (rows < cols).astype(f32).astype(bf16))
    code = jnp.where(chosen & (rank < CAPACITY), rank, jnp.where(chosen, -1.0, -2.0))
    codes[...] = code
    for copy in copies[12:] + copies[:4]:
        copy.wait()
    cos = cos_v[...][None]
    sin = sin_v[...][None]

    def rotated(value, heads):
        value = value.T.reshape(heads, HD, TOK)
        a, b = value[:, : HD // 2], value[:, HD // 2 :]
        return jnp.concatenate([a * cos - b * sin, b * cos + a * sin], 1).astype(bf16)

    key = rotated(dot(n1, wk_v[...]), KV)
    for copy in copies[4:8]:
        copy.wait()
    value = dot(n1, wv_v[...]).T.reshape(KV, HD, TOK).astype(bf16)
    for copy in copies[8:12]:
        copy.wait()
    query = rotated(dot(n1, wq_v[...]), H)
    for h in range(H):
        out[h, 0:64] = query[h]
        out[h, 64:128] = key[h // 2]
        out[h, 128:192] = value[h // 2]
        out[h, 192:224] = code.astype(bf16)


def attend_body(recv, att_send, att_out, totals, qkv_out, codes, att, qkv, sems):
    for s in range(16):
        qkv[:, 128 * s : 128 * s + 128] = recv[s, 0:192]
        codes[s] = recv[s, 192:224].astype(f32)
    copies = [pltpu.make_async_copy(qkv, qkv_out, sems.at[8])]
    copies[0].start()
    rows = lax.broadcasted_iota(jnp.int32, (256, 256), 0)
    cols = lax.broadcasted_iota(jnp.int32, (256, 256), 1)
    visible = rows <= cols
    for i in range(8):
        here = slice(256 * i, 256 * i + 256)
        query = qkv[0:64, here]
        weights = jnp.exp(dot_tn(qkv[64:128, here], query) * score_scale)
        weights = jnp.where(visible, weights, 0.0)
        total = jnp.sum(weights, 0, keepdims=True)
        mixture = dot(qkv[128:192, here], weights.astype(bf16))
        if i:
            before = slice(0, 256 * i)
            weights = jnp.exp(dot_tn(qkv[64:128, before], query) * score_scale)
            total = total + jnp.sum(weights, 0, keepdims=True)
            mixture = mixture + dot(qkv[128:192, before], weights.astype(bf16))
        mixed = mixture / total
        att[:, here] = mixed
        totals[:, here] = total
        att_send[2 * i] = mixed[:, :128].astype(bf16)
        att_send[2 * i + 1] = mixed[:, 128:].astype(bf16)
        copies.append(pltpu.make_async_copy(att.at[:, pl.ds(256 * i, 256)], att_out.at[:, pl.ds(256 * i, 256)], sems.at[i]))
        copies[-1].start()
    for copy in copies:
        copy.wait()


def middle_body(att_t, hid, wo, gain, middle, scale, normed):
    attended = att_t[...].reshape(D, TOK).T
    mid = hid[...].astype(f32) + dot(attended, wo[...])
    r2 = lax.rsqrt(jnp.mean(mid * mid, -1, keepdims=True) + epsilon)
    middle[...] = mid
    scale[...] = jnp.broadcast_to(r2, scale.shape)
    normed[...] = (mid * r2 * gain[...]).astype(bf16)


def softmax_chosen(logits, codes):
    chosen = codes > -1.5
    top = jnp.max(jnp.where(chosen, logits, -1e30), 0, keepdims=True)
    powers = jnp.where(chosen, jnp.exp(logits - top), 0.0)
    return powers / jnp.sum(powers, 0, keepdims=True)


def row_of(table, index):
    rows = lax.broadcasted_iota(jnp.int32, table.shape, 0)
    return jnp.sum(jnp.where(rows == index, table, 0.0), 0, keepdims=True)


def expert_body(i, *refs):
    n2, (cot, code, router, *refs) = refs[: 1 + (i == 2)], refs[1 + (i == 2) :]
    if i == 0:
        wgu_in, wd_in, part, x_out, g_out, act_out, gb_out, wgu, wd = refs[:9]
    else:
        wgu, wd, part, x_out, g_out, act_out, gb_out = refs[:7]
    cot_v, x, g, act_v, gb, dx, sems = refs[-7:]
    at = Place()
    me = at.me
    fetched = [pltpu.make_async_copy(cot.at[at.source(i, j)], cot_v.at[j], sems.at[6 + j]) for j in range(4)]
    for copy in fetched:
        copy.start()
    weights = []
    if i == 0:
        for e in range(2):
            weights.append(pltpu.make_async_copy(wgu_in.at[e], wgu.at[e], sems.at[10 + 2 * e]))
            weights.append(pltpu.make_async_copy(wd_in.at[e], wd.at[e], sems.at[11 + 2 * e]))
        for copy in weights:
            copy.start()
    slots = lax.broadcasted_iota(jnp.int32, (CAPACITY, TOK), 0).astype(f32)
    places = []
    gates = []
    for j in range(4):
        rows = rows_at(n2, j)[...]
        logits = dot_nt(router[...], rows)
        fetched[j].wait()
        codes = code[at.source(i, j)]
        prob = softmax_chosen(logits, codes)
        where = [row_of(codes, 2 * me + e) == slots for e in range(2)]
        places.append(jnp.concatenate([w.astype(f32) for w in where], 0).astype(bf16))
        gates.append([jnp.sum(jnp.where(where[e], row_of(prob, 2 * me + e), 0.0), 1, keepdims=True) for e in range(2)])
        here = slice(64 * j, 64 * j + 64)
        picked = dot(places[j], rows).astype(bf16)
        x[0, here] = picked[:64]
        x[1, here] = picked[64:]
        picked = dot(places[j], cot_v[j]).astype(bf16)
        g[0, here] = picked[:64]
        g[1, here] = picked[64:]
    copies = [pltpu.make_async_copy(x, x_out, sems.at[0]), pltpu.make_async_copy(g, g_out, sems.at[1])]
    for copy in copies:
        copy.start()
    grad_gates = []
    for e in range(2):
        for copy in weights[2 * e : 2 * e + 2]:
            copy.wait()
        both = dot(x[e], wgu[e])
        active = dot_nt(g[e], wd[e])
        gate, up = both[:, :FF], both[:, FF:]
        s = 1.0 / (1.0 + jnp.exp(-gate))
        silu = gate * s
        act = silu * up
        weight = jnp.concatenate([gates[j][e] for j in range(4)], 0)
        act_v[e] = (act * weight).astype(bf16)
        grad_gates.append(jnp.sum(act * active, 1, keepdims=True))
        grad_active = active * weight
        gb[e, :, :FF] = (grad_active * up * s * (1.0 + gate * (1.0 - s))).astype(bf16)
        gb[e, :, FF:] = (grad_active * silu).astype(bf16)
        for n, (held, out) in enumerate(((act_v, act_out), (gb, gb_out))):
            copies.append(pltpu.make_async_copy(held.at[e], out.at[e], sems.at[2 + 2 * e + n]))
            copies[-1].start()
        grad_x = dot_nt(gb[e], wgu[e]).astype(bf16)
        for j in range(4):
            dx[j, 64 * e : 64 * e + 64] = grad_x[64 * j : 64 * j + 64]
    lane = lax.broadcasted_iota(jnp.int32, (16, D), 1) // TOK
    row = lax.broadcasted_iota(jnp.int32, (16, D), 0)
    cell = jnp.where(row < 4, lane * 4 + row, -1)
    for j in range(4):
        part[j, 0:TOK] = dot_tn(places[j], dx[j]).astype(bf16)
        tail = jnp.zeros((16, D), f32)
        for e in range(2):
            column = grad_gates[e][64 * j : 64 * j + 64]
            value = jnp.sum(places[j][64 * e : 64 * e + 64].astype(f32) * column, 0, keepdims=True)
            tail = jnp.where(cell == 2 * me + e, jnp.concatenate([value] * 8, 1), tail)
        part[j, TOK : TOK + 16] = tail.astype(bf16)
    for copy in copies:
        copy.wait()


def expert_grad_body(*refs):
    x, g, act, gb = refs[0:4], refs[4:8], refs[8:12], refs[12:16]
    done, gu_out, down_out, xs, gs, acts, gbs, up_v, down_v, sems = refs[16:]
    done[...] = jnp.zeros_like(done)
    written = []
    copies = []
    for e in range(2):
        for i in range(4):
            here = pl.ds(256 * i, 256)
            for n, (ref, held) in enumerate(((x[i], xs), (gb[i], gbs), (act[i], acts), (g[i], gs))):
                copies.append(pltpu.make_async_copy(ref.at[e], held.at[e, here], sems.at[16 * e + 4 * i + n]))
    for copy in copies:
        copy.start()
    for e in range(2):
        for copy in copies[16 * e : 16 * e + 16]:
            copy.wait()
        for b in range(4):
            here = slice(256 * b, 256 * b + 256)
            up_v[e, here] = dot_tn(xs[e, :, here], gbs[e]).astype(bf16)
            written.append(pltpu.make_async_copy(up_v.at[e, here], gu_out.at[e, here], sems.at[32 + 6 * e + b]))
            written[-1].start()
        for b in range(2):
            here = slice(256 * b, 256 * b + 256)
            down_v[e, here] = dot_tn(acts[e, :, here], gs[e]).astype(bf16)
            written.append(pltpu.make_async_copy(down_v.at[e, here], down_out.at[e, here], sems.at[36 + 6 * e + b]))
            written[-1].start()
    for copy in written:
        copy.wait()


def expert_result_body(a0, a1, a2, a3, wd, code, done, out, rows_v, out_v, sems):
    at = Place()
    done[...] = jnp.zeros_like(done)
    slots = lax.broadcasted_iota(jnp.int32, (CAPACITY, TOK), 0).astype(f32)
    for i, act in enumerate((a0, a1, a2, a3)):
        for e in range(2):
            result = dot(act[e], wd[e]).astype(bf16)
            for j in range(4):
                rows_v[4 * i + j, 64 * e : 64 * e + 64] = result[64 * j : 64 * j + 64]
    written = []
    for r in range(16):
        codes = code[at.source(r // 4, r % 4)]
        place = [(row_of(codes, 2 * at.me + e) == slots).astype(f32) for e in range(2)]
        out_v[r] = dot_tn(jnp.concatenate(place, 0).astype(bf16), rows_v[r]).astype(bf16)
        written.append(pltpu.make_async_copy(out_v.at[r], out.at[at.source(r // 4, r % 4)], sems.at[r]))
        written[-1].start()
    for copy in written:
        copy.wait()


def norm_back_body(
    p0, p1, p2, p3, n2, middle, scale, gain, cot, code, router, wo, grad_mid, low_mid, datt, router_grad, second, wo_v, sem
):
    fetch = pltpu.make_async_copy(wo, wo_v, sem)
    fetch.start()
    total = added([p0[...], p1[...], p2[...], p3[...]])
    grad = total[:TOK]
    grad_gate = unpacked(total[TOK : TOK + 4])
    rows = n2[...]
    prob = softmax_chosen(dot_nt(router[...], rows), code[...])
    grad_chosen = prob * (grad_gate - jnp.sum(prob * grad_gate, 0, keepdims=True))
    grad_logits = grad_chosen.astype(bf16)
    router_grad[...] = dot(grad_logits, rows)
    grad = grad + dot_tn(grad_logits, router[...])
    mid = middle[...]
    r2 = scale[:, 0:1]
    g2 = grad * gain[...]
    second[...] = jnp.sum(grad * mid * r2, 0, keepdims=True)
    grad_middle = cot[...].astype(f32) + r2 * g2 - mid * r2 * r2 * r2 * jnp.mean(g2 * mid, -1, keepdims=True)
    grad_mid[...] = grad_middle
    low = grad_middle.astype(bf16)
    low_mid[...] = low
    fetch.wait()
    datt[...] = dot_nt(wo_v[...], low).astype(bf16).reshape(H, HD, TOK)


def touch_body(array, out):
    out[...] = jnp.zeros_like(out)


def finish_body(middle, result, out):
    out[...] = (middle[...] + result[...].astype(f32)).astype(bf16)


def sum4_body(*refs):
    for n in range(4):
        refs[n - 4][...] = added([ref[n] for ref in refs[:-4]]).astype(bf16)


def attend_back_body(datt, qkv_in, att_in, totals, cosine, sine, out, dq, dk, dv, dmix, qkv, att, sems):
    copies = [pltpu.make_async_copy(qkv_in, qkv, sems.at[0]), pltpu.make_async_copy(att_in, att, sems.at[1])]
    for copy in copies:
        copy.start()
    for s in range(16):
        dmix[:, 128 * s : 128 * s + 128] = datt[s]
    rows = lax.broadcasted_iota(jnp.int32, (256, 256), 0)
    cols = lax.broadcasted_iota(jnp.int32, (256, 256), 1)
    visible = rows <= cols
    dk[...] = jnp.zeros_like(dk)
    dv[...] = jnp.zeros_like(dv)
    for copy in copies:
        copy.wait()
    for i in range(8):
        here = slice(256 * i, 256 * i + 256)
        query = qkv[0:64, here]
        inverse = 1.0 / totals[:, here]
        grad_att = dmix[:, here].astype(f32)
        delta = jnp.sum(grad_att * att[:, here], 0, keepdims=True) * inverse
        grad_mix = (grad_att * inverse).astype(bf16)
        for at, diagonal in ((slice(0, 256 * i), False), (here, True)):
            if at.stop == 0:
                continue
            key = qkv[64:128, at]
            weights = jnp.exp(dot_tn(key, query) * score_scale)
            if diagonal:
                weights = jnp.where(visible, weights, 0.0)
            grad_weights = dot_tn(qkv[128:192, at], grad_mix)
            grad_scores = (weights * (grad_weights - delta)).astype(bf16)
            more = dot(key, grad_scores)
            dq[:, here] = more if not diagonal or i == 0 else dq[:, here] + more
            dk[:, at] += dot_nt(query, grad_scores)
            dv[:, at] += dot_nt(grad_mix, weights.astype(bf16))

    def unrotated(value):
        value = value * score_scale
        a, b = value[: HD // 2], value[HD // 2 :]
        cos, sin = cosine[...], sine[...]
        return jnp.concatenate([a * cos + b * sin, b * cos - a * sin], 0).astype(bf16)

    low_q, low_k, low_v = unrotated(dq[...]), unrotated(dk[...]), dv[...].astype(bf16)
    for s in range(16):
        out[s, 0:64] = low_q[:, 128 * s : 128 * s + 128]
        out[s, 64:128] = low_k[:, 128 * s : 128 * s + 128]
        out[s, 128:192] = low_v[:, 128 * s : 128 * s + 128]


def weight_grad_body(own, recv, n1, att, low, router_grad, second, *refs):
    more = refs[: 4 * own]
    outs, rows_v, one_v, low_v = refs[4 * own : -3], refs[-3], refs[-2], refs[-1]
    outs = [outs[0:1], outs[1:2], outs[2:4], outs[4:5]] if own else [outs[n : n + 1] for n in range(4)]
    at = Place()
    core = at.core if own else 1 - at.core
    columns = pl.ds(pl.multiple_of(core * 512, 512), 512)
    got = recv[...]
    query = got[:, 0:64]
    pairs = got[:, 64:192].astype(f32).reshape(KV, 2, 128, TOK)
    pairs = (pairs[:, 0] + pairs[:, 1]).astype(bf16)
    rows = jnp.concatenate([query.reshape(KV, 2, 64, TOK), pairs.reshape(KV, 2, 64, TOK)], 2)
    rows_v[...] = rows.reshape(H, 128, TOK)
    one_v[...] = n1[:, columns]
    low_v[...] = low[:, columns]
    index = lax.broadcasted_iota(jnp.int32, (16, 512), 0)
    for i in range(4):
        for j in range(4):
            h = at.source(i, j, core)
            tail = jnp.where(index == 0, row_of(router_grad[:, columns], 2 * h), 0.0)
            tail = jnp.where(index == 1, row_of(router_grad[:, columns], 2 * h + 1), tail)
            tail = jnp.where((index == 2) & (h == 0), second[:, columns], tail)
            part = jnp.concatenate([dot(rows_v[h], one_v[...]), dot(att[h], low_v[...]), tail], 0)
            if own:
                part = part + more[i][j].astype(f32)
            rows_at(outs[i], j)[...] = part.astype(bf16)


def join_body(right, before, left, after, right_out, left_out):
    right_out[0:2] = (right[0:2].astype(f32) + before[...].astype(f32)).astype(bf16)
    right_out[2:4] = right[2:4]
    left_out[0:2] = left[0:2]
    left_out[2:4] = (left[2:4].astype(f32) + after[...].astype(f32)).astype(bf16)


def half_sum_body(w0, w1, w2, w3, out):
    out[...] = added([w0[...], w1[...], w2[...], w3[...]]).astype(bf16)


def hidden_grad_body(recv, hid, gain, grad_mid, wq_in, wk_in, wv_in, out, wq, wk, wv, sems):
    copies = []
    for n, (source, held) in enumerate(((wk_in, wk), (wv_in, wv), (wq_in, wq))):
        for k in range(2):
            here = pl.ds(512 * k, 512)
            copies.append(pltpu.make_async_copy(source.at[here], held.at[here], sems.at[2 * n + k]))
    for copy in copies:
        copy.start()
    got = recv[...]
    grad_q = got[:, 0:64].reshape(D, TOK).T
    pairs = got[:, 64:192].astype(f32).reshape(KV, 2, 128, TOK)
    pairs = (pairs[:, 0] + pairs[:, 1]).astype(bf16)
    grad_k = pairs[:, 0:64].reshape(KV * HD, TOK).T
    grad_v = pairs[:, 64:128].reshape(KV * HD, TOK).T
    for copy in copies:
        copy.wait()
    grad = dot_nt(grad_k, wk[...]) + dot_nt(grad_v, wv[...]) + dot_nt(grad_q, wq[...])
    hidden = hid[...].astype(f32)
    r1 = lax.rsqrt(jnp.mean(hidden * hidden, -1, keepdims=True) + epsilon)
    g1 = grad * gain[...]
    back = r1 * g1 - hidden * r1 * r1 * r1 * jnp.mean(g1 * hidden, -1, keepdims=True)
    out[...] = (grad_mid[...] + back).astype(bf16)


def z_sum_body(p0, p1, p2, p3, out):
    at = Place()
    total = added([p0[...], p1[...], p2[...], p3[...]])
    for b in range(4):
        part = total[:, 128 * b : 128 * b + 128]
        k = lax.rem(b - at.z + 4, 4)
        out[k, 0:128] = part[0:128].T.astype(bf16)
        out[k, 128:208] = part[128:208].astype(bf16)


def assemble_body(half, table, *refs):
    parts = refs[0:4]
    wq, wk, wv, gain = refs[4:8]
    q_out, k_out, v_out, o_out, r_out, e_out, tiles, tails = refs[9 + 6 * half :]
    k = pl.program_id(0)
    for i in range(4):
        for j in range(4):
            h = table[8 + 16 * half + 4 * i + j]
            block = parts[i][j, k]
            tiles[h] = block[0:128].astype(f32)
            o_out[pl.ds(pl.multiple_of(h * 64, 64), 64)] = block[128:192].astype(f32)
            tails[h] = block[192:208].astype(f32)
    for p in range(8):
        q_out[:, 128 * p : 128 * p + 128] = jnp.concatenate([tiles[2 * p][:, :64], tiles[2 * p + 1][:, :64]], 1)
    for m in range(4):
        here = slice(128 * m, 128 * m + 128)
        k_out[:, here] = jnp.concatenate([tiles[4 * m][:, 64:], tiles[4 * m + 2][:, 64:]], 1)
        v_out[:, here] = jnp.concatenate([tiles[4 * m + 1][:, 64:], tiles[4 * m + 3][:, 64:]], 1)
    for h in range(16):
        r_out[2 * h : 2 * h + 2] = tails[h][0:2]
    total = jnp.sum(q_out[...] * wq[...].astype(f32), 1, keepdims=True)
    total = total + jnp.sum(k_out[...] * wk[...].astype(f32), 1, keepdims=True)
    total = total + jnp.sum(v_out[...] * wv[...].astype(f32), 1, keepdims=True)
    first = jnp.broadcast_to(total / gain[...], (128, 128)).T
    index = lax.broadcasted_iota(jnp.int32, (8, 128), 0)
    e_out[...] = jnp.where(index == 0, first[0:8], jnp.broadcast_to(tails[0][2:3], (8, 128)))


def assemble(half, table, parts, wq, wk, wv, gain, after, begun=()):
    def at(g, t):
        return t[4 * half + g]

    rows = pl.BlockSpec((128, 1024), lambda g, t: (at(g, t), 0))
    half_rows = pl.BlockSpec((128, 512), lambda g, t: (at(g, t), 0))
    column = pl.BlockSpec((128, 1), lambda g, t: (at(g, t), 0))
    grid_spec = pltpu.PrefetchScalarGridSpec(
        num_scalar_prefetch=1,
        grid=(4,),
        in_specs=[VM] * 4 + [rows, half_rows, half_rows, column, ANY] + [ANY] * len(begun),
        out_specs=[
            rows,
            half_rows,
            half_rows,
            pl.BlockSpec((1024, 128), lambda g, t: (0, at(g, t))),
            pl.BlockSpec((32, 128), lambda g, t: (0, at(g, t))),
            pl.BlockSpec((8, 128), lambda g, t: (0, at(g, t))),
        ],
        scratch_shapes=[pltpu.VMEM((16, 128, 128), f32), pltpu.VMEM((16, 16, 128), f32)],
    )
    return pl.pallas_call(
        lambda *refs: assemble_body(half, *refs),
        grid_spec=grid_spec,
        out_shape=[
            shape((1024, 1024), f32),
            shape((1024, 512), f32),
            shape((1024, 512), f32),
            shape((1024, 1024), f32),
            shape((32, 1024), f32),
            shape((8, 1024), f32),
        ],
        input_output_aliases={10 + n: n for n in range(len(begun))},
        compiler_params=pltpu.CompilerParams(vmem_limit_bytes=24 * 1024 * 1024),
        cost_estimate=pl.CostEstimate(flops=30 * 10**9, bytes_accessed=1024, transcendentals=0),
        name="assemble",
    )(table, *parts, wq, wk, wv, gain, after, *begun)


def widen_body(up, down, token, up_out, down_out, done):
    done[...] = jnp.zeros_like(done)
    up_out[...] = up[...].astype(f32)
    down_out[...] = down[...].astype(f32)


def widen(up, down, after):
    def spec(rows):
        return pl.BlockSpec((1, rows, D), lambda e, n: (e, n, 0))

    return pl.pallas_call(
        widen_body,
        grid=(2, 4),
        in_specs=[spec(256), spec(128), ANY],
        out_specs=[spec(256), spec(128), pl.BlockSpec((8, 128), lambda e, n: (0, 0))],
        out_shape=[outside((2, D, 2 * FF), f32), outside((2, FF, D), f32), shape((8, 128), f32)],
        compiler_params=pltpu.CompilerParams(vmem_limit_bytes=16 * 1024 * 1024),
        name="widen",
    )(up, down, after)


def on_device(
    hidden_in,
    routes,
    first_gain,
    query_weight,
    key_weight,
    value_weight,
    output_weight,
    second_gain,
    router_weight,
    gateup_weight,
    down_weight,
    cotangent,
):
    at = Place()
    z, core = at.z, at.core
    order = Order()
    steps = jnp.arange(4)
    gain_one = first_gain.astype(f32)[None]
    gain_two = second_gain.astype(f32)[None]
    router_t = router_weight.T
    inverse = 10000.0 ** (-np.arange(0, HD, 2).astype(np.float32) / HD)
    angles = inverse[:, None] * np.arange(SEQ).astype(np.float32)[None, :]
    cos_all, sin_all = np.cos(angles).astype(np.float32), np.sin(angles).astype(np.float32)

    def by_source(table):
        return held_outside(jnp.asarray(table.reshape(HD // 2, 16, TOK).transpose(1, 0, 2)))

    cot_all = held_outside(lax.all_gather(cotangent, "expert", axis=0, tiled=False))
    to_heads, normed_one, codes = order.call(
        project_body,
        [shape((16, 224, TOK)), shape((TOK, D)), shape((EXPERTS, TOK), f32)],
        [
            hidden_in,
            gain_one,
            routes.T,
            held_outside(query_weight),
            held_outside(key_weight),
            held_outside(value_weight),
            by_source(cos_all),
            by_source(sin_all),
        ],
        specs=[VM, VM, VM, HBM, HBM, HBM, HBM, HBM],
        scratch=[
            pltpu.VMEM((D, D), bf16),
            pltpu.VMEM((D, 512), bf16),
            pltpu.VMEM((D, 512), bf16),
            pltpu.VMEM((HD // 2, TOK), f32),
            pltpu.VMEM((HD // 2, TOK), f32),
            pltpu.SemaphoreType.DMA((14,)),
        ],
        name="project",
    )
    at_heads = lax.all_to_all(to_heads, "expert", split_axis=0, concat_axis=0, tiled=True)
    att_low, att, totals, qkv, code_all = order.call(
        attend_body,
        [
            shape((16, HD, TOK)),
            outside((HD, SEQ), f32),
            shape((1, SEQ), f32),
            outside((192, SEQ)),
            shape((16, EXPERTS, TOK), f32),
        ],
        [at_heads],
        out_specs=[VM, HBM, VM, HBM, VM],
        scratch=[pltpu.VMEM((HD, SEQ), f32), pltpu.VMEM((192, SEQ), bf16), pltpu.SemaphoreType.DMA((9,))],
        name="attend",
    )
    att_t = lax.all_to_all(att_low, "expert", split_axis=0, concat_axis=0, tiled=True)
    middle, scale_two, normed_two = order.call(
        middle_body,
        [shape((TOK, D), f32), shape((TOK, 128), f32), shape((TOK, D))],
        [att_t, hidden_in, output_weight, gain_two],
        name="middle",
    )
    row = order.stack(gather_axis(normed_two, along_u), after=(cot_all,))
    right, left = send(row, along_v(-1)), send(row, along_v(1))
    chunks = {0: [row], 1: [right], 3: [left]}
    worked = {}
    held = [held_outside(gateup_weight), held_outside(down_weight)]
    for i in (0, 1, 3, 2):
        if i == 1:
            halves = order.call(split_body, [shape((2, TOK, D))] * 2, [right, left], name="split")
            chunks[2] = [send(halves[0], along_v(-1)), send(halves[1], along_v(1))]
        worked[i] = order.call(
            lambda *refs, i=i: expert_body(i, *refs),
            [
                shape((4, TOK + 16, D)),
                outside((2, 256, D)),
                outside((2, 256, D)),
                outside((2, 256, FF)),
                outside((2, 256, 2 * FF)),
            ]
            + ([shape((2, D, 2 * FF)), shape((2, FF, D))] if i == 0 else []),
            [*chunks[i], cot_all, code_all, router_t, *held],
            specs=[VM] * len(chunks[i]) + [HBM, VM, VM] + [HBM if i == 0 else VM] * 2,
            out_specs=[VM, HBM, HBM, HBM, HBM] + [VM] * (2 if i == 0 else 0),
            scratch=[
                pltpu.VMEM((4, TOK, D), bf16),
                pltpu.VMEM((2, 256, D), bf16),
                pltpu.VMEM((2, 256, D), bf16),
                pltpu.VMEM((2, 256, FF), bf16),
                pltpu.VMEM((2, 256, 2 * FF), bf16),
                pltpu.VMEM((4, TOK, D), bf16),
                pltpu.SemaphoreType.DMA((14,)),
            ],
            us=6,
            limit=24,
            name="experts",
        )
        if i == 0:
            held = worked[i][5:]
    parts = sum_axis([worked[i][0] for i in range(4)], along_v)
    saved = [[held_outside(worked[i][k]) for i in range(4)] for k in range(1, 5)]
    done, gateup_grad, down_grad = order.call(
        expert_grad_body,
        [shape((8, 128), f32), outside((2, D, 2 * FF)), outside((2, FF, D))],
        [*saved[0], *saved[1], *saved[2], *saved[3]],
        specs=[HBM] * 16,
        scratch=[
            pltpu.VMEM((2, 1024, D), bf16),
            pltpu.VMEM((2, 1024, D), bf16),
            pltpu.VMEM((2, 1024, FF), bf16),
            pltpu.VMEM((2, 1024, 2 * FF), bf16),
            pltpu.VMEM((2, D, 2 * FF), bf16),
            pltpu.VMEM((2, FF, D), bf16),
            pltpu.SemaphoreType.DMA((44,)),
        ],
        out_specs=[VM, HBM, HBM],
        limit=40,
        us=11,
        name="expert_grads",
    )
    gateup_grad, down_grad = lax.psum((gateup_grad, down_grad), "dp")
    grad_rows = sum_axis(order.sum4(parts, "sum_grads"), along_u)
    grad_middle, grad_middle_low, to_back, router_grad, second_part = order.call(
        norm_back_body,
        [
            outside((TOK, D), f32),
            shape((TOK, D)),
            shape((H, HD, TOK)),
            shape((EXPERTS, D), f32),
            shape((1, D), f32),
        ],
        [
            *grad_rows,
            normed_two,
            middle,
            scale_two,
            gain_two,
            cotangent,
            codes,
            router_t,
            held_outside(output_weight),
        ],
        specs=[VM] * 11 + [HBM],
        out_specs=[pl.BlockSpec(), VM, VM, VM, VM],
        scratch=[pltpu.VMEM((D, D), bf16), pltpu.SemaphoreType.DMA],
        name="norm_back",
    )
    at_back = lax.all_to_all(to_back, "expert", split_axis=0, concat_axis=0, tiled=True)
    (to_tokens,) = order.call(
        attend_back_body,
        [shape((16, 192, TOK))],
        [at_back, held_outside(qkv), held_outside(att), totals, jnp.asarray(cos_all), jnp.asarray(sin_all)],
        specs=[VM, HBM, HBM, VM, VM, VM],
        limit=24,
        scratch=[
            pltpu.VMEM((HD, SEQ), f32),
            pltpu.VMEM((HD, SEQ), f32),
            pltpu.VMEM((HD, SEQ), f32),
            pltpu.VMEM((HD, SEQ), bf16),
            pltpu.VMEM((192, SEQ), bf16),
            pltpu.VMEM((HD, SEQ), f32),
            pltpu.SemaphoreType.DMA((2,)),
        ],
        name="attend_back",
    )
    at_tokens = lax.all_to_all(to_tokens, "expert", split_axis=0, concat_axis=0, tiled=True)
    sources = [at_tokens, normed_one, att_t, grad_middle_low, router_grad, second_part]
    held_rows = [pltpu.VMEM((H, 128, TOK), bf16), pltpu.VMEM((TOK, 512), bf16), pltpu.VMEM((TOK, 512), bf16)]
    far = order.call(
        lambda *refs: weight_grad_body(0, *refs),
        [shape((4, 208, 512))] * 4,
        sources,
        scratch=held_rows,
        limit=24,
        name="weight_grad",
    )
    far = [send(part, other_core()) for part in far]
    (hidden_grad,) = order.call(
        hidden_grad_body,
        [shape((TOK, D))],
        [
            at_tokens,
            hidden_in,
            gain_one,
            grad_middle,
            held_outside(query_weight),
            held_outside(key_weight),
            held_outside(value_weight),
        ],
        specs=[VM] * 4 + [HBM] * 3,
        scratch=[
            pltpu.VMEM((D, D), bf16),
            pltpu.VMEM((D, 512), bf16),
            pltpu.VMEM((D, 512), bf16),
            pltpu.SemaphoreType.DMA((6,)),
        ],
        name="hidden_grad",
    )
    near, right, far_first, far_last, left = order.call(
        lambda *refs: weight_grad_body(1, *refs),
        [shape((4, 208, 512))] * 2 + [shape((2, 208, 512))] * 2 + [shape((4, 208, 512))],
        [*sources, *far],
        scratch=held_rows,
        limit=24,
        name="weight_grad",
    )
    far_first, far_last = send(far_first, along_v(1)), send(far_last, along_v(-1))
    done, results = order.call(
        expert_result_body,
        [shape((8, 128), f32), outside((16, TOK, D))],
        [*[worked[i][3] for i in range(4)], down_weight, code_all],
        out_specs=[VM, HBM],
        scratch=[
            pltpu.VMEM((16, TOK, D), bf16),
            pltpu.VMEM((16, TOK, D), bf16),
            pltpu.SemaphoreType.DMA((16,)),
        ],
        limit=24,
        us=5,
        name="expert_results",
    )
    result = lax.psum_scatter(results, "expert", scatter_dimension=0, tiled=False)
    right, left = order.call(
        join_body, [shape((4, 208, 512))] * 2, [right, far_first, left, far_last], limit=8, name="join"
    )
    weight_parts = [near, send(right, along_v(1)), send(left, along_v(-1))]
    weight_rows = sum_axis(order.sum4(weight_parts, "sum_weights"), along_u)
    order.call(touch_body, [shape((8, 128), f32)], [held_outside(gateup_grad)], specs=[HBM], name="touch")
    (half,) = order.call(half_sum_body, [shape((208, 512))], weight_rows, name="half")
    (block,) = order.call(z_sum_body, [shape((4, 208, 128))], gather_axis(half, along_z), name="z_sum")
    block = gather_axis(block, along_u)
    block = gather_axis(order.stack(block), along_v)
    gateup_grad, down_grad, done = widen(held_outside(gateup_grad), held_outside(down_grad), order.last[0])
    order.last = (done,)
    others = [send(part, other_core()) for part in block]
    i, j = steps[:, None], steps[None, :]
    own_blocks = jnp.concatenate([core * 4 + (z + steps) % 4, (1 - core) * 4 + (z + steps) % 4])
    table = jnp.concatenate([own_blocks, at.source(i, j).reshape(-1), at.source(i, j, 1 - core).reshape(-1)])
    table = table.astype(jnp.int32)
    weights = (query_weight, key_weight, value_weight, first_gain.astype(f32)[:, None])
    begun = assemble(0, table, block, *weights, done)
    query_grad, key_grad, value_grad, output_grad, router_out, ends = assemble(
        1, table, others, *weights, done, begun
    )
    order.last = (ends,)
    (layer_out,) = order.call(finish_body, [shape((TOK, D))], [middle, result], name="finish")
    return (
        layer_out,
        hidden_grad,
        gateup_grad,
        down_grad,
        query_grad,
        key_grad,
        value_grad,
        output_grad,
        router_out.T,
        ends[0],
        ends[1],
    )


def solution(mesh):
    rows = P(("dp", "expert"), None)
    experts = P("expert", None, None)
    return jax.shard_map(
        on_device,
        mesh=mesh,
        in_specs=(rows, rows, P(), P(), P(), P(), P(), P(), P(), experts, experts, rows),
        out_specs=(rows, rows, experts, experts, P(), P(), P(), P(), P(), P(), P()),
        check_vma=False,
    )
```
